32 devices in a mesh: dp: 2 (over core), fsdp: 16 (over z, y, x).
Axes of the slice: x: 2, y: 2, z: 4, core: 2. Of those that a mesh axis runs over, the one named last changes fastest.
Arguments:
- tokens: bfloat16 [64, 392, 768], P(('dp', 'fsdp')), may hold values from -6 to 6
- positions: int32 [64, 392], P(('dp', 'fsdp')), may hold values from 0 to 1567, as said below
- counts: int32 [64], P(('dp', 'fsdp')), may hold values from 78 to 392, as said below
- cotangent: bfloat16 [64, 392, 768], P(('dp', 'fsdp')), may hold values from -6 to 6
- qkv_weight: float32 [768, 2304], P('fsdp'), may hold values from -0.21875 to 0.21875
- out_weight: float32 [768, 768], P('fsdp'), may hold values from -3.5 to 3.5
- up_weight: float32 [768, 3072], P('fsdp'), may hold values from -0.21875 to 0.21875
- down_weight: float32 [3072, 768], P('fsdp'), may hold values from -0.109375 to 0.109375
- small_params: float32 [768, 12], P('fsdp'), may hold values from -2 to 2
- qkv_momentum: float32 [768, 2304], P('fsdp'), may hold values from -256 to 256
- out_momentum: float32 [768, 768], P('fsdp'), may hold values from -48 to 48
- up_momentum: float32 [768, 3072], P('fsdp'), may hold values from -384 to 384
- down_momentum: float32 [3072, 768], P('fsdp'), may hold values from -384 to 384
- small_momentum: float32 [768, 12], P('fsdp'), may hold values from -512 to 512
- qkv_average: float32 [768, 2304], P('fsdp'), may hold values from -0.21875 to 0.21875
- out_average: float32 [768, 768], P('fsdp'), may hold values from -3.5 to 3.5
- up_average: float32 [768, 3072], P('fsdp'), may hold values from -0.21875 to 0.21875
- down_average: float32 [3072, 768], P('fsdp'), may hold values from -0.109375 to 0.109375
- small_average: float32 [768, 12], P('fsdp'), may hold values from -6 to 6
Outputs:
- block_out: bfloat16 [64, 392, 768], P(('dp', 'fsdp'))
- token_grad: float32 [64, 392, 768], P(('dp', 'fsdp'))
- new_qkv_weight: float32 [768, 2304], P('fsdp')
- new_out_weight: float32 [768, 768], P('fsdp')
- new_up_weight: float32 [768, 3072], P('fsdp')
- new_down_weight: float32 [3072, 768], P('fsdp')
- new_small_params: float32 [768, 12], P('fsdp')
- new_qkv_momentum: float32 [768, 2304], P('fsdp')
- new_out_momentum: float32 [768, 768], P('fsdp')
- new_up_momentum: float32 [768, 3072], P('fsdp')
- new_down_momentum: float32 [3072, 768], P('fsdp')
- new_small_momentum: float32 [768, 12], P('fsdp')
- new_qkv_average: float32 [768, 2304], P('fsdp')
- new_out_average: float32 [768, 768], P('fsdp')
- new_up_average: float32 [768, 3072], P('fsdp')
- new_down_average: float32 [3072, 768], P('fsdp')
- new_small_average: float32 [768, 12], P('fsdp')
- norms: float32 [10], replicated
The draws below stay inside these ranges and needn't reach their ends.
Inputs may be any that keep to these rules, and one draw needn't show every extreme that they name: `counts`: some clip has exactly 392 visible tubelets and some exactly 78. The 392 positions of a clip are distinct; rows at and after a clip's count are padding.
All inputs are finite; a program needn't handle non-finite values.
Results may differ from the reference program's by a relative error of at most 0.012.
The reference program's roundings to bfloat16 on the way count: a program that leaves them out, or rounds other values in their place, can miss the bound.
Values may be sent and summed in bfloat16 or wider, within the bound.
No kernel may reach another device: no remote copies, remote signals or barrier semaphores. Data moves between devices by JAX's collectives and lax.ppermute only.
A program may use at most 256 MiB of HBM per device.

```python
import math
import jax
import jax.numpy as jnp
from jax import lax

D = 768
FF = 3072
HEADS = 12
HEAD_DIM = 64
POSITIONS = 1568
VISMAX = 392
VISMIN = 78
CLIPS = 64
SMALL_COLS = 12


def draw_counts(key, part):
    key_base, key_top, key_least = jax.random.split(key, 3)
    base = jax.random.randint(key_base, (CLIPS,), VISMIN, VISMAX + 1)
    top_at = jax.random.randint(key_top, (), 0, CLIPS)
    least_at = (top_at + 1 + jax.random.randint(key_least, (), 0, CLIPS - 1)) % CLIPS
    slots = jnp.arange(CLIPS)
    base = jnp.where(slots == top_at, VISMAX, base)
    return jnp.where(slots == least_at, VISMIN, base).astype(jnp.int32)


def one_clip(clip_key):
    return jax.random.permutation(clip_key, POSITIONS)[:VISMAX]


def draw_positions(key, part):
    clip_keys = jax.random.split(key, CLIPS)
    return jax.vmap(one_clip)(clip_keys).astype(jnp.int32)


def draw_small_params(key, part):
    key_gain, key_bias = jax.random.split(key, 2)
    columns = jnp.arange(SMALL_COLS)[None, :] + jnp.zeros((D, 1), jnp.int32)
    is_gain = (columns == 0) | (columns == 2)
    gains = jax.random.uniform(key_gain, (D, SMALL_COLS), jnp.float32, 0.5, 1.5)
    biases = 0.3 * jnp.clip(jax.random.normal(key_bias, (D, SMALL_COLS), jnp.float32), -6.0, 6.0)
    return jnp.where(is_gain, gains, biases).astype(jnp.float32)


def shard_levels(key, shape, cuts, low, top_value):
    loudness, own = 1.0, jax.random.fold_in(key, 6)
    for dim, parts in cuts:
        draws = jnp.exp(jax.random.uniform(jax.random.fold_in(own, dim), (parts,), jnp.float32, low / len(cuts), top_value / len(cuts)))
        loudness = loudness * jnp.repeat(draws, shape[dim] // parts).reshape([-1 if axis == dim else 1 for axis in range(len(shape))])
    return loudness


def normal_values(rng, shape, scale, most, cuts=(), held_as=jnp.bfloat16):
    factor_of = shard_levels(rng, shape, cuts, -0.22, 0.18) if cuts else 1.0
    array = jax.random.normal(rng, shape, jnp.float32) * scale * factor_of
    return jnp.minimum(jnp.maximum(array, -most), most).astype(held_as)


def setup_inputs(seed: int = 0) -> dict:
    key_of = jax.random.split(jax.random.key(seed), 20)
    tokens = normal_values(key_of[0], (CLIPS, VISMAX, D), 1.0, 6.0, ((0, 32),))
    positions = draw_positions(jax.random.fold_in(key_of[19], 71), 0)
    counts = draw_counts(jax.random.fold_in(key_of[19], 71), 0)
    cotangent = normal_values(key_of[3], (CLIPS, VISMAX, D), 1.0, 6.0, ((0, 32),))
    qkv_weight = normal_values(key_of[4], (D, 3 * D), D ** -0.5, 0.21875, ((0, 16),), jnp.float32)
    out_weight = normal_values(key_of[5], (D, D), (max(1, D * 5 // (3 * VISMAX))) ** -0.5, 3.5, ((0, 16),), jnp.float32)
    up_weight = normal_values(key_of[6], (D, FF), D ** -0.5, 0.21875, ((0, 16),), jnp.float32)
    down_weight = normal_values(key_of[7], (FF, D), FF ** -0.5, 0.109375, ((0, 16),), jnp.float32)
    small_params = draw_small_params(jax.random.fold_in(key_of[19], 71), 0)
    qkv_momentum = normal_values(key_of[9], (D, 3 * D), ((VISMAX * CLIPS) ** 0.5 * 0.3), 256.0, ((0, 16),), jnp.float32)
    out_momentum = normal_values(key_of[10], (D, D), ((VISMAX * CLIPS) ** 0.5 * 0.05), 48.0, ((0, 16),), jnp.float32)
    up_momentum = normal_values(key_of[11], (D, FF), ((VISMAX * CLIPS) ** 0.5 * 0.4), 384.0, ((0, 16),), jnp.float32)
    down_momentum = normal_values(key_of[12], (FF, D), ((VISMAX * CLIPS) ** 0.5 * 0.4), 384.0, ((0, 16),), jnp.float32)
    small_momentum = normal_values(key_of[13], (D, SMALL_COLS), ((VISMAX * CLIPS) ** 0.5 * 0.5), 512.0, ((0, 16),), jnp.float32)
    qkv_average = normal_values(key_of[14], (D, 3 * D), D ** -0.5, 0.21875, ((0, 16),), jnp.float32)
    out_average = normal_values(key_of[15], (D, D), (max(1, D * 5 // (3 * VISMAX))) ** -0.5, 3.5, ((0, 16),), jnp.float32)
    up_average = normal_values(key_of[16], (D, FF), D ** -0.5, 0.21875, ((0, 16),), jnp.float32)
    down_average = normal_values(key_of[17], (FF, D), FF ** -0.5, 0.109375, ((0, 16),), jnp.float32)
    small_average = normal_values(key_of[18], (D, SMALL_COLS), 0.5, 6.0, ((0, 16),), jnp.float32)
    return dict(tokens=tokens, positions=positions, counts=counts, cotangent=cotangent, qkv_weight=qkv_weight, out_weight=out_weight, up_weight=up_weight, down_weight=down_weight, small_params=small_params, qkv_momentum=qkv_momentum, out_momentum=out_momentum, up_momentum=up_momentum, down_momentum=down_momentum, small_momentum=small_momentum, qkv_average=qkv_average, out_average=out_average, up_average=up_average, down_average=down_average, small_average=small_average)


EPS_NORM = 1e-06
MOMENTUM_DECAY = 0.9
WEIGHT_DECAY = 0.0001
TRUST_RATE = 0.2
AVERAGE_DECAY = 0.8
HIGH = lax.Precision.HIGHEST

@jax.custom_vjp
def low(v):
    return lax.optimization_barrier(v.astype(jnp.bfloat16)).astype(jnp.float32)

@jax.custom_vjp
def low_back(v):
    return v

def low_keep(v):
    return (low(v), None)

def low_pass(kept, grad):
    return (grad,)

def back_keep(v):
    return (v, None)

def back_low(kept, grad):
    return (low(grad),)
low.defvjp(low_keep, low_pass)
low_back.defvjp(back_keep, back_low)

def sinusoid(positions, width):
    half_width = width // 2
    freqs = jnp.exp(jnp.arange(half_width, dtype=jnp.float32) * (-2.0 * math.log(10000.0) / width))
    angles = positions.astype(jnp.float32)[..., None] * freqs
    return jnp.stack([jnp.sin(angles), jnp.cos(angles)], axis=-1).reshape(positions.shape + (width,))

def normalize(values):
    center = values - lax.optimization_barrier(jnp.mean(values, axis=-1, keepdims=True))
    inv_std = lax.rsqrt(lax.optimization_barrier(jnp.mean(center * center, axis=-1, keepdims=True)) + EPS_NORM)
    return center * inv_std

def update_group(weight, grad, moment, average, grad_norm, weight_norm):
    effective = grad + WEIGHT_DECAY * weight
    moment_new = MOMENTUM_DECAY * moment + effective
    rate = TRUST_RATE * weight_norm / (grad_norm + WEIGHT_DECAY * weight_norm)
    weight_new = weight - rate * (effective + MOMENTUM_DECAY * moment_new)
    average_new = AVERAGE_DECAY * average + (1.0 - AVERAGE_DECAY) * weight_new
    return (weight_new, moment_new, average_new)

def reference(tokens, positions, counts, cotangent, qkv_weight, out_weight, up_weight, down_weight, small_params, qkv_momentum, out_momentum, up_momentum, down_momentum, small_momentum, qkv_average, out_average, up_average, down_average, small_average):
    key_ok = jnp.arange(VISMAX)[None, :] < counts[:, None]
    embed_pos = sinusoid(positions, D)
    score_scale = HEAD_DIM ** (-0.5)

    def forward(token_vals, wq_full, wo_full, up_full, down_full, small_full):
        small_low = low(small_full)
        pieces = [small_low[:, i] for i in range(8)]
        gain_one, shift_one, gain_two, shift_two, bias_query, bias_value, bias_out, bias_down = pieces
        bias_up = small_low[:, 8:].reshape(FF)
        bias_qkv = jnp.concatenate([bias_query, jnp.zeros((D,), jnp.float32), bias_value])
        wq_low = low(wq_full)
        wo_low = low(wo_full)
        up_low = low(up_full)
        down_low = low(down_full)
        embed = token_vals + embed_pos
        grouped = embed.reshape(CLIPS // 8, 8, VISMAX, D)
        ok_grouped = key_ok.reshape(CLIPS // 8, 8, VISMAX)

        def group_layer(group_args):
            group_embed, group_ok = group_args
            attn_in = low(normalize(group_embed) * gain_one + shift_one)
            qkv = jnp.einsum('bld,de->ble', attn_in, wq_low, precision=HIGH) + bias_qkv
            qkv = low_back(low(qkv))
            query = qkv[..., :D].reshape(8, VISMAX, HEADS, HEAD_DIM)
            keys = qkv[..., D:2 * D].reshape(8, VISMAX, HEADS, HEAD_DIM)
            values = qkv[..., 2 * D:].reshape(8, VISMAX, HEADS, HEAD_DIM)
            scores = low_back(jnp.einsum('blhe,bmhe->bhlm', query, keys, precision=HIGH) * score_scale)
            scores = jnp.where(group_ok[:, None, None, :], scores, -1000000000.0)
            attention = jax.nn.softmax(scores, axis=-1)
            mixed = jnp.einsum('bhlm,bmhe->blhe', low(attention), values, precision=HIGH)
            attn_out = low_back(low(mixed)).reshape(8, VISMAX, D)
            resid = group_embed + low_back(jnp.einsum('bld,de->ble', attn_out, wo_low, precision=HIGH) + bias_out)
            mlp_in = low(normalize(resid) * gain_two + shift_two)
            pre = low_back(jnp.einsum('bld,df->blf', mlp_in, up_low, precision=HIGH) + bias_up)
            act = low(jax.nn.gelu(pre, approximate=False))
            down = low_back(jnp.einsum('blf,fd->bld', act, down_low, precision=HIGH) + bias_down)
            return resid + down
        outs = lax.map(jax.checkpoint(group_layer), (grouped, ok_grouped))
        return outs.reshape(CLIPS, VISMAX, D)
    masters = (qkv_weight, out_weight, up_weight, down_weight, small_params)
    moments = (qkv_momentum, out_momentum, up_momentum, down_momentum, small_momentum)
    averages = (qkv_average, out_average, up_average, down_average, small_average)
    block_rows, pullback = jax.vjp(forward, tokens.astype(jnp.float32), *masters)
    cot = cotangent.astype(jnp.float32) * key_ok[..., None].astype(jnp.float32)
    cot_grads = pullback(cot)
    token_grad = cot_grads[0]
    grads = cot_grads[1:]
    grad_norms = [jnp.sqrt(jnp.sum(grad * grad)) for grad in grads]
    weight_norms = [jnp.sqrt(jnp.sum(weight * weight)) for weight in masters]
    results = [update_group(masters[i], grads[i], moments[i], averages[i], grad_norms[i], weight_norms[i]) for i in range(5)]
    norms = jnp.stack(grad_norms + weight_norms)
    return (block_rows.astype(jnp.bfloat16), token_grad, results[0][0], results[1][0], results[2][0], results[3][0], results[4][0], results[0][1], results[1][1], results[2][1], results[3][1], results[4][1], results[0][2], results[1][2], results[2][2], results[3][2], results[4][2], norms)
```

```python
import math

import jax
import jax.numpy as jnp
import numpy as np
from jax import lax
from jax.experimental import pallas as pl
from jax.experimental.pallas import tpu as pltpu
from jax.sharding import PartitionSpec as P

HEAD_DIM = 64
EPS_NORM = 1e-06
MOMENTUM_DECAY = 0.9
WEIGHT_DECAY = 0.0001
TRUST_RATE = 0.2
AVERAGE_DECAY = 0.8
NEG = -1000000000.0

BF = jnp.bfloat16
F32 = jnp.float32
AXES = ("dp", "fsdp")
ANY = pl.BlockSpec(memory_space=pl.ANY)
SMEM = pl.BlockSpec(memory_space=pltpu.SMEM)


def params(mib):
    return pltpu.CompilerParams(
        vmem_limit_bytes=mib * 1024 * 1024, dimension_semantics=("arbitrary",)
    )


def params2(mib):
    return pltpu.CompilerParams(
        vmem_limit_bytes=mib * 1024 * 1024, dimension_semantics=("arbitrary", "arbitrary")
    )


def dot(a, b):
    return lax.dot_general(a, b, (((1,), (0,)), ((), ())), preferred_element_type=F32)


def dot_nt(a, b):
    return lax.dot_general(a, b, (((1,), (1,)), ((), ())), preferred_element_type=F32)


def whole(shape):
    zeros = (0,) * len(shape)
    return pl.BlockSpec(shape, lambda *i: zeros)


class Links:
    def __init__(self, dp, fsdp):
        self.dp, self.fsdp = dp, fsdp
        self.paired = dp == 2 and fsdp == 16
        self.steps = ((4, 4), (8, 8), (1, 2), (2, 1))

    def masks(self):
        table = np.zeros((2, 16), np.int32)
        for core in range(2):
            for p in range(16):
                for bit in range(4):
                    if p >> bit & 1:
                        table[core, p] ^= self.steps[bit][core]
        return table

    def swap(self, x, step):
        pairs = []
        for c in range(2):
            for f in range(16):
                if step == "core":
                    pairs.append((c * 16 + f, (1 - c) * 16 + f))
                else:
                    pairs.append((c * 16 + f, c * 16 + (f ^ self.steps[step][c])))
        return lax.ppermute(x, AXES, pairs)

    def gather(self, block):
        held = block
        for step in range(3):
            held = jnp.concatenate([held, self.swap(held, step)], axis=0)
        return held, self.swap(held, 3)

    def scatter_sum(self, keep, send):
        for step in (3, 2, 1, 0):
            total = keep + self.swap(send, step).astype(F32)
            half = total.shape[0] // 2
            if half:
                keep, send = total[:half], total[half:].astype(BF)
        return total[0]

    def sum_chips(self, x):
        for step in range(4):
            x = x + self.swap(x, step)
        return x


def assemble(pieces, order, rows, target, sems, at=0, columns=None):
    copies = []
    n = 0
    for piece in pieces:
        for j in range(piece.shape[0]):
            source = piece.at[j] if columns is None else piece.at[j, :, columns]
            start = pl.multiple_of(order(n) * rows, 16)
            copies.append(
                pltpu.make_async_copy(source, target.at[pl.ds(start, rows)], sems.at[at + n])
            )
            n += 1
    return copies


def deliver(source, order, rows, first, targets, sems, at=0, columns=None):
    copies = []
    n = first
    for target in targets:
        for j in range(target.shape[0]):
            start = pl.multiple_of(order(n) * rows, 16)
            place = target.at[j] if columns is None else target.at[j, :, columns]
            copies.append(
                pltpu.make_async_copy(source.at[pl.ds(start, rows)], place, sems.at[at + n - first])
            )
            n += 1
    return copies


def run_all(copies):
    for copy in copies:
        copy.start()
    for copy in copies:
        copy.wait()


def norm_parts(values):
    center = values - jnp.mean(values, axis=-1, keepdims=True)
    inv = lax.rsqrt(jnp.mean(center * center, axis=-1, keepdims=True) + EPS_NORM)
    return center * inv, inv


def norm_back(u, hat, inv):
    first = jnp.mean(u, axis=-1, keepdims=True)
    second = jnp.mean(u * hat, axis=-1, keepdims=True)
    return inv * (u - first - hat * second)


def embed_kernel(tok, pos, table, small, embed, attn_in):
    p = pos[0]
    turns = p * table[0:1, :]
    turns = turns - jnp.round(turns)
    turns = turns + (p * table[1:2, :] + table[2:3, :])
    turns = turns - jnp.round(turns)
    fold = jnp.where(turns > 0.25, 0.5 - turns, jnp.where(turns < -0.25, -0.5 - turns, turns))
    x = fold * (2.0 * math.pi)
    x2 = x * x
    poly = -1.0 / 39916800.0
    for coef in (1.0 / 362880.0, -1.0 / 5040.0, 1.0 / 120.0, -1.0 / 6.0, 1.0):
        poly = poly * x2 + coef
    rows = tok[0].astype(F32) + x * poly
    embed[0] = rows
    hat, _ = norm_parts(rows)
    attn_in[0] = (hat * small[0:1, :] + small[1:2, :]).astype(BF)


def embed_norm(tokens, positions, small):
    n, length, width = tokens.shape
    exact = 10000.0 ** (-2.0 * (np.arange(width) // 2) / width) / (2.0 * math.pi)
    scale = 2.0 ** (11 - np.floor(np.log2(exact)))
    high = np.round(exact * scale) / scale
    table = np.zeros((8, width), np.float32)
    table[0], table[1], table[2] = high, exact - high, 0.25 * (np.arange(width) % 2)
    clip = pl.BlockSpec((1, length, width), lambda i: (i, 0, 0))
    return pl.pallas_call(
        embed_kernel,
        grid=(n,),
        in_specs=[
            clip,
            pl.BlockSpec((1, length, 1), lambda i: (i, 0, 0)),
            whole((8, width)),
            whole((16, width)),
        ],
        out_specs=[clip, clip],
        out_shape=[
            jax.ShapeDtypeStruct(tokens.shape, F32),
            jax.ShapeDtypeStruct(tokens.shape, BF),
        ],
        compiler_params=params(24),
        cost_estimate=pl.CostEstimate(
            flops=60 * tokens.size, bytes_accessed=8 * tokens.size, transcendentals=0
        ),
        name="embed_norm",
    )(tokens, positions.astype(F32)[..., None], jnp.asarray(table), small)


def pair_specs(groups, block):
    specs, first = [], 0
    for array in groups:
        n = array.shape[0]

        def index(*at, first=first, n=n):
            return (jnp.clip(at[-1] - first, 0, n - 1), 0, 0)

        specs.append(pl.BlockSpec((1,) + block, index))
        first += n
    return specs, first


def choose(refs, step, each):
    value = refs[0][0]
    for k in range(1, len(refs)):
        value = jnp.where(step >= k * each, refs[k][0], value)
    return value


def attend_forward(groups, order, counts, bias, pieces, rows):
    each, length, width = groups[0].shape
    columns = pieces[0].shape[2]
    part = columns // 3
    heads = part // HEAD_DIM
    specs, clips = pair_specs(groups, (length, width))
    n_groups, n_pieces = len(groups), len(pieces)
    blocks = sum(piece.shape[0] for piece in pieces)

    def kernel(order_ref, count_ref, bias_ref, *refs):
        ins = refs[:n_groups]
        piece_refs = refs[n_groups : n_groups + n_pieces]
        qkv, mixed, logs, weight, scores, sems = refs[n_groups + n_pieces :]
        step = pl.program_id(0)

        @pl.when(step == 0)
        def _():
            run_all(assemble(piece_refs, lambda n: order_ref[n], rows, weight, sems))

        rows_in = choose(ins, step, each)
        low = (dot(rows_in, weight[...]) + bias_ref[...]).astype(BF)
        qkv[0] = low
        count = count_ref[step]
        valid = lax.broadcasted_iota(jnp.int32, (length, 1), 0) < count
        lane = lax.broadcasted_iota(jnp.int32, (1, 2 * HEAD_DIM), 1)
        outs, log_rows = [], []
        for pair in range(heads // 2):
            at = 2 * HEAD_DIM * pair
            q = low[:, at : at + 128] * jnp.asarray(HEAD_DIM**-0.5, BF)
            k = low[:, part + at : part + at + 128]
            v_t = low[:, 2 * part + at : 2 * part + at + 128].T
            for half in range(2):
                mine = (lane >= HEAD_DIM) if half else (lane < HEAD_DIM)
                s = dot_nt(jnp.where(mine, k, jnp.zeros_like(k)), q)
                s = jnp.where(valid, s, NEG)
                top = jnp.max(s, axis=0, keepdims=True)
                e = jnp.exp(s - top)
                total = jnp.sum(e, axis=0, keepdims=True)
                p = (e * (1.0 / total)).astype(BF)
                outs.append(dot(v_t[HEAD_DIM * half : HEAD_DIM * half + HEAD_DIM], p))
                log_rows.append(top + jnp.log(total))
        mixed[0] = jnp.concatenate(outs, axis=0).T.astype(BF)
        logs[0] = jnp.concatenate(log_rows, axis=0)

    n_rows = clips * length
    return pl.pallas_call(
        kernel,
        grid=(clips,),
        in_specs=[SMEM, SMEM, whole((1, columns))] + specs + [ANY] * n_pieces,
        out_specs=[
            pl.BlockSpec((1, length, columns), lambda i: (i, 0, 0)),
            pl.BlockSpec((1, length, part), lambda i: (i, 0, 0)),
            pl.BlockSpec((1, heads, length), lambda i: (i, 0, 0)),
        ],
        out_shape=[
            jax.ShapeDtypeStruct((clips, length, columns), BF),
            jax.ShapeDtypeStruct((clips, length, part), BF),
            jax.ShapeDtypeStruct((clips, heads, length), F32),
        ],
        scratch_shapes=[
            pltpu.VMEM((width, columns), BF),
            pltpu.VMEM((8, 128), F32),
            pltpu.SemaphoreType.DMA((blocks,)),
        ],
        compiler_params=params(48),
        cost_estimate=pl.CostEstimate(
            flops=2 * n_rows * width * columns + 16 * n_rows * length * part,
            bytes_accessed=2 * n_rows * (width + columns + part),
            transcendentals=n_rows * length * heads,
        ),
        name="attend_forward",
    )(order, counts, bias, *groups, *pieces)


def out_weight_copies(own, other, meta, rows, weight, sems):
    if other is None:
        return assemble(own, lambda n: meta[1 + n], rows, weight.at[0], sems)
    core = meta[0]
    copies = assemble(own, lambda n: meta[1 + n], rows, weight.at[core], sems)
    return copies + assemble(other, lambda n: meta[17 + n], rows, weight.at[1 - core], sems, 16)


def project_norm(own, recv, embed, small, meta, pieces, others, rows):
    n, length, width = embed.shape
    part = own.shape[2]
    mixes = [own] if recv is None else [own, recv]
    n_mix, n_p, n_o = len(mixes), len(pieces), len(others)
    halves = 1 if recv is None else 2
    half_width = width // halves

    def kernel(meta_ref, small_ref, embed_ref, *refs):
        mix_refs = refs[:n_mix]
        own_refs = refs[n_mix : n_mix + n_p]
        other_refs = refs[n_mix + n_p : n_mix + n_p + n_o] or None
        resid, mlp_in, weight, sems = refs[n_mix + n_p + n_o :]

        @pl.when(pl.program_id(0) == 0)
        def _():
            run_all(out_weight_copies(own_refs, other_refs, meta_ref, rows, weight, sems))

        outs = []
        for half in range(halves):
            total = 0.0
            for k, mix in enumerate(mix_refs):
                at = pl.multiple_of((meta_ref[0] ^ k) * part, 128) if n_mix > 1 else 0
                total = total + dot(mix[0], weight[half, pl.ds(at, part), :])
            outs.append(total)
        total = jnp.concatenate(outs, axis=1) if halves > 1 else outs[0]
        values = embed_ref[0] + total + small_ref[6:7, :]
        resid[0] = values
        hat, _ = norm_parts(values)
        mlp_in[0] = (hat * small_ref[2:3, :] + small_ref[3:4, :]).astype(BF)

    clip = pl.BlockSpec((1, length, width), lambda i: (i, 0, 0))
    mix_spec = pl.BlockSpec((1, length, part), lambda i: (i, 0, 0))
    return pl.pallas_call(
        kernel,
        grid=(n,),
        in_specs=[SMEM, whole((16, width)), clip] + [mix_spec] * n_mix + [ANY] * (n_p + n_o),
        out_specs=[clip, clip],
        out_shape=[
            jax.ShapeDtypeStruct(embed.shape, F32),
            jax.ShapeDtypeStruct(embed.shape, BF),
        ],
        scratch_shapes=[
            pltpu.VMEM((halves, width, half_width), BF),
            pltpu.SemaphoreType.DMA((32,)),
        ],
        compiler_params=params(24),
        cost_estimate=pl.CostEstimate(
            flops=2 * embed.size * width, bytes_accessed=14 * embed.size, transcendentals=0
        ),
        name="project_norm",
    )(meta, small, embed, *mixes, *pieces, *others)


def mlp_both(groups, cots, order, counts, bias, pieces, rows, block, relative):
    each, length, width = groups[0].shape
    hidden = bias.shape[1]
    n_groups, n_pieces = len(groups), len(pieces)
    n_blocks = sum(piece.shape[0] for piece in pieces)
    hidden_rows = hidden // n_blocks
    specs, clips = pair_specs(groups, (length, width))
    steps = hidden // block
    if relative:
        half = n_blocks // 2
        grad_shapes = [
            jax.ShapeDtypeStruct((half, rows, 2 * width), F32),
            jax.ShapeDtypeStruct((half, rows, 2 * width), BF),
        ]
    else:
        grad_shapes = [
            jax.ShapeDtypeStruct((1, width, hidden), F32),
            jax.ShapeDtypeStruct((1, hidden, width), F32),
        ]
    own_shape = (each, length, width)
    out_shapes = [jax.ShapeDtypeStruct(own_shape, F32)] * 2
    if n_groups > 1:
        out_shapes += [jax.ShapeDtypeStruct(own_shape, BF)] * 2
    out_shapes += [jax.ShapeDtypeStruct((1, hidden), F32)]

    def kernel(order_ref, count_ref, bias_ref, *refs):
        ins = refs[:n_groups]
        cot_refs = refs[n_groups : 2 * n_groups]
        piece_refs = refs[2 * n_groups : 2 * n_groups + n_pieces]
        outs = refs[2 * n_groups + n_pieces :]
        own_out, own_dm = outs[0], outs[1]
        sent = outs[2:4] if n_groups > 1 else None
        n_out = 4 if n_groups > 1 else 2
        bias_grad = outs[n_out]
        grad_a, grad_b = outs[n_out + 1 : n_out + 3]
        (up, down, g_up, g_down, low_up, low_down, acc_out, acc_dm, sems) = outs[n_out + 3 :]
        j, i = pl.program_id(0), pl.program_id(1)

        @pl.when((j == 0) & (i == 0))
        def _():
            place = lambda n: order_ref[n]
            copies = assemble(piece_refs, place, rows, up, sems, 0, slice(0, hidden))
            if relative:
                copies += assemble(
                    piece_refs, place, hidden_rows, down, sems, n_blocks, slice(hidden, None)
                )
            else:
                copies += [pltpu.make_async_copy(piece_refs[1].at[0], down, sems.at[1])]
            run_all(copies)

        at = pl.multiple_of(j * block, block)
        cols = pl.ds(at, block)
        x = choose(ins, i, each)
        valid = lax.broadcasted_iota(jnp.int32, (length, 1), 0) < count_ref[i]
        cot = choose(cot_refs, i, each)
        dd = jnp.where(valid, cot, jnp.zeros_like(cot))
        up_block = up[:, cols]
        down_block = down[cols, :]
        pre = dot(x, up_block) + bias_ref[:, cols]
        cdf = 0.5 + 0.5 * lax.erf(pre * 0.7071067811865476)
        pdf = jnp.exp(pre * pre * -0.5) * 0.3989422804014327
        act = (pre * cdf).astype(BF)
        d_pre = (dot_nt(dd, down_block) * (cdf + pre * pdf)).astype(BF)
        out = dot(act, down_block)
        dm = dot_nt(d_pre, up_block)
        up_part = dot(x.T, d_pre)
        down_part = dot(act.T, dd)
        bias_part = jnp.sum(d_pre.astype(F32), axis=0, keepdims=True)

        @pl.when(j == 0)
        def _():
            acc_out[i] = out
            acc_dm[i] = dm

        @pl.when(j > 0)
        def _():
            acc_out[i] += out
            acc_dm[i] += dm

        @pl.when(i == 0)
        def _():
            g_up[:, cols] = up_part
            g_down[cols, :] = down_part
            bias_grad[:, cols] = bias_part

        @pl.when(i > 0)
        def _():
            g_up[:, cols] += up_part
            g_down[cols, :] += down_part
            bias_grad[:, cols] += bias_part

        @pl.when(j == steps - 1)
        def _():
            @pl.when(i < each)
            def _():
                own_out[0] = acc_out[i]
                own_dm[0] = acc_dm[i]

            if sent is not None:

                @pl.when(i >= each)
                def _():
                    sent[0][0] = acc_out[i].astype(BF)
                    sent[1][0] = acc_dm[i].astype(BF)

        @pl.when((j == steps - 1) & (i == clips - 1))
        def _():
            place = lambda n: order_ref[n]
            if relative:
                low_up[...] = g_up[...].astype(BF)
                low_down[...] = g_down[...].astype(BF)
                one, two = slice(0, width), slice(width, 2 * width)
                copies = deliver(g_up, place, rows, 0, [grad_a], sems, 0, one)
                copies += deliver(low_up, place, rows, half, [grad_b], sems, half, one)
                copies += deliver(g_down, place, rows, 0, [grad_a], sems, 2 * half, two)
                copies += deliver(low_down, place, rows, half, [grad_b], sems, 3 * half, two)
            else:
                copies = [
                    pltpu.make_async_copy(g_up, grad_a.at[0], sems.at[0]),
                    pltpu.make_async_copy(g_down, grad_b.at[0], sems.at[1]),
                ]
            run_all(copies)

    def own_index(j, i):
        return (jnp.where(j == steps - 1, jnp.minimum(i, each - 1), 0), 0, 0)

    def sent_index(j, i):
        return (jnp.where(j == steps - 1, jnp.clip(i - each, 0, each - 1), 0), 0, 0)

    out_specs = [pl.BlockSpec((1, length, width), own_index)] * 2
    if n_groups > 1:
        out_specs += [pl.BlockSpec((1, length, width), sent_index)] * 2
    out_specs += [whole((1, hidden)), ANY, ANY]
    low_shape = (width, hidden) if relative else (16, 128)
    low_shape_down = (hidden, width) if relative else (16, 128)
    n_rows = clips * length
    return pl.pallas_call(
        kernel,
        grid=(steps, clips),
        in_specs=[SMEM, SMEM, whole((1, hidden))] + specs + specs + [ANY] * n_pieces,
        out_specs=out_specs,
        out_shape=out_shapes + grad_shapes,
        scratch_shapes=[
            pltpu.VMEM((width, hidden), BF),
            pltpu.VMEM((hidden, width), BF),
            pltpu.VMEM((width, hidden), F32),
            pltpu.VMEM((hidden, width), F32),
            pltpu.VMEM(low_shape, BF),
            pltpu.VMEM(low_shape_down, BF),
            pltpu.VMEM((clips, length, width), F32),
            pltpu.VMEM((clips, length, width), F32),
            pltpu.SemaphoreType.DMA((max(2 * n_blocks, 2),)),
        ],
        compiler_params=params2(56),
        cost_estimate=pl.CostEstimate(
            flops=12 * n_rows * width * hidden,
            bytes_accessed=12 * n_rows * width + 10 * width * hidden,
            transcendentals=2 * n_rows * hidden,
        ),
        name="mlp_both",
    )(order, counts, bias, *groups, *cots, *pieces)


def norm_two_back(dms, resid, cot, small, meta, counts, pieces, others, rows, part):
    n, length, width = resid.shape
    n_dm, n_p, n_o = len(dms), len(pieces), len(others)
    halves = 2 if others else 1
    half_width = width // halves

    def kernel(meta_ref, count_ref, small_ref, resid_ref, cot_ref, *refs):
        dm_refs = refs[:n_dm]
        own_refs = refs[n_dm : n_dm + n_p]
        other_refs = refs[n_dm + n_p : n_dm + n_p + n_o] or None
        outs = refs[n_dm + n_p + n_o :]
        mixes = outs[: halves]
        proj, d_resid, sums, weight, sems = outs[halves:]
        step = pl.program_id(0)

        @pl.when(step == 0)
        def _():
            run_all(out_weight_copies(own_refs, other_refs, meta_ref, rows, weight, sems))

        valid = lax.broadcasted_iota(jnp.int32, (length, 1), 0) < count_ref[step]
        dy = jnp.where(valid, cot_ref[0].astype(F32), 0.0)
        dm = dm_refs[0][0].astype(F32)
        for ref in dm_refs[1:]:
            dm = dm + ref[0].astype(F32)
        hat, inv = norm_parts(resid_ref[0])
        total = dy + norm_back(dm * small_ref[2:3, :], hat, inv)
        d_resid[0] = total
        low = total.astype(BF)
        proj[0] = low
        row = lambda v: jnp.sum(v, axis=0, keepdims=True)
        parts = jnp.concatenate(
            [row(dm * hat), row(dm), row(low.astype(F32)), row(dy), jnp.zeros((4, width), F32)]
        )
        for k in range(halves):
            at = pl.multiple_of((meta_ref[0] ^ k) * part, 128) if halves > 1 else 0
            value = 0.0
            for half in range(halves):
                cut = low[:, half * half_width : (half + 1) * half_width]
                value = value + dot_nt(cut, weight[half, pl.ds(at, part), :])
            mixes[k][0] = value.astype(BF)

        @pl.when(step == 0)
        def _():
            sums[...] = parts

        @pl.when(step > 0)
        def _():
            sums[...] += parts

    clip = pl.BlockSpec((1, length, width), lambda i: (i, 0, 0))
    mix_spec = pl.BlockSpec((1, length, part), lambda i: (i, 0, 0))
    shape = resid.shape
    mix_shape = jax.ShapeDtypeStruct((n, length, part), BF)
    return pl.pallas_call(
        kernel,
        grid=(n,),
        in_specs=[SMEM, SMEM, whole((16, width)), clip, clip]
        + [clip] * n_dm
        + [ANY] * (n_p + n_o),
        out_specs=[mix_spec] * halves + [clip, clip, whole((8, width))],
        out_shape=[mix_shape] * halves
        + [
            jax.ShapeDtypeStruct(shape, BF),
            jax.ShapeDtypeStruct(shape, F32),
            jax.ShapeDtypeStruct((8, width), F32),
        ],
        scratch_shapes=[
            pltpu.VMEM((halves, width, half_width), BF),
            pltpu.SemaphoreType.DMA((32,)),
        ],
        compiler_params=params(32),
        cost_estimate=pl.CostEstimate(
            flops=2 * resid.size * width, bytes_accessed=24 * resid.size, transcendentals=0
        ),
        name="norm_two_back",
    )(meta, counts, small, resid, cot, *dms, *pieces, *others)


def out_weight_grad(own, recv, proj, meta, rows):
    n, length, width = proj.shape
    part = own.shape[2]
    mixes = [own] if recv is None else [own, recv]
    n_mix = len(mixes)
    halves = n_mix
    half_width = width // halves
    blocks = width // rows

    def kernel(meta_ref, proj_ref, *refs):
        mix_refs = refs[:n_mix]
        if halves > 1:
            keep, send, total, low, sems = refs[n_mix:]
        else:
            keep, total, sems = refs[n_mix:]
        step = pl.program_id(0)

        @pl.when(step == 0)
        def _():
            total[...] = jnp.zeros_like(total)

        for k in range(n_mix):
            turned = mix_refs[k][0].T
            at = pl.multiple_of((meta_ref[0] ^ k) * part, 128) if halves > 1 else 0
            for half in range(halves):
                cut = proj_ref[0, :, half * half_width : (half + 1) * half_width]
                total[half, pl.ds(at, part), :] += dot(turned, cut)

        @pl.when(step == n - 1)
        def _():
            if halves > 1:
                core = meta_ref[0]
                low[...] = total[1 - core].astype(BF)
                copies = deliver(
                    total.at[core], lambda n: meta_ref[1 + n], rows, 0, [keep], sems, 0
                )
                copies += deliver(low, lambda n: meta_ref[17 + n], rows, 0, [send], sems, blocks)
                run_all(copies)
            else:
                run_all([pltpu.make_async_copy(total, keep, sems.at[0])])

    clip = pl.BlockSpec((1, length, width), lambda i: (i, 0, 0))
    mix_spec = pl.BlockSpec((1, length, part), lambda i: (i, 0, 0))
    if halves > 1:
        shapes = [
            jax.ShapeDtypeStruct((blocks, rows, half_width), F32),
            jax.ShapeDtypeStruct((blocks, rows, half_width), BF),
        ]
        scratch = [
            pltpu.VMEM((halves, width, half_width), F32),
            pltpu.VMEM((width, half_width), BF),
            pltpu.SemaphoreType.DMA((2 * blocks,)),
        ]
    else:
        shapes = [jax.ShapeDtypeStruct((1, width, width), F32)]
        scratch = [pltpu.VMEM((1, width, width), F32), pltpu.SemaphoreType.DMA((1,))]
    return pl.pallas_call(
        kernel,
        grid=(n,),
        in_specs=[SMEM, clip] + [mix_spec] * n_mix,
        out_specs=[ANY] * len(shapes),
        out_shape=shapes,
        scratch_shapes=scratch,
        compiler_params=params(24),
        cost_estimate=pl.CostEstimate(
            flops=2 * proj.size * width, bytes_accessed=6 * proj.size, transcendentals=0
        ),
        name="out_weight_grad",
    )(meta, proj, *mixes)


def attend_back(groups, qkv, logs, d_mixes, order, counts, rows, relative):
    each, length, width = groups[0].shape
    clips, _, columns = qkv.shape
    part = columns // 3
    heads = part // HEAD_DIM
    n_groups = len(groups)
    specs, _ = pair_specs(groups, (length, width))
    mix_specs, _ = pair_specs(d_mixes, (length, part))
    blocks = width // rows
    half_blocks = blocks // 2

    def kernel(order_ref, count_ref, qkv_ref, log_ref, *refs):
        ins = refs[:n_groups]
        mix_refs = refs[n_groups : 2 * n_groups]
        d_qkv, bias_grad = refs[2 * n_groups : 2 * n_groups + 2]
        if relative:
            keep, send, total, low, sems = refs[2 * n_groups + 2 :]
        else:
            keep, total, sems = refs[2 * n_groups + 2 :]
        step = pl.program_id(0)
        valid = lax.broadcasted_iota(jnp.int32, (length, 1), 0) < count_ref[step]
        lane = lax.broadcasted_iota(jnp.int32, (1, 2 * HEAD_DIM), 1)
        d_mix = choose(mix_refs, step, each)
        turned_q, d_keys, d_values = [], [], []
        scale = HEAD_DIM**-0.5
        for pair in range(heads // 2):
            at = 2 * HEAD_DIM * pair
            q = qkv_ref[0, :, at : at + 128] * jnp.asarray(scale, BF)
            k = qkv_ref[0, :, part + at : part + at + 128]
            v = qkv_ref[0, :, 2 * part + at : 2 * part + at + 128]
            do = d_mix[:, at : at + 128]
            k_t = k.T
            dk = dv = None
            for half in range(2):
                mine = (lane >= HEAD_DIM) if half else (lane < HEAD_DIM)
                only = lambda x: jnp.where(mine, x, jnp.zeros_like(x))
                s = dot_nt(only(k), q)
                h = 2 * pair + half
                p = jnp.exp(jnp.where(valid, s, NEG) - log_ref[0, h : h + 1, :])
                dp = dot_nt(only(v), do)
                inner = jnp.sum(dp * p, axis=0, keepdims=True)
                ds = (p * (dp - inner)).astype(BF)
                dv_half = dot(p.astype(BF), only(do))
                dk_half = dot(ds, only(q))
                dv = dv_half if dv is None else dv + dv_half
                dk = dk_half if dk is None else dk + dk_half
                turned_q.append(dot(k_t[HEAD_DIM * half : HEAD_DIM * half + HEAD_DIM], ds))
            d_keys.append(dk)
            d_values.append(dv)
        dq = (jnp.concatenate(turned_q, axis=0) * scale).T
        low_rows = jnp.concatenate([dq] + d_keys + d_values, axis=1).astype(BF)
        d_qkv[0] = low_rows
        bias_part = jnp.sum(low_rows.astype(F32), axis=0, keepdims=True)
        weight_part = dot(choose(ins, step, each).T, low_rows)

        @pl.when(step == 0)
        def _():
            total[...] = weight_part
            bias_grad[...] = bias_part

        @pl.when(step > 0)
        def _():
            total[...] += weight_part
            bias_grad[...] += bias_part

        @pl.when(step == clips - 1)
        def _():
            place = lambda n: order_ref[n]
            if relative:
                low[...] = total[...].astype(BF)
                copies = deliver(total, place, rows, 0, [keep], sems, 0)
                copies += deliver(low, place, rows, half_blocks, [send], sems, half_blocks)
                run_all(copies)
            else:
                run_all([pltpu.make_async_copy(total, keep.at[0], sems.at[0])])

    clip = lambda c: pl.BlockSpec((1, length, c), lambda i: (i, 0, 0))
    if relative:
        shapes = [
            jax.ShapeDtypeStruct((half_blocks, rows, columns), F32),
            jax.ShapeDtypeStruct((half_blocks, rows, columns), BF),
        ]
        scratch = [pltpu.VMEM((width, columns), F32), pltpu.VMEM((width, columns), BF)]
    else:
        shapes = [jax.ShapeDtypeStruct((1, width, columns), F32)]
        scratch = [pltpu.VMEM((width, columns), F32)]
    n_rows = clips * length
    return pl.pallas_call(
        kernel,
        grid=(clips,),
        in_specs=[SMEM, SMEM, clip(columns), pl.BlockSpec((1, heads, length), lambda i: (i, 0, 0))]
        + specs
        + mix_specs,
        out_specs=[clip(columns), whole((1, columns))] + [ANY] * len(shapes),
        out_shape=[
            jax.ShapeDtypeStruct((clips, length, columns), BF),
            jax.ShapeDtypeStruct((1, columns), F32),
        ]
        + shapes,
        scratch_shapes=scratch + [pltpu.SemaphoreType.DMA((blocks,))],
        compiler_params=params(56),
        cost_estimate=pl.CostEstimate(
            flops=2 * n_rows * width * columns + 40 * n_rows * length * part,
            bytes_accessed=2 * n_rows * (2 * width + 2 * columns),
            transcendentals=n_rows * length * heads,
        ),
        name="attend_back",
    )(order, counts, qkv, logs, *groups, *d_mixes)


def attn_in_grad(d_qkv, order, pieces, rows, each, width):
    clips, length, columns = d_qkv.shape
    n_pieces = len(pieces)
    blocks = sum(piece.shape[0] for piece in pieces)
    split = clips > each

    def kernel(order_ref, rows_ref, *refs):
        piece_refs = refs[:n_pieces]
        outs = refs[n_pieces:]
        weight, sems = outs[-2:]
        step = pl.program_id(0)

        @pl.when(step == 0)
        def _():
            run_all(assemble(piece_refs, lambda n: order_ref[n], rows, weight, sems))

        value = dot_nt(rows_ref[0], weight[...])
        if split:

            @pl.when(step < each)
            def _():
                outs[0][0] = value

            @pl.when(step >= each)
            def _():
                outs[1][0] = value.astype(BF)
        else:
            outs[0][0] = value

    own = pl.BlockSpec((1, length, width), lambda i: (jnp.minimum(i, each - 1), 0, 0))
    other = pl.BlockSpec((1, length, width), lambda i: (jnp.clip(i - each, 0, each - 1), 0, 0))
    shapes = [jax.ShapeDtypeStruct((each, length, width), F32)]
    if split:
        shapes.append(jax.ShapeDtypeStruct((each, length, width), BF))
    return pl.pallas_call(
        kernel,
        grid=(clips,),
        in_specs=[SMEM, pl.BlockSpec((1, length, columns), lambda i: (i, 0, 0))] + [ANY] * n_pieces,
        out_specs=[own, other][: len(shapes)],
        out_shape=shapes,
        scratch_shapes=[pltpu.VMEM((width, columns), BF), pltpu.SemaphoreType.DMA((blocks,))],
        compiler_params=params(32),
        cost_estimate=pl.CostEstimate(
            flops=2 * clips * length * width * columns,
            bytes_accessed=2 * clips * length * (columns + 2 * width),
            transcendentals=0,
        ),
        name="attn_in_grad",
    )(order, d_qkv, *pieces)


def norm_one_back(das, embed, d_resid, small):
    n, length, width = embed.shape
    n_da = len(das)

    def kernel(small_ref, embed_ref, resid_ref, *refs):
        da_refs = refs[:n_da]
        grad, sums = refs[n_da:]
        step = pl.program_id(0)
        da = da_refs[0][0].astype(F32)
        for ref in da_refs[1:]:
            da = da + ref[0].astype(F32)
        hat, inv = norm_parts(embed_ref[0])
        grad[0] = resid_ref[0] + norm_back(da * small_ref[0:1, :], hat, inv)
        row = lambda v: jnp.sum(v, axis=0, keepdims=True)
        parts = jnp.concatenate([row(da * hat), row(da), jnp.zeros((6, width), F32)])

        @pl.when(step == 0)
        def _():
            sums[...] = parts

        @pl.when(step > 0)
        def _():
            sums[...] += parts

    clip = pl.BlockSpec((1, length, width), lambda i: (i, 0, 0))
    return pl.pallas_call(
        kernel,
        grid=(n,),
        in_specs=[whole((16, width)), clip, clip] + [clip] * n_da,
        out_specs=[clip, whole((8, width))],
        out_shape=[
            jax.ShapeDtypeStruct(embed.shape, F32),
            jax.ShapeDtypeStruct((8, width), F32),
        ],
        compiler_params=params(24),
        cost_estimate=pl.CostEstimate(
            flops=30 * embed.size, bytes_accessed=18 * embed.size, transcendentals=0
        ),
        name="norm_one_back",
    )(small, embed, d_resid, *das)


def update_group(weight, grad, moment, average, grad_norm, weight_norm):
    effective = grad + WEIGHT_DECAY * weight
    moment_new = MOMENTUM_DECAY * moment + effective
    rate = TRUST_RATE * weight_norm / (grad_norm + WEIGHT_DECAY * weight_norm)
    weight_new = weight - rate * (effective + MOMENTUM_DECAY * moment_new)
    average_new = AVERAGE_DECAY * average + (1.0 - AVERAGE_DECAY) * weight_new
    return (weight_new, moment_new, average_new)


def finish(masters, moments, averages, grads, totals):
    norms = jnp.sqrt(totals)
    results = [
        update_group(masters[i], grads[i], moments[i], averages[i], norms[i], norms[5 + i])
        for i in range(5)
    ]
    return (
        tuple(r[0] for r in results)
        + tuple(r[1] for r in results)
        + tuple(r[2] for r in results)
        + (norms,)
    )


def square_sum(x):
    return jnp.sum(x * x)


def small_rows(table):
    rows = table.shape[0]
    return jnp.concatenate([table[:, :8].T, table[:, 8:].reshape(4, rows)], axis=0)


def small_table(rows12):
    rows = rows12.shape[1]
    return jnp.concatenate([rows12[:8].T, rows12[8:12].reshape(rows, 4)], axis=1)


def paired_device(links, tokens, positions, counts, cotangent, *state):
    masters, moments, averages = state[:5], state[5:10], state[10:]
    w_qkv, w_out, w_up, w_down, w_small = masters
    each, length, width = tokens.shape
    rows = w_qkv.shape[0]
    core = lax.axis_index("dp")
    chip = lax.axis_index("fsdp")
    table = jnp.asarray(links.masks())
    mine = lax.dynamic_index_in_dim(table, core, 0, False) ^ chip
    partner = lax.dynamic_index_in_dim(table, 1 - core, 0, False) ^ chip
    meta = jnp.concatenate([core[None].astype(jnp.int32), mine, partner])
    part = width // 2

    pick_core = lambda x, axis: lax.dynamic_index_in_dim(x, core, axis, False)
    pack_qkv = pick_core(w_qkv.reshape(rows, 3, 2, part), 2).astype(BF).reshape(1, rows, 3 * part)
    pack_out = pick_core(w_out.reshape(rows, 2, part), 1).astype(BF).reshape(1, rows, part)
    up_cut = pick_core(w_up.reshape(rows, 16, 2, 2, rows), 2).astype(BF)
    down_cut = pick_core(w_down.reshape(2, 2, rows, width), 0).astype(BF)
    packs = [
        jnp.concatenate([up_cut[:, :, h].reshape(rows, 16 * rows), down_cut[h]], axis=1)[None]
        for h in range(2)
    ]

    cot_other = links.swap(cotangent, "core")
    counts_all = jnp.concatenate([counts, links.swap(counts, "core")])
    qkv_a, qkv_b = links.gather(pack_qkv)

    placed = jnp.zeros((16, width), BF)
    placed = lax.dynamic_update_slice(placed, small_rows(w_small).astype(BF), (0, chip * rows))
    small = links.sum_chips(placed).astype(F32)

    mlp_w = [links.gather(packs[0])]
    out_a, out_b = links.gather(pack_out)
    out_c, out_d = links.swap(out_a, "core"), links.swap(out_b, "core")
    mlp_w.append(links.gather(packs[1]))

    embed, attn_own = embed_norm(tokens, positions, small)
    attn_other = links.swap(attn_own, "core")
    zeros = jnp.zeros((1, part), F32)
    bias_qkv = jnp.concatenate(
        [
            lax.dynamic_slice(small, (4, core * part), (1, part)),
            zeros,
            lax.dynamic_slice(small, (5, core * part), (1, part)),
        ],
        axis=1,
    )
    attn_groups = [attn_own, attn_other]
    qkv, mixed, logs = attend_forward(
        attn_groups, mine, counts_all, bias_qkv, [qkv_a, qkv_b], rows
    )
    mix_own = mixed[:each]
    mix_recv = links.swap(mixed[each:], "core")
    resid, mlp_own = project_norm(
        mix_own, mix_recv, embed, small, meta, [out_a, out_b], [out_c, out_d], rows
    )
    mlp_groups = [mlp_own, links.swap(mlp_own, "core")]
    cots = [cotangent, cot_other]
    outs, dms, bias_ups, mlp_grads = [], [], [], []
    for h in range(2):
        bias = lax.dynamic_slice(small, (8 + 2 * core + h, 0), (1, width))
        own_out, own_dm, sent_out, sent_dm, bias_up, keep, send = mlp_both(
            mlp_groups, cots, mine, counts_all, bias, list(mlp_w[h]), rows, 384, True
        )
        dms += [own_dm, links.swap(sent_dm, "core")]
        outs += [own_out, links.swap(sent_out, "core")]
        bias_ups.append(bias_up)
        mlp_grads.append(links.scatter_sum(keep, send))
    d_mix_own, d_mix_send, proj, d_resid, sums_two = norm_two_back(
        dms, resid, cotangent, small, meta, counts, [out_a, out_b], [out_c, out_d], rows, part
    )
    d_mixes = [d_mix_own, links.swap(d_mix_send, "core")]
    keep, send = out_weight_grad(mix_own, mix_recv, proj, meta, rows)
    total = keep + links.swap(send, "core").astype(F32)
    out_grad = links.scatter_sum(total[:8], total[8:].astype(BF))
    d_qkv, bias_qkv_grad, keep, send = attend_back(
        attn_groups, qkv, logs, d_mixes, mine, counts_all, rows, True
    )
    qkv_grad = links.scatter_sum(keep, send)
    da_own, da_send = attn_in_grad(d_qkv, mine, [qkv_a, qkv_b], rows, each, width)
    token_grad, sums_one = norm_one_back(
        [da_own, links.swap(da_send, "core")], embed, d_resid, small
    )
    block_rows = resid + small[7]
    for value in outs:
        block_rows = block_rows + value.astype(F32)
    block_out = block_rows.astype(BF)

    wide = lambda v: lax.dynamic_update_slice(jnp.zeros((1, width), F32), v, (0, core * part))
    hidden = lax.dynamic_update_slice(
        jnp.zeros((4, width), F32), jnp.concatenate(bias_ups, axis=0), (2 * core, 0)
    )
    small_grad = jnp.concatenate(
        [
            sums_one[:2],
            sums_two[:2],
            wide(bias_qkv_grad[:, :part]),
            wide(bias_qkv_grad[:, 2 * part :]),
            sums_two[2:4],
            hidden,
            jnp.zeros((4, width), F32),
        ],
        axis=0,
    )
    small_grad = links.sum_chips(small_grad + links.swap(small_grad, "core"))

    def both(own):
        other = links.swap(own, "core")
        first = jnp.where(core == 0, own, other)
        second = jnp.where(core == 0, other, own)
        return first, second

    halves = both(qkv_grad)
    g_qkv = jnp.stack([half.reshape(rows, 3, part) for half in halves], axis=2)
    g_qkv = g_qkv.reshape(rows, 3 * width)
    g_out = jnp.concatenate(both(out_grad), axis=1)
    quarters = [both(grad) for grad in mlp_grads]
    cut = lambda c, h: quarters[h][c]
    g_up = jnp.stack(
        [cut(c, h)[:, :width].reshape(rows, 16, rows) for c in range(2) for h in range(2)], axis=2
    ).reshape(rows, 4 * width)
    g_down = jnp.concatenate(
        [cut(c, h)[:, width:] for c in range(2) for h in range(2)], axis=0
    )
    g_small = small_table(lax.dynamic_slice(small_grad, (0, chip * rows), (16, rows)))
    grads = (g_qkv, g_out, g_up, g_down, g_small)
    squares = [square_sum(grad) for grad in grads[:4]]
    squares += [square_sum(weight) for weight in masters]
    sums = jnp.zeros((8, 128), F32).at[0, :9].set(jnp.stack(squares))
    sums = links.sum_chips(sums)[0]
    totals = jnp.concatenate([sums[:4], square_sum(small_grad)[None], sums[4:9]])
    return (block_out, token_grad) + finish(masters, moments, averages, grads, totals)


def plain_device(tokens, positions, counts, cotangent, *state):
    masters, moments, averages = state[:5], state[5:10], state[10:]
    each, length, width = tokens.shape
    full = [
        lax.all_gather(w.astype(BF), "fsdp", axis=0, tiled=True) for w in masters
    ]
    wq, wo, up, down, table = full
    table = table.astype(F32)
    vectors = jnp.concatenate([table[:, :8].T, jnp.zeros((8, width), F32)], axis=0)
    bias_up = table[:, 8:].reshape(1, -1)
    hidden = bias_up.shape[1]
    order = jnp.zeros((33,), jnp.int32)
    embed, attn_in = embed_norm(tokens, positions, vectors)
    bias_qkv = jnp.concatenate([vectors[4:5], jnp.zeros((1, width), F32), vectors[5:6]], axis=1)
    qkv, mixed, logs = attend_forward([attn_in], order, counts, bias_qkv, [wq[None]], width)
    resid, mlp_in = project_norm(mixed, None, embed, vectors, order, [wo[None]], [], width)
    outs, dms, bias_ups, ups, downs = [], [], [], [], []
    parts = 4
    size = hidden // parts
    for h in range(parts):
        cols = slice(h * size, (h + 1) * size)
        out, dm, bias, g_up, g_down = mlp_both(
            [mlp_in],
            [cotangent],
            order,
            counts,
            bias_up[:, cols],
            [up[:, cols][None], down[cols][None]],
            width,
            size // 2,
            False,
        )
        outs.append(out)
        dms.append(dm)
        bias_ups.append(bias)
        ups.append(g_up[0])
        downs.append(g_down[0])
    d_mix, proj, d_resid, sums_two = norm_two_back(
        dms, resid, cotangent, vectors, order, counts, [wo[None]], [], width, width
    )
    g_out = out_weight_grad(mixed, None, proj, order, width)[0][0]
    d_qkv, bias_grad, g_qkv = attend_back(
        [attn_in], qkv, logs, [d_mix], order, counts, width, False
    )
    g_qkv = g_qkv[0]
    da = attn_in_grad(d_qkv, order, [wq[None]], width, each, width)[0]
    token_grad, sums_one = norm_one_back([da], embed, d_resid, vectors)
    block_rows = resid + vectors[7]
    for value in outs:
        block_rows = block_rows + value
    block_out = block_rows.astype(BF)
    columns = jnp.stack(
        [
            sums_one[0],
            sums_one[1],
            sums_two[0],
            sums_two[1],
            bias_grad[0, :width],
            bias_grad[0, 2 * width :],
            sums_two[2],
            sums_two[3],
        ],
        axis=1,
    )
    small = jnp.concatenate(
        [columns, jnp.concatenate(bias_ups, axis=1).reshape(width, -1)], axis=1
    )
    partial = (
        g_qkv,
        g_out,
        jnp.concatenate(ups, axis=1),
        jnp.concatenate(downs, axis=0),
        small,
    )
    grads = []
    for grad in partial:
        shard = lax.psum_scatter(grad, "fsdp", scatter_dimension=0, tiled=True)
        grads.append(lax.psum(shard, "dp"))
    squares = jnp.stack([square_sum(g) for g in grads] + [square_sum(w) for w in masters])
    totals = lax.psum(squares, "fsdp")
    return (block_out, token_grad) + finish(masters, moments, averages, tuple(grads), totals)


def solution(mesh):
    clips = P(("dp", "fsdp"), None, None)
    in_specs = (clips, P(("dp", "fsdp"), None), P(("dp", "fsdp")), clips) + (P("fsdp", None),) * 15
    out_specs = (clips, clips) + (P("fsdp", None),) * 15 + (P(),)
    links = Links(mesh.shape["dp"], mesh.shape["fsdp"])

    def on_device(*args):
        if links.paired:
            return paired_device(links, *args)
        return plain_device(*args)

    return jax.shard_map(
        on_device, mesh=mesh, in_specs=in_specs, out_specs=out_specs, check_vma=False
    )
```

```python
import math

import jax
import jax.numpy as jnp
import numpy as np
from jax import lax
from jax.experimental import pallas as pl
from jax.experimental.pallas import tpu as pltpu
from jax.sharding import PartitionSpec as P

HEAD_DIM = 64
EPS_NORM = 1e-06
MOMENTUM_DECAY = 0.9
WEIGHT_DECAY = 0.0001
TRUST_RATE = 0.2
AVERAGE_DECAY = 0.8
NEG = -1000000000.0
LEAST = 60

BF = jnp.bfloat16
F32 = jnp.float32
AXES = ("dp", "fsdp")
SHORT = pl.CostEstimate(flops=1, bytes_accessed=1, transcendentals=0)
ANY = pl.BlockSpec(memory_space=pl.ANY)
SMEM = pl.BlockSpec(memory_space=pltpu.SMEM)


def params(mib):
    return pltpu.CompilerParams(
        vmem_limit_bytes=max(mib, LEAST) * 1024 * 1024, dimension_semantics=("arbitrary",)
    )


def dot(a, b):
    return lax.dot_general(a, b, (((1,), (0,)), ((), ())), preferred_element_type=F32)


def dot_nt(a, b):
    return lax.dot_general(a, b, (((1,), (1,)), ((), ())), preferred_element_type=F32)


def dot_tn(a, b):
    return lax.dot_general(a, b, (((0,), (0,)), ((), ())), preferred_element_type=F32)


def whole(shape):
    zeros = (0,) * len(shape)
    return pl.BlockSpec(shape, lambda *i: zeros)


class Links:
    def __init__(self, dp, fsdp):
        self.paired = dp == 2 and fsdp == 16
        self.bits = ((4, 4), (8, 8), (1, 2), (2, 1))

    def masks(self):
        table = np.zeros((2, 16), np.int32)
        for core in range(2):
            for p in range(16):
                for bit in range(4):
                    if p >> bit & 1:
                        table[core, p] ^= self.bits[bit][core]
        return table

    def flip(self, x, p):
        table = self.masks()
        pairs = [(c * 16 + f, c * 16 + (f ^ int(table[c, p]))) for c in range(2) for f in range(16)]
        return lax.ppermute(x, AXES, pairs)

    def cross(self, x):
        pairs = [(c * 16 + f, (1 - c) * 16 + f) for c in range(2) for f in range(16)]
        return lax.ppermute(x, AXES, pairs)

    def along_z(self, blocks):
        return [self.flip(block, p) for p, block in zip((1, 2, 3), blocks)]

    def sum_all(self, x):
        x = x + self.cross(x)
        for step in (1, 4):
            one, two, three = [self.flip(x, step * p) for p in (1, 2, 3)]
            x = (x + one) + (two + three)
        return x


def assemble(pieces, order, rows, target, sems, at=0, columns=None):
    copies = []
    n = 0
    for piece in pieces:
        for j in range(piece.shape[0]):
            source = piece.at[j] if columns is None else piece.at[j, :, columns]
            start = pl.multiple_of(order(n) * rows, 16)
            copies.append(
                pltpu.make_async_copy(source, target.at[pl.ds(start, rows)], sems.at[at + n])
            )
            n += 1
    return copies


def deliver(source, order, rows, first, targets, sems, at=0, columns=None):
    copies = []
    n = first
    for target in targets:
        for j in range(target.shape[0]):
            start = pl.multiple_of(order(n) * rows, 16)
            place = target.at[j] if columns is None else target.at[j, :, columns]
            copies.append(
                pltpu.make_async_copy(source.at[pl.ds(start, rows)], place, sems.at[at + n - first])
            )
            n += 1
    return copies


def run_all(copies):
    for copy in copies:
        copy.start()
    for copy in copies:
        copy.wait()


def norm_parts(values):
    center = values - jnp.mean(values, axis=-1, keepdims=True)
    inv = lax.rsqrt(jnp.mean(center * center, axis=-1, keepdims=True) + EPS_NORM)
    return center * inv, inv


def norm_back(u, hat, inv):
    first = jnp.mean(u, axis=-1, keepdims=True)
    second = jnp.mean(u * hat, axis=-1, keepdims=True)
    return inv * (u - first - hat * second)


def embed_kernel(each, n_groups):
    def kernel(table, *refs):
        toks, poss = refs[:n_groups], refs[n_groups : 2 * n_groups]
        embed = refs[-1]
        step = pl.program_id(0)
        p = choose(poss, step, each)
        turns = p * table[0:1, :]
        turns = turns - jnp.round(turns)
        turns = turns + (p * table[1:2, :] + table[2:3, :])
        turns = turns - jnp.round(turns)
        fold = jnp.where(turns > 0.25, 0.5 - turns, jnp.where(turns < -0.25, -0.5 - turns, turns))
        x = fold * (2.0 * math.pi)
        x2 = x * x
        poly = -1.0 / 39916800.0
        for coef in (1.0 / 362880.0, -1.0 / 5040.0, 1.0 / 120.0, -1.0 / 6.0, 1.0):
            poly = poly * x2 + coef
        embed[0] = choose(toks, step, each).astype(F32) + x * poly

    return kernel


def embed_rows(tokens, positions):
    each, length, width = tokens[0].shape
    exact = 10000.0 ** (-2.0 * (np.arange(width) // 2) / width) / (2.0 * math.pi)
    scale = 2.0 ** (11 - np.floor(np.log2(exact)))
    high = np.round(exact * scale) / scale
    table = np.zeros((8, width), np.float32)
    table[0], table[1], table[2] = high, exact - high, 0.25 * (np.arange(width) % 2)
    specs, clips = pair_specs(tokens, (length, width))
    pos_specs, _ = pair_specs(positions, (length, 1))
    size = clips * length * width
    return pl.pallas_call(
        embed_kernel(each, len(tokens)),
        grid=(clips,),
        in_specs=[whole((8, width))] + specs + pos_specs,
        out_specs=pl.BlockSpec((1, length, width), lambda i: (i, 0, 0)),
        out_shape=jax.ShapeDtypeStruct((clips, length, width), F32),
        compiler_params=params(24),
        cost_estimate=SHORT,
        name="embed_rows",
    )(jnp.asarray(table), *tokens, *positions)


def pair_specs(groups, block, column=0):
    specs, first = [], 0
    for array in groups:
        n = array.shape[0]

        def index(*at, first=first, n=n):
            return (jnp.clip(at[-1] - first, 0, n - 1), 0, column)

        specs.append(pl.BlockSpec((1,) + block, index))
        first += n
    return specs, first


def choose(refs, step, each):
    value = refs[0][0]
    for k in range(1, len(refs)):
        value = jnp.where(step >= k * each, refs[k][0], value)
    return value


def attend_forward(
    sources, small, order, core, counts, pieces, rows, each, first, heads, apart, block
):
    length, width = sources[0].shape[1:]
    source_each, n_sources = sources[0].shape[0], len(sources)
    source_specs, clips = pair_specs(sources, (length, width))
    part = heads * HEAD_DIM
    columns = 3 * part
    fresh = sources[0].dtype == F32
    gathered = small is None
    total_columns = columns + (128 if gathered else 0)
    split = clips > each
    n_pieces = len(pieces)
    blocks = sum(piece.shape[0] for piece in pieces)
    smalls = [] if gathered else [small]

    def kernel(order_ref, core_ref, count_ref, *refs):
        source_refs = refs[:n_sources]
        refs = list(refs[n_sources:])
        small_in = None if gathered else refs.pop(0)
        piece_refs = refs[:n_pieces]
        refs = refs[n_pieces:]
        vectors = refs.pop(0) if gathered else small_in
        normed = refs.pop(0) if fresh else None
        qkv, logs, mixes = refs[0], refs[1], refs[2 : 4 if split else 3]
        weight, bias, sems = refs[-3:]
        step = pl.program_id(0)

        @pl.when(step == 0)
        def _():
            cut = slice(columns * block, columns * block + columns)
            target = weight.at[:, :columns]
            copies = assemble(piece_refs, lambda n: order_ref[n], rows, target, sems, 0, cut)
            if gathered:
                last = piece_refs[0].shape[2]
                target = weight.at[:, columns:]
                cut = slice(last - 128, last)
                copies += assemble(
                    piece_refs, lambda n: order_ref[n], rows, target, sems, blocks, cut
                )
            run_all(copies)
            if gathered:
                vectors[...] = weight[:, columns:].astype(F32).T[:16]
            bias[...] = jnp.zeros_like(bias)
            for pair in range(heads // 2):
                head = first + core_ref[0] * apart + 2 * pair
                at = pl.ds(pl.multiple_of(head * HEAD_DIM, 128), 128)
                bias[0:1, 384 * pair : 384 * pair + 128] = vectors[4:5, at]
                bias[0:1, 384 * pair + 256 : 384 * pair + 384] = vectors[5:6, at]

        if fresh:
            hat, _ = norm_parts(choose(source_refs, step, source_each))
            x = (hat * vectors[0:1, :] + vectors[1:2, :]).astype(BF)
            normed[0] = x
        else:
            x = choose(source_refs, step, source_each)
        low = (dot(x, weight[:, :columns]) + bias[0:1, :]).astype(BF)
        qkv[0] = low
        valid = lax.broadcasted_iota(jnp.int32, (length, 1), 0) < count_ref[step]
        lane = lax.broadcasted_iota(jnp.int32, (1, 2 * HEAD_DIM), 1)
        outs, log_rows = [], []
        for pair in range(heads // 2):
            at = 384 * pair
            q = low[:, at : at + 128] * jnp.asarray(HEAD_DIM**-0.5, BF)
            k = low[:, at + 128 : at + 256]
            v = low[:, at + 256 : at + 384]
            mixed_heads = []
            for half in range(2):
                mine = (lane >= HEAD_DIM) if half else (lane < HEAD_DIM)
                s = dot_nt(jnp.where(mine, k, jnp.zeros_like(k)), q)
                s = jnp.where(valid, s, NEG)
                top = jnp.max(s, axis=0, keepdims=True)
                e = jnp.exp(s - top)
                total = jnp.sum(e, axis=0, keepdims=True)
                p = (e * (1.0 / total)).astype(BF)
                mixed_heads.append(dot_tn(p, v))
                log_rows.append(top + jnp.log(total))
            outs.append(jnp.where(lane < HEAD_DIM, mixed_heads[0], mixed_heads[1]))
        mixed = jnp.concatenate(outs, axis=1).astype(BF)
        logs[0] = jnp.concatenate(log_rows, axis=0)
        if split:

            @pl.when(step < each)
            def _():
                mixes[0][0] = mixed

            @pl.when(step >= each)
            def _():
                mixes[1][0] = mixed

        else:
            mixes[0][0] = mixed

    clip = lambda c: pl.BlockSpec((1, length, c), lambda i: (i, 0, 0))
    own = pl.BlockSpec((1, length, part), lambda i: (jnp.minimum(i, each - 1), 0, 0))
    other = pl.BlockSpec((1, length, part), lambda i: (jnp.clip(i - each, 0, each - 1), 0, 0))
    out_specs, out_shapes = [], []
    if gathered:
        out_specs.append(whole((16, width)))
        out_shapes.append(jax.ShapeDtypeStruct((16, width), F32))
    if fresh:
        out_specs.append(clip(width))
        out_shapes.append(jax.ShapeDtypeStruct((clips, length, width), BF))
    out_specs += [clip(columns), pl.BlockSpec((1, heads, length), lambda i: (i, 0, 0)), own]
    out_shapes += [
        jax.ShapeDtypeStruct((clips, length, columns), BF),
        jax.ShapeDtypeStruct((clips, heads, length), F32),
        jax.ShapeDtypeStruct((each, length, part), BF),
    ]
    if split:
        out_specs.append(other)
        out_shapes.append(jax.ShapeDtypeStruct((clips - each, length, part), BF))
    n_rows = clips * length
    return pl.pallas_call(
        kernel,
        grid=(clips,),
        in_specs=[SMEM, SMEM, SMEM]
        + source_specs
        + [whole((16, width))] * len(smalls)
        + [ANY] * n_pieces,
        out_specs=out_specs,
        out_shape=out_shapes,
        scratch_shapes=[
            pltpu.VMEM((width, total_columns), BF),
            pltpu.VMEM((8, columns), F32),
            pltpu.SemaphoreType.DMA((2 * blocks,)),
        ],
        compiler_params=params(48),
        cost_estimate=SHORT,
        name="attend_forward",
    )(order, core, counts, *sources, *smalls, *pieces)


def out_weight_copies(own, other, meta, rows, weight, sems):
    cut = slice(own[0].shape[2] - weight.shape[2], None)
    if other is None:
        return assemble(own, lambda n: meta[1 + n], rows, weight.at[0], sems, 0, cut)
    core = meta[0]
    copies = assemble(own, lambda n: meta[1 + n], rows, weight.at[core], sems, 0, cut)
    return copies + assemble(other, lambda n: meta[17 + n], rows, weight.at[1 - core], sems, 16)


def project_norm(mixes, places, embed, small, meta, pieces, others, rows):
    n, length, width = mixes[0].shape[0], embed.shape[1], embed.shape[2]
    parts = [mix.shape[2] for mix in mixes]
    n_mix, n_p, n_o = len(mixes), len(pieces), len(others)
    halves = 2 if others else 1
    half_width = width // halves

    def kernel(meta_ref, small_ref, embed_ref, *refs):
        mix_refs = refs[:n_mix]
        own_refs = refs[n_mix : n_mix + n_p]
        other_refs = refs[n_mix + n_p : n_mix + n_p + n_o] or None
        resid, mlp_in, weight, sems = refs[n_mix + n_p + n_o :]

        @pl.when(pl.program_id(0) == 0)
        def _():
            run_all(out_weight_copies(own_refs, other_refs, meta_ref, rows, weight, sems))

        outs = []
        for half in range(halves):
            total = 0.0
            for k, mix in enumerate(mix_refs):
                flip, first = places[k]
                at = first
                if halves > 1:
                    at = pl.multiple_of((meta_ref[0] ^ flip) * half_width + first, 128)
                total = total + dot(mix[0], weight[half, pl.ds(at, parts[k]), :])
            outs.append(total)
        total = jnp.concatenate(outs, axis=1) if halves > 1 else outs[0]
        values = embed_ref[0] + total + small_ref[6:7, :]
        resid[0] = values
        hat, _ = norm_parts(values)
        mlp_in[0] = (hat * small_ref[2:3, :] + small_ref[3:4, :]).astype(BF)

    clip = pl.BlockSpec((1, length, width), lambda i: (i, 0, 0))
    mix_specs = [pl.BlockSpec((1, length, c), lambda i: (i, 0, 0)) for c in parts]
    size = n * length * width
    return pl.pallas_call(
        kernel,
        grid=(n,),
        in_specs=[SMEM, whole((16, width)), clip] + mix_specs + [ANY] * (n_p + n_o),
        out_specs=[clip, clip],
        out_shape=[
            jax.ShapeDtypeStruct((n, length, width), F32),
            jax.ShapeDtypeStruct((n, length, width), BF),
        ],
        scratch_shapes=[
            pltpu.VMEM((halves, width, half_width), BF),
            pltpu.SemaphoreType.DMA((32,)),
        ],
        compiler_params=params(24),
        cost_estimate=SHORT,
        name="project_norm",
    )(meta, small, embed, *mixes, *pieces, *others)


def mlp_both(groups, cots, order, counts, bias, pieces, rows, relative):
    each, length, width = groups[0].shape
    hidden = bias.shape[1]
    n_groups, n_pieces = len(groups), len(pieces)
    n_blocks = sum(piece.shape[0] for piece in pieces)
    hidden_rows = hidden // n_blocks
    specs, clips = pair_specs(groups, (length, width))
    if relative:
        half = n_blocks // 2
        grad_shapes = [
            jax.ShapeDtypeStruct((half, rows, 2 * width), F32),
            jax.ShapeDtypeStruct((half, rows, 2 * width), BF),
        ]
    else:
        grad_shapes = [
            jax.ShapeDtypeStruct((1, width, hidden), F32),
            jax.ShapeDtypeStruct((1, hidden, width), F32),
        ]
    own_shape = (each, length, width)
    out_shapes = [jax.ShapeDtypeStruct(own_shape, F32)] * 2
    if n_groups > 1:
        out_shapes += [jax.ShapeDtypeStruct(own_shape, BF)] * 2
    out_shapes += [jax.ShapeDtypeStruct((1, hidden), F32)]

    def kernel(order_ref, count_ref, bias_ref, *refs):
        ins = refs[:n_groups]
        cot_refs = refs[n_groups : 2 * n_groups]
        piece_refs = refs[2 * n_groups : 2 * n_groups + n_pieces]
        outs = refs[2 * n_groups + n_pieces :]
        own_out, own_dm = outs[0], outs[1]
        sent = outs[2:4] if n_groups > 1 else None
        n_out = 4 if n_groups > 1 else 2
        bias_grad = outs[n_out]
        grad_a, grad_b = outs[n_out + 1 : n_out + 3]
        (up, down, g_up, g_down, low_up, low_down, sems) = outs[n_out + 3 :]
        i = pl.program_id(0)
        place = lambda n: order_ref[n]

        @pl.when(i == 0)
        def _():
            copies = assemble(piece_refs, place, rows, up, sems, 0, slice(0, hidden))
            if relative:
                copies += assemble(
                    piece_refs, place, hidden_rows, down, sems, n_blocks, slice(hidden, None)
                )
            else:
                copies = [
                    pltpu.make_async_copy(piece_refs[0].at[0], up, sems.at[0]),
                    pltpu.make_async_copy(piece_refs[1].at[0], down, sems.at[1]),
                ]
            run_all(copies)

        x = choose(ins, i, each)
        valid = lax.broadcasted_iota(jnp.int32, (length, 1), 0) < count_ref[i]
        cot = choose(cot_refs, i, each)
        dd = jnp.where(valid, cot, jnp.zeros_like(cot))
        pre = dot(x, up[...]) + bias_ref[...]
        cdf = 0.5 + 0.5 * lax.erf(pre * 0.7071067811865476)
        pdf = jnp.exp(pre * pre * -0.5) * 0.3989422804014327
        act = (pre * cdf).astype(BF)
        d_pre = (dot_nt(dd, down[...]) * (cdf + pre * pdf)).astype(BF)
        out = dot(act, down[...])
        dm = dot_nt(d_pre, up[...])
        up_part = dot(x.T, d_pre)
        down_part = dot(act.T, dd)
        bias_part = jnp.sum(d_pre.astype(F32), axis=0, keepdims=True)

        @pl.when(i < each)
        def _():
            own_out[0] = out
            own_dm[0] = dm

        if sent is not None:

            @pl.when(i >= each)
            def _():
                sent[0][0] = out.astype(BF)
                sent[1][0] = dm.astype(BF)

        @pl.when(i == 0)
        def _():
            g_up[...] = up_part
            g_down[...] = down_part
            bias_grad[...] = bias_part

        @pl.when((i > 0) & (i < clips - 1))
        def _():
            g_up[...] += up_part
            g_down[...] += down_part
            bias_grad[...] += bias_part

        @pl.when(i == clips - 1)
        def _():
            bias_grad[...] += bias_part
            if relative:
                total_up = g_up[...] + up_part
                g_up[...] = total_up
                low_up[...] = total_up.astype(BF)
                one, two = slice(0, width), slice(width, 2 * width)
                copies = deliver(g_up, place, rows, 0, [grad_a], sems, 0, one)
                copies += deliver(low_up, place, rows, half, [grad_b], sems, half, one)
                for copy in copies:
                    copy.start()
                total_down = g_down[...] + down_part
                g_down[...] = total_down
                low_down[...] = total_down.astype(BF)
                more = deliver(g_down, place, rows, 0, [grad_a], sems, 2 * half, two)
                more += deliver(low_down, place, rows, half, [grad_b], sems, 3 * half, two)
                for copy in more:
                    copy.start()
                for copy in copies + more:
                    copy.wait()
            else:
                g_up[...] += up_part
                g_down[...] += down_part
                copies = [
                    pltpu.make_async_copy(g_up, grad_a.at[0], sems.at[0]),
                    pltpu.make_async_copy(g_down, grad_b.at[0], sems.at[1]),
                ]
                run_all(copies)

    own_index = lambda i: (jnp.minimum(i, each - 1), 0, 0)
    sent_index = lambda i: (jnp.clip(i - each, 0, each - 1), 0, 0)
    out_specs = [pl.BlockSpec((1, length, width), own_index)] * 2
    if n_groups > 1:
        out_specs += [pl.BlockSpec((1, length, width), sent_index)] * 2
    out_specs += [whole((1, hidden)), ANY, ANY]
    low_shape = (width, hidden) if relative else (16, 128)
    low_shape_down = (hidden, width) if relative else (16, 128)
    n_rows = clips * length
    return pl.pallas_call(
        kernel,
        grid=(clips,),
        in_specs=[SMEM, SMEM, whole((1, hidden))] + specs + specs + [ANY] * n_pieces,
        out_specs=out_specs,
        out_shape=out_shapes + grad_shapes,
        scratch_shapes=[
            pltpu.VMEM((width, hidden), BF),
            pltpu.VMEM((hidden, width), BF),
            pltpu.VMEM((width, hidden), F32),
            pltpu.VMEM((hidden, width), F32),
            pltpu.VMEM(low_shape, BF),
            pltpu.VMEM(low_shape_down, BF),
            pltpu.SemaphoreType.DMA((max(2 * n_blocks, 2),)),
        ],
        compiler_params=params(56),
        cost_estimate=SHORT,
        name="mlp_both",
    )(order, counts, bias, *groups, *cots, *pieces)


def norm_two_back(dms, resid, cot, small, meta, counts, pieces, others, rows, part):
    n, length, width = resid.shape
    n_dm, n_p, n_o = len(dms), len(pieces), len(others)
    halves = 2 if others else 1
    half_width = width // halves

    def kernel(meta_ref, count_ref, small_ref, resid_ref, cot_ref, *refs):
        dm_refs = refs[:n_dm]
        own_refs = refs[n_dm : n_dm + n_p]
        other_refs = refs[n_dm + n_p : n_dm + n_p + n_o] or None
        outs = refs[n_dm + n_p + n_o :]
        mixes = outs[: halves]
        proj, d_resid, sums, weight, sems = outs[halves:]
        step = pl.program_id(0)

        @pl.when(step == 0)
        def _():
            run_all(out_weight_copies(own_refs, other_refs, meta_ref, rows, weight, sems))

        valid = lax.broadcasted_iota(jnp.int32, (length, 1), 0) < count_ref[step]
        dy = jnp.where(valid, cot_ref[0].astype(F32), 0.0)
        dm = dm_refs[0][0].astype(F32)
        for ref in dm_refs[1:]:
            dm = dm + ref[0].astype(F32)
        hat, inv = norm_parts(resid_ref[0])
        total = dy + norm_back(dm * small_ref[2:3, :], hat, inv)
        d_resid[0] = total
        low = total.astype(BF)
        proj[0] = low
        row = lambda v: jnp.sum(v, axis=0, keepdims=True)
        parts = jnp.concatenate(
            [row(dm * hat), row(dm), row(low.astype(F32)), row(dy), jnp.zeros((4, width), F32)]
        )
        for k in range(halves):
            at = pl.multiple_of((meta_ref[0] ^ k) * part, 128) if halves > 1 else 0
            value = 0.0
            for half in range(halves):
                cut = low[:, half * half_width : (half + 1) * half_width]
                value = value + dot_nt(cut, weight[half, pl.ds(at, part), :])
            mixes[k][0] = value.astype(BF)

        @pl.when(step == 0)
        def _():
            sums[...] = parts

        @pl.when(step > 0)
        def _():
            sums[...] += parts

    clip = pl.BlockSpec((1, length, width), lambda i: (i, 0, 0))
    mix_spec = pl.BlockSpec((1, length, part), lambda i: (i, 0, 0))
    shape = resid.shape
    mix_shape = jax.ShapeDtypeStruct((n, length, part), BF)
    return pl.pallas_call(
        kernel,
        grid=(n,),
        in_specs=[SMEM, SMEM, whole((16, width)), clip, clip]
        + [clip] * n_dm
        + [ANY] * (n_p + n_o),
        out_specs=[mix_spec] * halves + [clip, clip, whole((8, width))],
        out_shape=[mix_shape] * halves
        + [
            jax.ShapeDtypeStruct(shape, BF),
            jax.ShapeDtypeStruct(shape, F32),
            jax.ShapeDtypeStruct((8, width), F32),
        ],
        scratch_shapes=[
            pltpu.VMEM((halves, width, half_width), BF),
            pltpu.SemaphoreType.DMA((32,)),
        ],
        compiler_params=params(32),
        cost_estimate=SHORT,
        name="norm_two_back",
    )(meta, counts, small, resid, cot, *dms, *pieces, *others)


def out_weight_grad(mixes, places, proj, meta, rows):
    n, length, width = proj.shape
    parts = [mix.shape[2] for mix in mixes]
    n_mix = len(mixes)
    halves = 2 if any(flip for flip, _ in places) else 1
    half_width = width // halves
    blocks = width // rows

    def kernel(meta_ref, proj_ref, *refs):
        mix_refs = refs[:n_mix]
        if halves > 1:
            keep, send, total, low, sems = refs[n_mix:]
        else:
            keep, total, sems = refs[n_mix:]
        step = pl.program_id(0)

        @pl.when(step == 0)
        def _():
            total[...] = jnp.zeros_like(total)

        for k in range(n_mix):
            turned = mix_refs[k][0].T
            flip, at = places[k]
            if halves > 1:
                at = pl.multiple_of((meta_ref[0] ^ flip) * half_width + at, 128)
            for half in range(halves):
                cut = proj_ref[0, :, half * half_width : (half + 1) * half_width]
                total[half, pl.ds(at, parts[k]), :] += dot(turned, cut)

        @pl.when(step == n - 1)
        def _():
            if halves > 1:
                core = meta_ref[0]
                low[...] = total[1 - core].astype(BF)
                copies = deliver(
                    total.at[core], lambda n: meta_ref[1 + n], rows, 0, [keep], sems, 0
                )
                copies += deliver(low, lambda n: meta_ref[17 + n], rows, 0, [send], sems, blocks)
                run_all(copies)
            else:
                run_all([pltpu.make_async_copy(total, keep, sems.at[0])])

    clip = lambda c: pl.BlockSpec((1, length, c), lambda i: (i, 0, 0))
    if halves > 1:
        shapes = [
            jax.ShapeDtypeStruct((blocks, rows, half_width), F32),
            jax.ShapeDtypeStruct((blocks, rows, half_width), BF),
        ]
        scratch = [
            pltpu.VMEM((halves, width, half_width), F32),
            pltpu.VMEM((width, half_width), BF),
            pltpu.SemaphoreType.DMA((2 * blocks,)),
        ]
    else:
        shapes = [jax.ShapeDtypeStruct((1, width, width), F32)]
        scratch = [pltpu.VMEM((1, width, width), F32), pltpu.SemaphoreType.DMA((1,))]
    return pl.pallas_call(
        kernel,
        grid=(n,),
        in_specs=[SMEM, clip(width)] + [clip(c) for c in parts],
        out_specs=[ANY] * len(shapes),
        out_shape=shapes,
        scratch_shapes=scratch,
        compiler_params=params(24),
        cost_estimate=SHORT,
        name="out_weight_grad",
    )(meta, proj, *mixes)


def attend_back(groups, qkv, logs, d_mixes, order, counts, rows, relative, first, at_pair, pairs):
    each, length, width = groups[0].shape
    clips = qkv.shape[0]
    columns, part = 384 * pairs, 128 * pairs
    all_heads = logs.shape[1]
    n_groups = len(groups)
    n_mix = len(d_mixes)
    specs, _ = pair_specs(groups, (length, width))
    mix_each = d_mixes[0].shape[0]
    mix_specs, _ = pair_specs(d_mixes, (length, part), at_pair // pairs)
    blocks = width // rows
    half_blocks = blocks // 2

    def kernel(order_ref, count_ref, qkv_ref, log_ref, *refs):
        ins = refs[:n_groups]
        mix_refs = refs[n_groups : n_groups + n_mix]
        refs = refs[n_groups + n_mix :]
        d_qkv, bias_grad = refs[:2]
        if relative:
            keep, send, total, low, sems = refs[2:]
        else:
            keep, total, sems = refs[2:]
        step = pl.program_id(0)
        valid = lax.broadcasted_iota(jnp.int32, (length, 1), 0) < count_ref[step]
        lane = lax.broadcasted_iota(jnp.int32, (1, 2 * HEAD_DIM), 1)
        d_mix = choose(mix_refs, step, mix_each)
        pieces = []
        scale = HEAD_DIM**-0.5
        for pair in range(pairs):
            at = 384 * pair
            q = qkv_ref[0, :, at : at + 128] * jnp.asarray(scale, BF)
            k = qkv_ref[0, :, at + 128 : at + 256]
            v = qkv_ref[0, :, at + 256 : at + 384]
            do = d_mix[:, 128 * pair : 128 * pair + 128]
            k_t = k.T
            dk = dv = None
            turned_q = []
            for half in range(2):
                mine = (lane >= HEAD_DIM) if half else (lane < HEAD_DIM)
                only = lambda x: jnp.where(mine, x, jnp.zeros_like(x))
                s = dot_nt(only(k), q)
                h = 2 * (first + pair) + half
                p = jnp.exp(jnp.where(valid, s, NEG) - log_ref[0, h : h + 1, :])
                dp = dot_nt(only(v), do)
                inner = jnp.sum(dp * p, axis=0, keepdims=True)
                ds = (p * (dp - inner)).astype(BF)
                dv_half = dot(p.astype(BF), only(do))
                dk_half = dot(ds, only(q))
                dv = dv_half if dv is None else dv + dv_half
                dk = dk_half if dk is None else dk + dk_half
                turned_q.append(dot(k_t[HEAD_DIM * half : HEAD_DIM * half + HEAD_DIM], ds))
            pieces += [(jnp.concatenate(turned_q, axis=0) * scale).T, dk, dv]
        low_rows = jnp.concatenate(pieces, axis=1).astype(BF)
        d_qkv[0] = low_rows
        bias_part = jnp.sum(low_rows.astype(F32), axis=0, keepdims=True)
        weight_part = dot(choose(ins, step, each).T, low_rows)

        @pl.when(step == 0)
        def _():
            total[...] = weight_part
            bias_grad[...] = bias_part

        @pl.when(step > 0)
        def _():
            total[...] += weight_part
            bias_grad[...] += bias_part

        @pl.when(step == clips - 1)
        def _():
            place = lambda n: order_ref[n]
            if relative:
                low[...] = total[...].astype(BF)
                copies = deliver(total, place, rows, 0, [keep], sems, 0)
                copies += deliver(low, place, rows, half_blocks, [send], sems, half_blocks)
                run_all(copies)
            else:
                run_all([pltpu.make_async_copy(total, keep.at[0], sems.at[0])])

    clip = lambda c: pl.BlockSpec((1, length, c), lambda i: (i, 0, 0))
    block_at = first // pairs
    qkv_spec = pl.BlockSpec((1, length, columns), lambda i: (i, 0, block_at))
    if relative:
        shapes = [
            jax.ShapeDtypeStruct((half_blocks, rows, columns), F32),
            jax.ShapeDtypeStruct((half_blocks, rows, columns), BF),
        ]
        scratch = [pltpu.VMEM((width, columns), F32), pltpu.VMEM((width, columns), BF)]
    else:
        shapes = [jax.ShapeDtypeStruct((1, width, columns), F32)]
        scratch = [pltpu.VMEM((width, columns), F32)]
    n_rows = clips * length
    return pl.pallas_call(
        kernel,
        grid=(clips,),
        in_specs=[
            SMEM,
            SMEM,
            qkv_spec,
            pl.BlockSpec((1, all_heads, length), lambda i: (i, 0, 0)),
        ]
        + specs
        + mix_specs,
        out_specs=[clip(columns), whole((1, columns))] + [ANY] * len(shapes),
        out_shape=[
            jax.ShapeDtypeStruct((clips, length, columns), BF),
            jax.ShapeDtypeStruct((1, columns), F32),
        ]
        + shapes,
        scratch_shapes=scratch + [pltpu.SemaphoreType.DMA((blocks,))],
        compiler_params=params(48),
        cost_estimate=SHORT,
        name="attend_back",
    )(order, counts, qkv, logs, *groups, *d_mixes)


def attn_in_grad(d_qkvs, order, pieces, rows, each, width):
    clips, length, _ = d_qkvs[0].shape
    sizes = [d.shape[2] for d in d_qkvs]
    total = sum(sizes)
    n_d = len(d_qkvs)
    flat = [array for arrays, _ in pieces for array in arrays]
    blocks = sum(array.shape[0] for array in flat)
    split = clips > each

    def kernel(order_ref, *refs):
        row_refs = refs[:n_d]
        piece_refs = refs[n_d : n_d + len(flat)]
        outs = refs[n_d + len(flat) :]
        weight, sems = outs[-2:]
        step = pl.program_id(0)

        @pl.when(step == 0)
        def _():
            copies, used, column = [], 0, 0
            for arrays, size in pieces:
                refs_here = piece_refs[used : used + len(arrays)]
                target = weight.at[:, column : column + size]
                copies += assemble(
                    refs_here, lambda n: order_ref[n], rows, target, sems, len(copies), slice(0, size)
                )
                used += len(arrays)
                column += size
            run_all(copies)

        low = jnp.concatenate([ref[0] for ref in row_refs], axis=1) if n_d > 1 else row_refs[0][0]
        value = dot_nt(low, weight[...])
        if split:

            @pl.when(step < each)
            def _():
                outs[0][0] = value

            @pl.when(step >= each)
            def _():
                outs[1][0] = value.astype(BF)
        else:
            outs[0][0] = value

    own = pl.BlockSpec((1, length, width), lambda i: (jnp.minimum(i, each - 1), 0, 0))
    other = pl.BlockSpec((1, length, width), lambda i: (jnp.clip(i - each, 0, each - 1), 0, 0))
    shapes = [jax.ShapeDtypeStruct((each, length, width), F32)]
    if split:
        shapes.append(jax.ShapeDtypeStruct((each, length, width), BF))
    return pl.pallas_call(
        kernel,
        grid=(clips,),
        in_specs=[SMEM]
        + [pl.BlockSpec((1, length, c), lambda i: (i, 0, 0)) for c in sizes]
        + [ANY] * len(flat),
        out_specs=[own, other][: len(shapes)],
        out_shape=shapes,
        scratch_shapes=[pltpu.VMEM((width, total), BF), pltpu.SemaphoreType.DMA((blocks,))],
        compiler_params=params(32),
        cost_estimate=SHORT,
        name="attn_in_grad",
    )(order, *d_qkvs, *flat)


def norm_one_back(das, embed, d_resid, small):
    n, length, width = d_resid.shape
    n_da = len(das)

    def kernel(small_ref, embed_ref, resid_ref, *refs):
        da_refs = refs[:n_da]
        grad, sums = refs[n_da:]
        step = pl.program_id(0)
        da = da_refs[0][0].astype(F32)
        for ref in da_refs[1:]:
            da = da + ref[0].astype(F32)
        hat, inv = norm_parts(embed_ref[0])
        grad[0] = resid_ref[0] + norm_back(da * small_ref[0:1, :], hat, inv)
        row = lambda v: jnp.sum(v, axis=0, keepdims=True)
        parts = jnp.concatenate([row(da * hat), row(da), jnp.zeros((6, width), F32)])

        @pl.when(step == 0)
        def _():
            sums[...] = parts

        @pl.when(step > 0)
        def _():
            sums[...] += parts

    clip = pl.BlockSpec((1, length, width), lambda i: (i, 0, 0))
    return pl.pallas_call(
        kernel,
        grid=(n,),
        in_specs=[whole((16, width)), clip, clip] + [clip] * n_da,
        out_specs=[clip, whole((8, width))],
        out_shape=[
            jax.ShapeDtypeStruct(d_resid.shape, F32),
            jax.ShapeDtypeStruct((8, width), F32),
        ],
        compiler_params=params(24),
        cost_estimate=SHORT,
        name="norm_one_back",
    )(small, embed, d_resid, *das)


def update_group(weight, grad, moment, average, grad_norm, weight_norm):
    effective = grad + WEIGHT_DECAY * weight
    moment_new = MOMENTUM_DECAY * moment + effective
    rate = TRUST_RATE * weight_norm / (grad_norm + WEIGHT_DECAY * weight_norm)
    weight_new = weight - rate * (effective + MOMENTUM_DECAY * moment_new)
    average_new = AVERAGE_DECAY * average + (1.0 - AVERAGE_DECAY) * weight_new
    return (weight_new, moment_new, average_new)


def update_all(state, sums, place, halves_q, halves_r, g_up, g_down, cuts):
    rows, width = state[1].shape
    part = width // 2
    pairs = part // 128
    n_sq = 9

    def kernel(place_ref, sums_ref, q_own, q_other, r_own, r_other, up_ref, down_ref, *refs):
        ins, outs = refs[:15], refs[15:30]
        norms_ref = refs[30]
        core, chip = place_ref[0], place_ref[1]
        small_rows = sums_ref[0:12, :]
        squares = [sums_ref[12:13, k : k + 1] for k in range(n_sq)]
        squares = squares[:4] + [jnp.sum(small_rows * small_rows).reshape(1, 1)] + squares[4:]
        norms = [jnp.sqrt(s) for s in squares]

        def write(group, weight_cols, grad):
            at = (slice(None), weight_cols)
            values = update_group(
                ins[group][at], grad, ins[5 + group][at], ins[10 + group][at],
                norms[group], norms[5 + group],
            )
            for k in range(3):
                outs[5 * k + group][at] = values[k]

        first = core == 0
        for c in range(2):
            pick = lambda own, other: jnp.where(first if c == 0 else ~first, own, other)
            for pair in range(pairs):
                for t in range(3):
                    if pair < 2:
                        cut = slice(384 * pair + 128 * t, 384 * pair + 128 * t + 128)
                        grad = pick(q_own[:, cut], q_other[:, cut])
                    else:
                        cut = slice(128 * t, 128 * t + 128)
                        grad = pick(r_own[:, cut], r_other[:, cut])
                    at = t * width + c * part + 128 * pair
                    write(0, slice(at, at + 128), grad)
            cut = slice(768, 768 + part)
            write(1, slice(c * part, c * part + part), pick(q_own[:, cut], q_other[:, cut]))
        write(2, slice(None), up_ref[...])
        write(3, slice(None), down_ref[...])

        @pl.when(pl.program_id(0) == 0)
        def _():
            lane = lax.broadcasted_iota(jnp.int32, (1, 128), 1)
            row = jnp.zeros((1, 128), F32)
            for k in range(10):
                row = jnp.where(lane == k, norms[k], row)
            norms_ref[...] = row
            shift = lax.rem(width - chip * rows, width)
            mine = pltpu.roll(sums_ref[...], shift, 1)[:, :128]
            grad = mine.T[:rows]
            at = lax.broadcasted_iota(jnp.int32, (rows, 1), 0)
            column = lax.broadcasted_iota(jnp.int32, (1, 16), 1)
            share = rows // 4
            for col in range(4):
                total = jnp.zeros((rows, 128), F32)
                for quarter in range(4):
                    source = (at - share * quarter) * 4 + col
                    inside = (at >= share * quarter) & (at < share * quarter + share)
                    here = inside & (lane == source)
                    total = jnp.where(here, mine[8 + quarter : 9 + quarter, :], total)
                value = jnp.sum(total, axis=1, keepdims=True)
                grad = jnp.where(column == 8 + col, value, grad)
            write(4, slice(None), grad.T[:12])

    tall = lambda x: pl.BlockSpec((x.shape[0] // cuts, x.shape[1]), lambda i: (i, 0))
    state_specs = [whole(x.shape) if k % 5 == 4 else tall(x) for k, x in enumerate(state)]
    return pl.pallas_call(
        kernel,
        grid=(cuts,),
        in_specs=[SMEM, whole(sums.shape)]
        + [tall(x) for x in (*halves_q, *halves_r, g_up, g_down)]
        + state_specs,
        out_specs=state_specs + [whole((1, 128))],
        out_shape=[jax.ShapeDtypeStruct(x.shape, F32) for x in state]
        + [jax.ShapeDtypeStruct((1, 128), F32)],
        compiler_params=params(48),
        cost_estimate=SHORT,
        name="update_all",
    )(place, sums, *halves_q, *halves_r, g_up, g_down, *state)


def weight_squares(state):
    def kernel(*refs):
        lane = lax.broadcasted_iota(jnp.int32, (1, 128), 1)
        row = jnp.zeros((1, 128), F32)
        for k, ref in enumerate(refs[:-1]):
            row = jnp.where(lane == k, 0.5 * jnp.sum(ref[...] * ref[...]), row)
        refs[-1][...] = row

    return pl.pallas_call(
        kernel,
        grid=(1,),
        in_specs=[whole(x.shape) for x in state],
        out_specs=whole((1, 128)),
        out_shape=jax.ShapeDtypeStruct((1, 128), F32),
        compiler_params=params(24),
        cost_estimate=SHORT,
        name="weight_squares",
    )(*state)


def interleave(own, other, place):
    rows, double = own[0].shape
    width = double // 2
    run = rows

    def kernel(place_ref, *refs):
        own_refs, other_refs = refs[:2], refs[2:4]
        up, down, squares = refs[4:]
        first = place_ref[0] == 0
        lane = lax.broadcasted_iota(jnp.int32, (1, 128), 1)
        total_up = sum(jnp.sum(r[:, :width] * r[:, :width]) for r in own_refs)
        total_down = sum(jnp.sum(r[:, width:] * r[:, width:]) for r in own_refs)
        squares[...] = jnp.where(lane == 0, total_up, jnp.where(lane == 1, total_down, 0.0))
        cells = []
        for c in range(2):
            for h in range(2):
                ahead = first if c == 0 else ~first
                cell = jnp.where(ahead, own_refs[h][...], other_refs[h][...])
                cells.append(cell[:, :width])
                at = (2 * c + h) * rows
                down[at : at + rows, :] = cell[:, width:]
        for tile in range(4 * width // 128):
            value = None
            low = 128 * tile
            for k in range(low // run, (low + 127) // run + 1):
                f, ch = k // 4, k % 4
                begin, place_at = f * run, k * run - low
                start = min(begin // 128 * 128, width - 256)
                window = cells[ch][:, start : start + 256]
                moved = pltpu.roll(window, (place_at - (begin - start)) % 256, 1)[:, :128]
                if value is None:
                    value = moved
                else:
                    value = jnp.where(lane >= place_at, moved, value)
            up[:, low : low + 128] = value

    return pl.pallas_call(
        kernel,
        grid=(1,),
        in_specs=[SMEM] + [whole(own[0].shape)] * 4,
        out_specs=[whole((rows, 4 * width)), whole((4 * rows, width)), whole((1, 128))],
        out_shape=[
            jax.ShapeDtypeStruct((rows, 4 * width), F32),
            jax.ShapeDtypeStruct((4 * rows, width), F32),
            jax.ShapeDtypeStruct((1, 128), F32),
        ],
        compiler_params=params(32),
        cost_estimate=SHORT,
        name="interleave",
    )(place, *own, *other)


def gather_sums(place, sums_one, sums_two, bias_grads, bias_ups, squares_mlp, squares_w):
    width = sums_one.shape[1]
    part = width // 2

    def kernel(place_ref, one, two, *refs):
        grads, ups = refs[: len(bias_grads)], refs[len(bias_grads) : len(bias_grads) + 2]
        sq_mlp, sq_w, out = refs[-3:]
        core = place_ref[0]
        out[...] = jnp.zeros_like(out)
        out[0:2, :] = one[0:2, :]
        out[2:4, :] = two[0:2, :]
        out[6:8, :] = two[2:4, :]
        for c in range(2):

            @pl.when(core == c)
            def _():
                for pair, ref in enumerate(grads):
                    at = c * part + 128 * pair
                    out[4:5, at : at + 128] = ref[:, 0:128]
                    out[5:6, at : at + 128] = ref[:, 256:384]
                for h in range(2):
                    out[8 + 2 * c + h : 9 + 2 * c + h, :] = ups[h][...]

        lane = lax.broadcasted_iota(jnp.int32, (1, 128), 1)
        row = jnp.where((lane == 2) | (lane == 3), pltpu.roll(sq_mlp[...], 2, 1), 0.0)
        moved = pltpu.roll(sq_w[...], 4, 1)
        out[12:13, :128] = jnp.where((lane >= 4) & (lane < 9), moved, row)

    ins = [sums_one, sums_two, *bias_grads, *bias_ups, squares_mlp, squares_w]
    return pl.pallas_call(
        kernel,
        grid=(1,),
        in_specs=[SMEM] + [whole(x.shape) for x in ins],
        out_specs=whole((16, width)),
        out_shape=jax.ShapeDtypeStruct((16, width), F32),
        compiler_params=params(16),
        cost_estimate=SHORT,
        name="gather_sums",
    )(place, *ins)


def last_shards(sums, keep_r, recv_r, shard_q):
    _, rows, columns = keep_r.shape
    wide = shard_q.shape[1]

    def kernel(sums_ref, keep, *refs):
        recvs, q, shard, out = refs[:-3], refs[-3], refs[-2], refs[-1]
        total = keep[0]
        for ref in recvs:
            total = total + ref[0].astype(F32)
        shard[...] = total
        out[...] = sums_ref[...]
        inner, outer = q[:, :768], q[:, 768:]
        square = jnp.sum(total * total) + jnp.sum(inner * inner)
        lane = lax.broadcasted_iota(jnp.int32, (1, 128), 1)
        old = sums_ref[12:13, :128]
        new = jnp.where(lane == 0, square, jnp.where(lane == 1, jnp.sum(outer * outer), old))
        out[12:13, :128] = new

    block = pl.BlockSpec((1, rows, columns), lambda i: (0, 0, 0))
    return pl.pallas_call(
        kernel,
        grid=(1,),
        in_specs=[whole(sums.shape), block] + [block] * len(recv_r) + [whole((rows, wide))],
        out_specs=[whole((rows, columns)), whole(sums.shape)],
        out_shape=[
            jax.ShapeDtypeStruct((rows, columns), F32),
            jax.ShapeDtypeStruct(sums.shape, F32),
        ],
        compiler_params=params(16),
        cost_estimate=SHORT,
        name="last_shards",
    )(sums, keep_r, *recv_r, shard_q)


def finish(masters, moments, averages, grads, totals):
    norms = jnp.sqrt(totals)
    results = [
        update_group(masters[i], grads[i], moments[i], averages[i], norms[i], norms[5 + i])
        for i in range(5)
    ]
    return (
        tuple(r[0] for r in results)
        + tuple(r[1] for r in results)
        + tuple(r[2] for r in results)
        + (norms,)
    )


def square_sum(x):
    return jnp.sum(x * x)


def tie(*arrays):
    return lax.optimization_barrier(arrays)


def paired_device(links, tokens, positions, counts, cotangent, *state):
    state = [x.T if k % 5 == 4 else x for k, x in enumerate(state)]
    w_qkv, w_out, w_up, w_down, w_small = state[:5]
    each, length, width = tokens.shape
    rows = w_qkv.shape[0]
    core = lax.axis_index("dp")
    chip = lax.axis_index("fsdp")
    table = jnp.asarray(links.masks())
    mine = lax.dynamic_index_in_dim(table, core, 0, False) ^ chip
    partner = lax.dynamic_index_in_dim(table, 1 - core, 0, False) ^ chip
    core_id = core[None].astype(jnp.int32)
    meta = jnp.concatenate([core_id, mine, partner])
    place = jnp.concatenate([core_id, chip[None].astype(jnp.int32)])
    part = width // 2
    pairs = part // 128
    cross, flip, along_z = links.cross, links.flip, links.along_z
    half_core = lambda x, axis: lax.dynamic_index_in_dim(x, core, axis, False)
    join = lambda *blocks: jnp.concatenate(blocks, axis=0)

    def onward(first, last, keep, *recvs):
        total = keep[first:last]
        for recv in recvs:
            total = total + recv[first:last].astype(F32)
        return total

    cut = half_core(w_qkv.reshape(rows, 3, 2, pairs, 128), 2).astype(BF)
    cut = jnp.swapaxes(cut, 1, 2).reshape(rows, pairs * 384)
    small_cut = jnp.concatenate([w_small[:8], w_small[8:].T.reshape(4, rows)], axis=0)
    small_cut = jnp.pad(small_cut.astype(BF).T, ((0, 0), (0, 116)))
    pack_one = jnp.concatenate([cut[:, :768], small_cut], axis=1)[None]
    pack_one, cut, positions, counts, tokens, w_out, w_up, w_down = tie(
        pack_one, cut, positions, counts, tokens, w_out, w_up, w_down
    )
    one_z = along_z([pack_one] * 3)
    token_other = cross(tokens)
    place_other = cross(jnp.concatenate([positions, counts[:, None]], axis=1))
    out_cut = half_core(w_out.reshape(rows, 2, part), 1).astype(BF)
    pack_two = jnp.concatenate([cut[:, 768:], out_cut], axis=1)[None]
    up_cut = half_core(w_up.reshape(rows, 16, 2, 2, rows), 2).astype(BF)
    down_cut = half_core(w_down.reshape(2, 2, rows, width), 0).astype(BF)
    pack_a, pack_b = [
        jnp.concatenate([up_cut[:, :, h].reshape(rows, 16 * rows), down_cut[h]], axis=1)[None]
        for h in range(2)
    ]
    *one_z, pack_two, pack_a, pack_b = tie(*one_z, pack_two, pack_a, pack_b)
    one_4 = join(pack_one, *one_z)

    column = lambda x: x.astype(F32)[..., None]
    one_4, pack_two, tokens = tie(one_4, pack_two, tokens)
    one_b = flip(one_4, 4)
    two_z = along_z([pack_two] * 3)
    embed = embed_rows([tokens], [column(positions)])
    one_b, *two_z, embed = tie(one_b, *two_z, embed)
    one_8, two_4 = join(one_4, one_b), join(pack_two, *two_z)

    one_8, two_4, pack_a, token_other, cotangent = tie(
        one_8, two_4, pack_a, token_other, cotangent
    )
    one_c = flip(one_8, 8)
    two_b = flip(two_4, 4)
    a_z = along_z([pack_a] * 3)
    cot_other = cross(cotangent)
    embed_other = embed_rows([token_other], [column(place_other[:, :length])])
    squares_w = weight_squares(state[:5])
    one_c, two_b, embed_other, squares_w = tie(one_c, two_b, embed_other, squares_w)
    counts_all = jnp.concatenate([counts, place_other[:, length]])
    two_8 = join(two_4, two_b)

    embed_other, two_8, pack_b = tie(embed_other, two_8, pack_b)
    qkv_one, embeds = [one_8, one_c], [embed, embed_other]
    two_c = flip(two_8, 8)
    b_z = along_z([pack_b] * 3)
    forward = lambda source, small, pieces, pair, at: attend_forward(
        source, small, mine, core_id, counts_all, pieces, rows, each, 2 * pair, 2, 6, at
    )
    small, attn_in, qkv_0, logs_0, mix_own_0, mix_send_0 = forward(embeds, None, qkv_one, 0, 0)
    two_c, mix_send_0, *a_z, attn_in = tie(two_c, mix_send_0, *a_z, attn_in)
    a_4 = join(pack_a, *a_z)
    qkv_two = [two_8, two_c]
    two_8o, two_co = two_8[:, :, part:], two_c[:, :, part:]

    a_4, attn_in_1, mix_send_0, two_8o, two_co = tie(a_4, attn_in, mix_send_0, two_8o, two_co)
    a_b = flip(a_4, 4)
    mix_recv_0 = cross(mix_send_0)
    out_c, out_d = cross(two_8o), cross(two_co)
    qkv_1, logs_1, mix_own_1, mix_send_1 = forward([attn_in_1], small, qkv_one, 1, 1)
    a_b, mix_send_1, *b_z = tie(a_b, mix_send_1, *b_z)
    a_8, b_4 = join(a_4, a_b), join(pack_b, *b_z)

    a_8, b_4, mix_send_1, attn_in_2 = tie(a_8, b_4, mix_send_1, attn_in)
    a_c = flip(a_8, 8)
    mix_recv_1 = cross(mix_send_1)
    qkv_2, logs_2, mix_own_2, mix_send_2 = forward([attn_in_2], small, qkv_two, 2, 0)
    mix_send_2, mix_recv_0, mix_recv_1, b_4 = tie(mix_send_2, mix_recv_0, mix_recv_1, b_4)

    mix_recv_2 = cross(mix_send_2)
    b_b = flip(b_4, 4)
    mixes = [mix_own_0, mix_own_1, mix_own_2, mix_recv_0, mix_recv_1, mix_recv_2]
    places = [(0, 0), (0, 128), (0, 256), (1, 0), (1, 128), (1, 256)]
    out_pieces = ([two_8, two_c], [out_c, out_d])
    resid, mlp_own = project_norm(mixes, places, embed, small, meta, *out_pieces, rows)
    mlp_own, a_c, b_b = tie(mlp_own, a_c, b_b)
    mlp_other = cross(mlp_own)
    b_8 = join(b_4, b_b)

    mlp_own, mlp_other, b_8 = tie(mlp_own, mlp_other, b_8)
    b_c = flip(b_8, 8)
    biases = [lax.dynamic_slice(small, (8 + 2 * core + h, 0), (1, width)) for h in range(2)]
    groups, cots = [mlp_own, mlp_other], [cotangent, cot_other]
    own_out_a, own_dm_a, sent_out_a, sent_dm_a, bias_up_a, keep_a, send_a = mlp_both(
        groups, cots, mine, counts_all, biases[0], [a_8, a_c], rows, True
    )
    mlp_own, mlp_other, send_a, b_c, sent_dm_a, sent_out_a = tie(
        mlp_own, mlp_other, send_a, b_c, sent_dm_a, sent_out_a
    )
    groups = [mlp_own, mlp_other]
    a_r3 = flip(send_a, 8)
    recv_dm_a, recv_out_a = cross(sent_dm_a), cross(sent_out_a)
    own_out_b, own_dm_b, sent_out_b, sent_dm_b, bias_up_b, keep_b, send_b = mlp_both(
        groups, cots, mine, counts_all, biases[1], [b_8, b_c], rows, True
    )
    sent_dm_b, sent_out_b, send_b, a_r3, recv_dm_a, recv_out_a = tie(
        sent_dm_b, sent_out_b, send_b, a_r3, recv_dm_a, recv_out_a
    )
    b_r3 = flip(send_b, 8)
    recv_dm_b = cross(sent_dm_b)
    send_a = onward(4, 8, keep_a, a_r3).astype(BF)
    recv_dm_b, send_a = tie(recv_dm_b, send_a)

    a_r2 = flip(send_a, 4)
    dms = [own_dm_a, own_dm_b, recv_dm_a, recv_dm_b]
    d_mix_own, d_mix_send, proj, d_resid, sums_two = norm_two_back(
        dms, resid, cotangent, small, meta, counts, *out_pieces, rows, part
    )
    d_mix_send, proj, sent_out_b = tie(d_mix_send, proj, sent_out_b)
    d_mix_recv = cross(d_mix_send)
    keep_o, send_o = out_weight_grad(mixes, places, proj, meta, rows)
    d_mix_recv, send_o, b_r3, a_r2 = tie(d_mix_recv, send_o, b_r3, a_r2)
    send_b = onward(4, 8, keep_b, b_r3).astype(BF)
    sends_a = [onward(k, k + 1, keep_a, a_r3, a_r2).astype(BF) for k in (1, 2, 3)]

    d_mix_recv, send_b, send_o, sent_out_b, *sends_a = tie(
        d_mix_recv, send_b, send_o, sent_out_b, *sends_a
    )
    b_r2 = flip(send_b, 4)
    a_rz = along_z(sends_a)
    recv_o = cross(send_o)
    recv_out_b = cross(sent_out_b)
    d_mixes = [d_mix_own, d_mix_recv]
    back = lambda qkv, logs, pair, ins: attend_back(
        [ins], qkv, logs, d_mixes, mine, counts_all, rows, True, 0, pair, 1
    )
    d_qkv_0, bias_grad_0, keep_0, send_0 = back(qkv_0, logs_0, 0, attn_in)
    send_0, b_r2, *a_rz, recv_o, recv_out_b = tie(send_0, b_r2, *a_rz, recv_o, recv_out_b)
    sends_b = [onward(k, k + 1, keep_b, b_r3, b_r2).astype(BF) for k in (1, 2, 3)]
    shard_a = onward(0, 1, keep_a, a_r3, a_r2, *a_rz)[0]

    send_0, shard_a, attn_in_1, *sends_b = tie(send_0, shard_a, attn_in, *sends_b)
    b_rz = along_z(sends_b)
    other_a = cross(shard_a)
    d_qkv_1, bias_grad_1, keep_1, send_1 = back(qkv_1, logs_1, 1, attn_in_1)
    send_1, *b_rz, other_a = tie(send_1, *b_rz, other_a)
    keep_q = jnp.concatenate([keep_0, keep_1, keep_o[:8] + recv_o[:8].astype(F32)], axis=2)
    send_o = keep_o[8:] + recv_o[8:].astype(F32)
    send_q = jnp.concatenate([send_0, send_1, send_o.astype(BF)], axis=2)
    shard_b = onward(0, 1, keep_b, b_r3, b_r2, *b_rz)[0]

    send_q, shard_b, attn_in_2 = tie(send_q, shard_b, attn_in)
    q_r3 = flip(send_q, 8)
    other_b = cross(shard_b)
    d_qkv_2, bias_grad_2, keep_r, send_r = back(qkv_2, logs_2, 2, attn_in_2)
    d_qkv_2, send_r, q_r3, other_b = tie(d_qkv_2, send_r, q_r3, other_b)
    send_q = onward(4, 8, keep_q, q_r3).astype(BF)

    d_qkv_2, send_r, send_q = tie(d_qkv_2, send_r, send_q)
    r_r3 = flip(send_r, 8)
    q_r2 = flip(send_q, 4)
    da_own, da_send = attn_in_grad(
        [d_qkv_0, d_qkv_1, d_qkv_2], mine, [(qkv_one, 768), (qkv_two, 384)], rows, each, width
    )
    da_send, r_r3, q_r2 = tie(da_send, r_r3, q_r2)
    send_r = onward(4, 8, keep_r, r_r3).astype(BF)
    sends_q = [onward(k, k + 1, keep_q, q_r3, q_r2).astype(BF) for k in (1, 2, 3)]

    da_send, send_r, *sends_q = tie(da_send, send_r, *sends_q)
    da_recv = cross(da_send)
    r_r2 = flip(send_r, 4)
    q_rz = along_z(sends_q)
    token_grad, sums_one = norm_one_back([da_own, da_recv], embed, d_resid, small)
    r_r2, sums_one = tie(r_r2, sums_one)
    sends_r = [onward(k, k + 1, keep_r, r_r3, r_r2).astype(BF) for k in (1, 2, 3)]

    resid, *sends_r = tie(resid, *sends_r)
    r_rz = along_z(sends_r)
    g_up, g_down, squares_mlp = interleave((shard_a, shard_b), (other_a, other_b), place)
    bias_grads = [bias_grad_0, bias_grad_1, bias_grad_2]
    sums = gather_sums(
        place, sums_one, sums_two, bias_grads, (bias_up_a, bias_up_b), squares_mlp, squares_w
    )
    block_rows = resid + small[7]
    for value in (own_out_a, own_out_b, recv_out_a, recv_out_b):
        block_rows = block_rows + value.astype(F32)
    block_out = block_rows.astype(BF)
    *q_rz, block_out, sums = tie(*q_rz, block_out, sums)
    shard_q = onward(0, 1, keep_q, q_r3, q_r2, *q_rz)[0]
    *r_rz, shard_q = tie(*r_rz, shard_q)
    other_q = cross(shard_q)
    shard_r, sums = last_shards(sums, keep_r, [r_r3, r_r2, *r_rz], shard_q)
    other_r = cross(shard_r)
    sums = links.sum_all(sums)
    results = update_all(
        state, sums, place, (shard_q, other_q), (shard_r, other_r), g_up, g_down, 3
    )
    outs = [x.T if k % 5 == 4 else x for k, x in enumerate(results[:15])]
    return (block_out, token_grad) + tuple(outs) + (results[15][0, :10],)


def plain_device(tokens, positions, counts, cotangent, *state):
    masters, moments, averages = state[:5], state[5:10], state[10:]
    each, length, width = tokens.shape
    heads = width // HEAD_DIM
    pairs = heads // 2
    full = [
        lax.all_gather(w.astype(BF), "fsdp", axis=0, tiled=True) for w in masters
    ]
    wq, wo, up, down, table = full
    wq = jnp.swapaxes(wq.reshape(width, 3, pairs, 128), 1, 2).reshape(1, width, 3 * width)
    table = table.astype(F32)
    vectors = jnp.concatenate([table[:, :8].T, jnp.zeros((8, width), F32)], axis=0)
    bias_up = table[:, 8:].reshape(1, -1)
    hidden = bias_up.shape[1]
    order = jnp.zeros((33,), jnp.int32)
    embed = embed_rows([tokens], [positions.astype(F32)[..., None]])
    attn_in, qkv, logs, mixed = attend_forward(
        [embed], vectors, order, order, counts, [wq], width, each, 0, heads, 0, 0
    )
    places = [(0, 0)]
    resid, mlp_in = project_norm([mixed], places, embed, vectors, order, [wo[None]], [], width)
    outs, dms, bias_ups, ups, downs = [], [], [], [], []
    parts = 4
    size = hidden // parts
    for h in range(parts):
        cols = slice(h * size, (h + 1) * size)
        out, dm, bias, g_up, g_down = mlp_both(
            [mlp_in],
            [cotangent],
            order,
            counts,
            bias_up[:, cols],
            [up[:, cols][None], down[cols][None]],
            width,
            False,
        )
        outs.append(out)
        dms.append(dm)
        bias_ups.append(bias)
        ups.append(g_up[0])
        downs.append(g_down[0])
    d_mix, proj, d_resid, sums_two = norm_two_back(
        dms, resid, cotangent, vectors, order, counts, [wo[None]], [], width, width
    )
    g_out = out_weight_grad([mixed], places, proj, order, width)[0][0]
    d_qkv, bias_grad, g_qkv = attend_back(
        [attn_in], qkv, logs, [d_mix], order, counts, width, False, 0, 0, pairs
    )
    natural = lambda g: jnp.swapaxes(g.reshape(-1, pairs, 3, 128), 1, 2).reshape(-1, 3 * width)
    g_qkv, bias_grad = natural(g_qkv), natural(bias_grad)
    da = attn_in_grad([d_qkv], order, [([wq], 3 * width)], width, each, width)[0]
    token_grad, sums_one = norm_one_back([da], embed, d_resid, vectors)
    block_rows = resid + vectors[7]
    for value in outs:
        block_rows = block_rows + value
    block_out = block_rows.astype(BF)
    columns = jnp.stack(
        [
            sums_one[0],
            sums_one[1],
            sums_two[0],
            sums_two[1],
            bias_grad[0, :width],
            bias_grad[0, 2 * width :],
            sums_two[2],
            sums_two[3],
        ],
        axis=1,
    )
    small = jnp.concatenate(
        [columns, jnp.concatenate(bias_ups, axis=1).reshape(width, -1)], axis=1
    )
    partial = (
        g_qkv,
        g_out,
        jnp.concatenate(ups, axis=1),
        jnp.concatenate(downs, axis=0),
        small,
    )
    grads = []
    for grad in partial:
        shard = lax.psum_scatter(grad, "fsdp", scatter_dimension=0, tiled=True)
        grads.append(lax.psum(shard, "dp"))
    squares = jnp.stack([square_sum(g) for g in grads] + [square_sum(w) for w in masters])
    totals = lax.psum(squares, "fsdp")
    return (block_out, token_grad) + finish(masters, moments, averages, tuple(grads), totals)


def solution(mesh):
    clips = P(("dp", "fsdp"), None, None)
    in_specs = (clips, P(("dp", "fsdp"), None), P(("dp", "fsdp")), clips) + (P("fsdp", None),) * 15
    out_specs = (clips, clips) + (P("fsdp", None),) * 15 + (P(),)
    links = Links(mesh.shape["dp"], mesh.shape["fsdp"])

    def on_device(*args):
        if links.paired:
            return paired_device(links, *args)
        return plain_device(*args)

    return jax.shard_map(
        on_device, mesh=mesh, in_specs=in_specs, out_specs=out_specs, check_vma=False
    )
```

```python
import math

import jax
import jax.numpy as jnp
import numpy as np
from jax import lax
from jax.experimental import pallas as pl
from jax.experimental.pallas import tpu as pltpu
from jax.sharding import PartitionSpec as P

HEAD_DIM = 64
EPS_NORM = 1e-06
MOMENTUM_DECAY = 0.9
WEIGHT_DECAY = 0.0001
TRUST_RATE = 0.2
AVERAGE_DECAY = 0.8
NEG = -1000000000.0
LEAST = 0

BF = jnp.bfloat16
F32 = jnp.float32
AXES = ("dp", "fsdp")
SHORT = pl.CostEstimate(flops=1, bytes_accessed=1, transcendentals=0)
def lasting(us):
    return pl.CostEstimate(flops=us * 10**9, bytes_accessed=us * 3 * 10**6, transcendentals=0)


ANY = pl.BlockSpec(memory_space=pl.ANY)
SMEM = pl.BlockSpec(memory_space=pltpu.SMEM)


def params(mib):
    return pltpu.CompilerParams(
        vmem_limit_bytes=max(mib, LEAST) * 1024 * 1024, dimension_semantics=("arbitrary",)
    )


def dot(a, b):
    return lax.dot_general(a, b, (((1,), (0,)), ((), ())), preferred_element_type=F32)


def dot_nt(a, b):
    return lax.dot_general(a, b, (((1,), (1,)), ((), ())), preferred_element_type=F32)


def dot_tn(a, b):
    return lax.dot_general(a, b, (((0,), (0,)), ((), ())), preferred_element_type=F32)


def whole(shape):
    zeros = (0,) * len(shape)
    return pl.BlockSpec(shape, lambda *i: zeros)


class Links:
    def __init__(self, dp, fsdp):
        self.paired = dp == 2 and fsdp == 16
        self.bits = ((4, 4), (8, 8), (1, 2), (2, 1))

    def masks(self):
        table = np.zeros((2, 16), np.int32)
        for core in range(2):
            for p in range(16):
                for bit in range(4):
                    if p >> bit & 1:
                        table[core, p] ^= self.bits[bit][core]
        return table

    def flip(self, x, p):
        table = self.masks()
        pairs = [(c * 16 + f, c * 16 + (f ^ int(table[c, p]))) for c in range(2) for f in range(16)]
        return lax.ppermute(x, AXES, pairs)

    def cross(self, x):
        pairs = [(c * 16 + f, (1 - c) * 16 + f) for c in range(2) for f in range(16)]
        return lax.ppermute(x, AXES, pairs)

    def along_z(self, blocks):
        return [self.flip(block, p) for p, block in zip((1, 2, 3), blocks)]

    def sum_all(self, x):
        x = x + self.cross(x)
        for step in (1, 4):
            one, two, three = [self.flip(x, step * p) for p in (1, 2, 3)]
            x = (x + one) + (two + three)
        return x


def assemble(pieces, order, rows, target, sems, at=0, columns=None):
    copies = []
    n = 0
    for piece in pieces:
        for j in range(piece.shape[0]):
            source = piece.at[j] if columns is None else piece.at[j, :, columns]
            start = pl.multiple_of(order(n) * rows, 16)
            copies.append(
                pltpu.make_async_copy(source, target.at[pl.ds(start, rows)], sems.at[at + n])
            )
            n += 1
    return copies


def deliver(source, order, rows, first, targets, sems, at=0, columns=None):
    copies = []
    n = first
    for target in targets:
        for j in range(target.shape[0]):
            start = pl.multiple_of(order(n) * rows, 16)
            place = target.at[j] if columns is None else target.at[j, :, columns]
            copies.append(
                pltpu.make_async_copy(source.at[pl.ds(start, rows)], place, sems.at[at + n - first])
            )
            n += 1
    return copies


def run_all(copies):
    for copy in copies:
        copy.start()
    for copy in copies:
        copy.wait()


def norm_parts(values):
    center = values - jnp.mean(values, axis=-1, keepdims=True)
    inv = lax.rsqrt(jnp.mean(center * center, axis=-1, keepdims=True) + EPS_NORM)
    return center * inv, inv


def norm_back(u, hat, inv):
    first = jnp.mean(u, axis=-1, keepdims=True)
    second = jnp.mean(u * hat, axis=-1, keepdims=True)
    return inv * (u - first - hat * second)


def embed_kernel(each, n_groups):
    def kernel(table, *refs):
        toks, poss = refs[:n_groups], refs[n_groups : 2 * n_groups]
        embed = refs[-1]
        step = pl.program_id(0)
        p = choose(poss, step, each)
        turns = p * table[0:1, :]
        turns = turns - jnp.round(turns)
        turns = turns + (p * table[1:2, :] + table[2:3, :])
        turns = turns - jnp.round(turns)
        fold = jnp.where(turns > 0.25, 0.5 - turns, jnp.where(turns < -0.25, -0.5 - turns, turns))
        x = fold * (2.0 * math.pi)
        x2 = x * x
        poly = -1.0 / 39916800.0
        for coef in (1.0 / 362880.0, -1.0 / 5040.0, 1.0 / 120.0, -1.0 / 6.0, 1.0):
            poly = poly * x2 + coef
        embed[0] = choose(toks, step, each).astype(F32) + x * poly

    return kernel


def embed_rows(tokens, positions):
    each, length, width = tokens[0].shape
    exact = 10000.0 ** (-2.0 * (np.arange(width) // 2) / width) / (2.0 * math.pi)
    scale = 2.0 ** (11 - np.floor(np.log2(exact)))
    high = np.round(exact * scale) / scale
    table = np.zeros((8, width), np.float32)
    table[0], table[1], table[2] = high, exact - high, 0.25 * (np.arange(width) % 2)
    specs, clips = pair_specs(tokens, (length, width))
    pos_specs, _ = pair_specs(positions, (length, 1))
    size = clips * length * width
    return pl.pallas_call(
        embed_kernel(each, len(tokens)),
        grid=(clips,),
        in_specs=[whole((8, width))] + specs + pos_specs,
        out_specs=pl.BlockSpec((1, length, width), lambda i: (i, 0, 0)),
        out_shape=jax.ShapeDtypeStruct((clips, length, width), F32),
        compiler_params=params(24),
        cost_estimate=lasting(4),
        name="embed_rows",
    )(jnp.asarray(table), *tokens, *positions)


def pair_specs(groups, block, column=0):
    specs, first = [], 0
    for array in groups:
        n = array.shape[0]

        def index(*at, first=first, n=n):
            return (jnp.clip(at[-1] - first, 0, n - 1), 0, column)

        specs.append(pl.BlockSpec((1,) + block, index))
        first += n
    return specs, first


def choose(refs, step, each):
    value = refs[0][0]
    for k in range(1, len(refs)):
        value = jnp.where(step >= k * each, refs[k][0], value)
    return value


def attend_forward(
    sources, small, order, core, counts, pieces, rows, each, first, heads, apart, block
):
    length, width = sources[0].shape[1:]
    source_each, n_sources = sources[0].shape[0], len(sources)
    source_specs, clips = pair_specs(sources, (length, width))
    part = heads * HEAD_DIM
    columns = 3 * part
    fresh = sources[0].dtype == F32
    gathered = small is None
    total_columns = columns + (128 if gathered else 0)
    split = clips > each
    n_pieces = len(pieces)
    blocks = sum(piece.shape[0] for piece in pieces)
    smalls = [] if gathered else [small]

    def kernel(order_ref, core_ref, count_ref, *refs):
        source_refs = refs[:n_sources]
        refs = list(refs[n_sources:])
        small_in = None if gathered else refs.pop(0)
        piece_refs = refs[:n_pieces]
        refs = refs[n_pieces:]
        vectors = refs.pop(0) if gathered else small_in
        normed = refs.pop(0) if fresh else None
        qkv, logs, mixes = refs[0], refs[1], refs[2 : 4 if split else 3]
        weight, bias, sems = refs[-3:]
        step = pl.program_id(0)

        @pl.when(step == 0)
        def _():
            cut = slice(columns * block, columns * block + columns)
            target = weight.at[:, :columns]
            copies = assemble(piece_refs, lambda n: order_ref[n], rows, target, sems, 0, cut)
            if gathered:
                last = piece_refs[0].shape[2]
                target = weight.at[:, columns:]
                cut = slice(last - 128, last)
                copies += assemble(
                    piece_refs, lambda n: order_ref[n], rows, target, sems, blocks, cut
                )
            run_all(copies)
            if gathered:
                vectors[...] = weight[:, columns:].astype(F32).T[:16]
            bias[...] = jnp.zeros_like(bias)
            for pair in range(heads // 2):
                head = first + core_ref[0] * apart + 2 * pair
                at = pl.ds(pl.multiple_of(head * HEAD_DIM, 128), 128)
                bias[0:1, 384 * pair : 384 * pair + 128] = vectors[4:5, at]
                bias[0:1, 384 * pair + 256 : 384 * pair + 384] = vectors[5:6, at]

        if fresh:
            hat, _ = norm_parts(choose(source_refs, step, source_each))
            x = (hat * vectors[0:1, :] + vectors[1:2, :]).astype(BF)
            normed[0] = x
        else:
            x = choose(source_refs, step, source_each)
        low = (dot(x, weight[:, :columns]) + bias[0:1, :]).astype(BF)
        qkv[0] = low
        valid = lax.broadcasted_iota(jnp.int32, (length, 1), 0) < count_ref[step]
        lane = lax.broadcasted_iota(jnp.int32, (1, 2 * HEAD_DIM), 1)
        outs, log_rows = [], []
        for pair in range(heads // 2):
            at = 384 * pair
            q = low[:, at : at + 128] * jnp.asarray(HEAD_DIM**-0.5, BF)
            k = low[:, at + 128 : at + 256]
            v = low[:, at + 256 : at + 384]
            mixed_heads = []
            for half in range(2):
                mine = (lane >= HEAD_DIM) if half else (lane < HEAD_DIM)
                s = dot_nt(jnp.where(mine, k, jnp.zeros_like(k)), q)
                s = jnp.where(valid, s, NEG)
                top = jnp.max(s, axis=0, keepdims=True)
                e = jnp.exp(s - top)
                total = jnp.sum(e, axis=0, keepdims=True)
                p = (e * (1.0 / total)).astype(BF)
                mixed_heads.append(dot_tn(p, v))
                log_rows.append(top + jnp.log(total))
            outs.append(jnp.where(lane < HEAD_DIM, mixed_heads[0], mixed_heads[1]))
        mixed = jnp.concatenate(outs, axis=1).astype(BF)
        logs[0] = jnp.concatenate(log_rows, axis=0)
        if split:

            @pl.when(step < each)
            def _():
                mixes[0][0] = mixed

            @pl.when(step >= each)
            def _():
                mixes[1][0] = mixed

        else:
            mixes[0][0] = mixed

    clip = lambda c: pl.BlockSpec((1, length, c), lambda i: (i, 0, 0))
    own = pl.BlockSpec((1, length, part), lambda i: (jnp.minimum(i, each - 1), 0, 0))
    other = pl.BlockSpec((1, length, part), lambda i: (jnp.clip(i - each, 0, each - 1), 0, 0))
    out_specs, out_shapes = [], []
    if gathered:
        out_specs.append(whole((16, width)))
        out_shapes.append(jax.ShapeDtypeStruct((16, width), F32))
    if fresh:
        out_specs.append(clip(width))
        out_shapes.append(jax.ShapeDtypeStruct((clips, length, width), BF))
    out_specs += [clip(columns), pl.BlockSpec((1, heads, length), lambda i: (i, 0, 0)), own]
    out_shapes += [
        jax.ShapeDtypeStruct((clips, length, columns), BF),
        jax.ShapeDtypeStruct((clips, heads, length), F32),
        jax.ShapeDtypeStruct((each, length, part), BF),
    ]
    if split:
        out_specs.append(other)
        out_shapes.append(jax.ShapeDtypeStruct((clips - each, length, part), BF))
    n_rows = clips * length
    return pl.pallas_call(
        kernel,
        grid=(clips,),
        in_specs=[SMEM, SMEM, SMEM]
        + source_specs
        + [whole((16, width))] * len(smalls)
        + [ANY] * n_pieces,
        out_specs=out_specs,
        out_shape=out_shapes,
        scratch_shapes=[
            pltpu.VMEM((width, total_columns), BF),
            pltpu.VMEM((8, columns), F32),
            pltpu.SemaphoreType.DMA((2 * blocks,)),
        ],
        compiler_params=params(48),
        cost_estimate=lasting(8),
        name="attend_forward",
    )(order, core, counts, *sources, *smalls, *pieces)


def out_weight_copies(own, other, meta, rows, weight, sems):
    cut = slice(own[0].shape[2] - weight.shape[2], None)
    if other is None:
        return assemble(own, lambda n: meta[1 + n], rows, weight.at[0], sems, 0, cut)
    core = meta[0]
    copies = assemble(own, lambda n: meta[1 + n], rows, weight.at[core], sems, 0, cut)
    return copies + assemble(other, lambda n: meta[17 + n], rows, weight.at[1 - core], sems, 16)


def project_norm(mixes, places, embed, small, meta, pieces, others, rows):
    n, length, width = mixes[0].shape[0], embed.shape[1], embed.shape[2]
    parts = [mix.shape[2] for mix in mixes]
    n_mix, n_p, n_o = len(mixes), len(pieces), len(others)
    halves = 2 if others else 1
    half_width = width // halves

    def kernel(meta_ref, small_ref, embed_ref, *refs):
        mix_refs = refs[:n_mix]
        own_refs = refs[n_mix : n_mix + n_p]
        other_refs = refs[n_mix + n_p : n_mix + n_p + n_o] or None
        resid, mlp_in, weight, sems = refs[n_mix + n_p + n_o :]

        @pl.when(pl.program_id(0) == 0)
        def _():
            run_all(out_weight_copies(own_refs, other_refs, meta_ref, rows, weight, sems))

        outs = []
        for half in range(halves):
            total = 0.0
            for k, mix in enumerate(mix_refs):
                flip, first = places[k]
                at = first
                if halves > 1:
                    at = pl.multiple_of((meta_ref[0] ^ flip) * half_width + first, 128)
                total = total + dot(mix[0], weight[half, pl.ds(at, parts[k]), :])
            outs.append(total)
        total = jnp.concatenate(outs, axis=1) if halves > 1 else outs[0]
        values = embed_ref[0] + total + small_ref[6:7, :]
        resid[0] = values
        hat, _ = norm_parts(values)
        mlp_in[0] = (hat * small_ref[2:3, :] + small_ref[3:4, :]).astype(BF)

    clip = pl.BlockSpec((1, length, width), lambda i: (i, 0, 0))
    mix_specs = [pl.BlockSpec((1, length, c), lambda i: (i, 0, 0)) for c in parts]
    size = n * length * width
    return pl.pallas_call(
        kernel,
        grid=(n,),
        in_specs=[SMEM, whole((16, width)), clip] + mix_specs + [ANY] * (n_p + n_o),
        out_specs=[clip, clip],
        out_shape=[
            jax.ShapeDtypeStruct((n, length, width), F32),
            jax.ShapeDtypeStruct((n, length, width), BF),
        ],
        scratch_shapes=[
            pltpu.VMEM((halves, width, half_width), BF),
            pltpu.SemaphoreType.DMA((32,)),
        ],
        compiler_params=params(24),
        cost_estimate=lasting(6),
        name="project_norm",
    )(meta, small, embed, *mixes, *pieces, *others)


def mlp_both(groups, cots, order, counts, bias, pieces, rows, relative):
    each, length, width = groups[0].shape
    hidden = bias.shape[1]
    n_groups, n_pieces = len(groups), len(pieces)
    n_blocks = sum(piece.shape[0] for piece in pieces)
    hidden_rows = hidden // n_blocks
    specs, clips = pair_specs(groups, (length, width))
    if relative:
        half = n_blocks // 2
        grad_shapes = [
            jax.ShapeDtypeStruct((half, rows, 2 * width), F32),
            jax.ShapeDtypeStruct((half, rows, 2 * width), BF),
        ]
    else:
        grad_shapes = [
            jax.ShapeDtypeStruct((1, width, hidden), F32),
            jax.ShapeDtypeStruct((1, hidden, width), F32),
        ]
    own_shape = (each, length, width)
    out_shapes = [jax.ShapeDtypeStruct(own_shape, F32)] * 2
    if n_groups > 1:
        out_shapes += [jax.ShapeDtypeStruct(own_shape, BF)] * 2
    out_shapes += [jax.ShapeDtypeStruct((1, hidden), F32)]

    def kernel(order_ref, count_ref, bias_ref, *refs):
        ins = refs[:n_groups]
        cot_refs = refs[n_groups : 2 * n_groups]
        piece_refs = refs[2 * n_groups : 2 * n_groups + n_pieces]
        outs = refs[2 * n_groups + n_pieces :]
        own_out, own_dm = outs[0], outs[1]
        sent = outs[2:4] if n_groups > 1 else None
        n_out = 4 if n_groups > 1 else 2
        bias_grad = outs[n_out]
        grad_a, grad_b = outs[n_out + 1 : n_out + 3]
        (up, down, g_up, g_down, low_up, low_down, sems) = outs[n_out + 3 :]
        i = pl.program_id(0)
        place = lambda n: order_ref[n]

        @pl.when(i == 0)
        def _():
            copies = assemble(piece_refs, place, rows, up, sems, 0, slice(0, hidden))
            if relative:
                copies += assemble(
                    piece_refs, place, hidden_rows, down, sems, n_blocks, slice(hidden, None)
                )
            else:
                copies = [
                    pltpu.make_async_copy(piece_refs[0].at[0], up, sems.at[0]),
                    pltpu.make_async_copy(piece_refs[1].at[0], down, sems.at[1]),
                ]
            run_all(copies)

        x = choose(ins, i, each)
        valid = lax.broadcasted_iota(jnp.int32, (length, 1), 0) < count_ref[i]
        cot = choose(cot_refs, i, each)
        dd = jnp.where(valid, cot, jnp.zeros_like(cot))
        pre = dot(x, up[...]) + bias_ref[...]
        cdf = 0.5 + 0.5 * lax.erf(pre * 0.7071067811865476)
        pdf = jnp.exp(pre * pre * -0.5) * 0.3989422804014327
        act = (pre * cdf).astype(BF)
        d_pre = (dot_nt(dd, down[...]) * (cdf + pre * pdf)).astype(BF)
        out = dot(act, down[...])
        dm = dot_nt(d_pre, up[...])
        up_part = dot(x.T, d_pre)
        down_part = dot(act.T, dd)
        bias_part = jnp.sum(d_pre.astype(F32), axis=0, keepdims=True)

        @pl.when(i < each)
        def _():
            own_out[0] = out
            own_dm[0] = dm

        if sent is not None:

            @pl.when(i >= each)
            def _():
                sent[0][0] = out.astype(BF)
                sent[1][0] = dm.astype(BF)

        @pl.when(i == 0)
        def _():
            g_up[...] = up_part
            g_down[...] = down_part
            bias_grad[...] = bias_part

        @pl.when((i > 0) & (i < clips - 1))
        def _():
            g_up[...] += up_part
            g_down[...] += down_part
            bias_grad[...] += bias_part

        @pl.when(i == clips - 1)
        def _():
            bias_grad[...] += bias_part
            if relative:
                total_up = g_up[...] + up_part
                g_up[...] = total_up
                low_up[...] = total_up.astype(BF)
                one, two = slice(0, width), slice(width, 2 * width)
                copies = deliver(g_up, place, rows, 0, [grad_a], sems, 0, one)
                copies += deliver(low_up, place, rows, half, [grad_b], sems, half, one)
                for copy in copies:
                    copy.start()
                total_down = g_down[...] + down_part
                g_down[...] = total_down
                low_down[...] = total_down.astype(BF)
                more = deliver(g_down, place, rows, 0, [grad_a], sems, 2 * half, two)
                more += deliver(low_down, place, rows, half, [grad_b], sems, 3 * half, two)
                for copy in more:
                    copy.start()
                for copy in copies + more:
                    copy.wait()
            else:
                g_up[...] += up_part
                g_down[...] += down_part
                copies = [
                    pltpu.make_async_copy(g_up, grad_a.at[0], sems.at[0]),
                    pltpu.make_async_copy(g_down, grad_b.at[0], sems.at[1]),
                ]
                run_all(copies)

    own_index = lambda i: (jnp.minimum(i, each - 1), 0, 0)
    sent_index = lambda i: (jnp.clip(i - each, 0, each - 1), 0, 0)
    out_specs = [pl.BlockSpec((1, length, width), own_index)] * 2
    if n_groups > 1:
        out_specs += [pl.BlockSpec((1, length, width), sent_index)] * 2
    out_specs += [whole((1, hidden)), ANY, ANY]
    low_shape = (width, hidden) if relative else (16, 128)
    low_shape_down = (hidden, width) if relative else (16, 128)
    n_rows = clips * length
    return pl.pallas_call(
        kernel,
        grid=(clips,),
        in_specs=[SMEM, SMEM, whole((1, hidden))] + specs + specs + [ANY] * n_pieces,
        out_specs=out_specs,
        out_shape=out_shapes + grad_shapes,
        scratch_shapes=[
            pltpu.VMEM((width, hidden), BF),
            pltpu.VMEM((hidden, width), BF),
            pltpu.VMEM((width, hidden), F32),
            pltpu.VMEM((hidden, width), F32),
            pltpu.VMEM(low_shape, BF),
            pltpu.VMEM(low_shape_down, BF),
            pltpu.SemaphoreType.DMA((max(2 * n_blocks, 2),)),
        ],
        compiler_params=params(56),
        cost_estimate=lasting(23),
        name="mlp_both",
    )(order, counts, bias, *groups, *cots, *pieces)


def norm_two_back(dms, resid, cot, small, meta, counts, pieces, others, rows, part):
    n, length, width = resid.shape
    n_dm, n_p, n_o = len(dms), len(pieces), len(others)
    halves = 2 if others else 1
    half_width = width // halves

    def kernel(meta_ref, count_ref, small_ref, resid_ref, cot_ref, *refs):
        dm_refs = refs[:n_dm]
        own_refs = refs[n_dm : n_dm + n_p]
        other_refs = refs[n_dm + n_p : n_dm + n_p + n_o] or None
        outs = refs[n_dm + n_p + n_o :]
        mixes = outs[: halves]
        proj, d_resid, sums, weight, sems = outs[halves:]
        step = pl.program_id(0)

        @pl.when(step == 0)
        def _():
            run_all(out_weight_copies(own_refs, other_refs, meta_ref, rows, weight, sems))

        valid = lax.broadcasted_iota(jnp.int32, (length, 1), 0) < count_ref[step]
        dy = jnp.where(valid, cot_ref[0].astype(F32), 0.0)
        dm = dm_refs[0][0].astype(F32)
        for ref in dm_refs[1:]:
            dm = dm + ref[0].astype(F32)
        hat, inv = norm_parts(resid_ref[0])
        total = dy + norm_back(dm * small_ref[2:3, :], hat, inv)
        d_resid[0] = total
        low = total.astype(BF)
        proj[0] = low
        row = lambda v: jnp.sum(v, axis=0, keepdims=True)
        parts = jnp.concatenate(
            [row(dm * hat), row(dm), row(low.astype(F32)), row(dy), jnp.zeros((4, width), F32)]
        )
        for k in range(halves):
            at = pl.multiple_of((meta_ref[0] ^ k) * part, 128) if halves > 1 else 0
            value = 0.0
            for half in range(halves):
                cut = low[:, half * half_width : (half + 1) * half_width]
                value = value + dot_nt(cut, weight[half, pl.ds(at, part), :])
            mixes[k][0] = value.astype(BF)

        @pl.when(step == 0)
        def _():
            sums[...] = parts

        @pl.when(step > 0)
        def _():
            sums[...] += parts

    clip = pl.BlockSpec((1, length, width), lambda i: (i, 0, 0))
    mix_spec = pl.BlockSpec((1, length, part), lambda i: (i, 0, 0))
    shape = resid.shape
    mix_shape = jax.ShapeDtypeStruct((n, length, part), BF)
    return pl.pallas_call(
        kernel,
        grid=(n,),
        in_specs=[SMEM, SMEM, whole((16, width)), clip, clip]
        + [clip] * n_dm
        + [ANY] * (n_p + n_o),
        out_specs=[mix_spec] * halves + [clip, clip, whole((8, width))],
        out_shape=[mix_shape] * halves
        + [
            jax.ShapeDtypeStruct(shape, BF),
            jax.ShapeDtypeStruct(shape, F32),
            jax.ShapeDtypeStruct((8, width), F32),
        ],
        scratch_shapes=[
            pltpu.VMEM((halves, width, half_width), BF),
            pltpu.SemaphoreType.DMA((32,)),
        ],
        compiler_params=params(32),
        cost_estimate=lasting(7),
        name="norm_two_back",
    )(meta, counts, small, resid, cot, *dms, *pieces, *others)


def out_weight_grad(mixes, places, proj, meta, rows):
    n, length, width = proj.shape
    parts = [mix.shape[2] for mix in mixes]
    n_mix = len(mixes)
    halves = 2 if any(flip for flip, _ in places) else 1
    half_width = width // halves
    blocks = width // rows

    def kernel(meta_ref, proj_ref, *refs):
        mix_refs = refs[:n_mix]
        if halves > 1:
            keep, send, total, low, sems = refs[n_mix:]
        else:
            keep, total, sems = refs[n_mix:]
        step = pl.program_id(0)

        @pl.when(step == 0)
        def _():
            total[...] = jnp.zeros_like(total)

        for k in range(n_mix):
            turned = mix_refs[k][0].T
            flip, at = places[k]
            if halves > 1:
                at = pl.multiple_of((meta_ref[0] ^ flip) * half_width + at, 128)
            for half in range(halves):
                cut = proj_ref[0, :, half * half_width : (half + 1) * half_width]
                total[half, pl.ds(at, parts[k]), :] += dot(turned, cut)

        @pl.when(step == n - 1)
        def _():
            if halves > 1:
                core = meta_ref[0]
                low[...] = total[1 - core].astype(BF)
                copies = deliver(
                    total.at[core], lambda n: meta_ref[1 + n], rows, 0, [keep], sems, 0
                )
                copies += deliver(low, lambda n: meta_ref[17 + n], rows, 0, [send], sems, blocks)
                run_all(copies)
            else:
                run_all([pltpu.make_async_copy(total, keep, sems.at[0])])

    clip = lambda c: pl.BlockSpec((1, length, c), lambda i: (i, 0, 0))
    if halves > 1:
        shapes = [
            jax.ShapeDtypeStruct((blocks, rows, half_width), F32),
            jax.ShapeDtypeStruct((blocks, rows, half_width), BF),
        ]
        scratch = [
            pltpu.VMEM((halves, width, half_width), F32),
            pltpu.VMEM((width, half_width), BF),
            pltpu.SemaphoreType.DMA((2 * blocks,)),
        ]
    else:
        shapes = [jax.ShapeDtypeStruct((1, width, width), F32)]
        scratch = [pltpu.VMEM((1, width, width), F32), pltpu.SemaphoreType.DMA((1,))]
    return pl.pallas_call(
        kernel,
        grid=(n,),
        in_specs=[SMEM, clip(width)] + [clip(c) for c in parts],
        out_specs=[ANY] * len(shapes),
        out_shape=shapes,
        scratch_shapes=scratch,
        compiler_params=params(24),
        cost_estimate=lasting(5),
        name="out_weight_grad",
    )(meta, proj, *mixes)


def attend_back(groups, qkv, logs, d_mixes, order, counts, rows, relative, first, at_pair, pairs):
    each, length, width = groups[0].shape
    clips = qkv.shape[0]
    columns, part = 384 * pairs, 128 * pairs
    all_heads = logs.shape[1]
    n_groups = len(groups)
    n_mix = len(d_mixes)
    specs, _ = pair_specs(groups, (length, width))
    mix_each = d_mixes[0].shape[0]
    mix_specs, _ = pair_specs(d_mixes, (length, part), at_pair // pairs)
    blocks = width // rows
    half_blocks = blocks // 2

    def kernel(order_ref, count_ref, qkv_ref, log_ref, *refs):
        ins = refs[:n_groups]
        mix_refs = refs[n_groups : n_groups + n_mix]
        refs = refs[n_groups + n_mix :]
        d_qkv, bias_grad = refs[:2]
        if relative:
            keep, send, total, low, sems = refs[2:]
        else:
            keep, total, sems = refs[2:]
        step = pl.program_id(0)
        valid = lax.broadcasted_iota(jnp.int32, (length, 1), 0) < count_ref[step]
        lane = lax.broadcasted_iota(jnp.int32, (1, 2 * HEAD_DIM), 1)
        d_mix = choose(mix_refs, step, mix_each)
        pieces = []
        scale = HEAD_DIM**-0.5
        for pair in range(pairs):
            at = 384 * pair
            q = qkv_ref[0, :, at : at + 128] * jnp.asarray(scale, BF)
            k = qkv_ref[0, :, at + 128 : at + 256]
            v = qkv_ref[0, :, at + 256 : at + 384]
            do = d_mix[:, 128 * pair : 128 * pair + 128]
            k_t = k.T
            dk = dv = None
            turned_q = []
            for half in range(2):
                mine = (lane >= HEAD_DIM) if half else (lane < HEAD_DIM)
                only = lambda x: jnp.where(mine, x, jnp.zeros_like(x))
                s = dot_nt(only(k), q)
                h = 2 * (first + pair) + half
                p = jnp.exp(jnp.where(valid, s, NEG) - log_ref[0, h : h + 1, :])
                dp = dot_nt(only(v), do)
                inner = jnp.sum(dp * p, axis=0, keepdims=True)
                ds = (p * (dp - inner)).astype(BF)
                dv_half = dot(p.astype(BF), only(do))
                dk_half = dot(ds, only(q))
                dv = dv_half if dv is None else dv + dv_half
                dk = dk_half if dk is None else dk + dk_half
                turned_q.append(dot(k_t[HEAD_DIM * half : HEAD_DIM * half + HEAD_DIM], ds))
            pieces += [(jnp.concatenate(turned_q, axis=0) * scale).T, dk, dv]
        low_rows = jnp.concatenate(pieces, axis=1).astype(BF)
        d_qkv[0] = low_rows
        bias_part = jnp.sum(low_rows.astype(F32), axis=0, keepdims=True)
        weight_part = dot(choose(ins, step, each).T, low_rows)

        @pl.when(step == 0)
        def _():
            total[...] = weight_part
            bias_grad[...] = bias_part

        @pl.when(step > 0)
        def _():
            total[...] += weight_part
            bias_grad[...] += bias_part

        @pl.when(step == clips - 1)
        def _():
            place = lambda n: order_ref[n]
            if relative:
                low[...] = total[...].astype(BF)
                copies = deliver(total, place, rows, 0, [keep], sems, 0)
                copies += deliver(low, place, rows, half_blocks, [send], sems, half_blocks)
                run_all(copies)
            else:
                run_all([pltpu.make_async_copy(total, keep.at[0], sems.at[0])])

    clip = lambda c: pl.BlockSpec((1, length, c), lambda i: (i, 0, 0))
    block_at = first // pairs
    qkv_spec = pl.BlockSpec((1, length, columns), lambda i: (i, 0, block_at))
    if relative:
        shapes = [
            jax.ShapeDtypeStruct((half_blocks, rows, columns), F32),
            jax.ShapeDtypeStruct((half_blocks, rows, columns), BF),
        ]
        scratch = [pltpu.VMEM((width, columns), F32), pltpu.VMEM((width, columns), BF)]
    else:
        shapes = [jax.ShapeDtypeStruct((1, width, columns), F32)]
        scratch = [pltpu.VMEM((width, columns), F32)]
    n_rows = clips * length
    return pl.pallas_call(
        kernel,
        grid=(clips,),
        in_specs=[
            SMEM,
            SMEM,
            qkv_spec,
            pl.BlockSpec((1, all_heads, length), lambda i: (i, 0, 0)),
        ]
        + specs
        + mix_specs,
        out_specs=[clip(columns), whole((1, columns))] + [ANY] * len(shapes),
        out_shape=[
            jax.ShapeDtypeStruct((clips, length, columns), BF),
            jax.ShapeDtypeStruct((1, columns), F32),
        ]
        + shapes,
        scratch_shapes=scratch + [pltpu.SemaphoreType.DMA((blocks,))],
        compiler_params=params(48),
        cost_estimate=lasting(12),
        name="attend_back",
    )(order, counts, qkv, logs, *groups, *d_mixes)


def attn_in_grad(d_qkvs, order, pieces, rows, each, width):
    clips, length, _ = d_qkvs[0].shape
    sizes = [d.shape[2] for d in d_qkvs]
    total = sum(sizes)
    n_d = len(d_qkvs)
    flat = [array for arrays, _ in pieces for array in arrays]
    blocks = sum(array.shape[0] for array in flat)
    split = clips > each

    def kernel(order_ref, *refs):
        row_refs = refs[:n_d]
        piece_refs = refs[n_d : n_d + len(flat)]
        outs = refs[n_d + len(flat) :]
        weight, sems = outs[-2:]
        step = pl.program_id(0)

        @pl.when(step == 0)
        def _():
            copies, used, column = [], 0, 0
            for arrays, size in pieces:
                refs_here = piece_refs[used : used + len(arrays)]
                target = weight.at[:, column : column + size]
                copies += assemble(
                    refs_here, lambda n: order_ref[n], rows, target, sems, len(copies), slice(0, size)
                )
                used += len(arrays)
                column += size
            run_all(copies)

        low = jnp.concatenate([ref[0] for ref in row_refs], axis=1) if n_d > 1 else row_refs[0][0]
        value = dot_nt(low, weight[...])
        if split:

            @pl.when(step < each)
            def _():
                outs[0][0] = value

            @pl.when(step >= each)
            def _():
                outs[1][0] = value.astype(BF)
        else:
            outs[0][0] = value

    own = pl.BlockSpec((1, length, width), lambda i: (jnp.minimum(i, each - 1), 0, 0))
    other = pl.BlockSpec((1, length, width), lambda i: (jnp.clip(i - each, 0, each - 1), 0, 0))
    shapes = [jax.ShapeDtypeStruct((each, length, width), F32)]
    if split:
        shapes.append(jax.ShapeDtypeStruct((each, length, width), BF))
    return pl.pallas_call(
        kernel,
        grid=(clips,),
        in_specs=[SMEM]
        + [pl.BlockSpec((1, length, c), lambda i: (i, 0, 0)) for c in sizes]
        + [ANY] * len(flat),
        out_specs=[own, other][: len(shapes)],
        out_shape=shapes,
        scratch_shapes=[pltpu.VMEM((width, total), BF), pltpu.SemaphoreType.DMA((blocks,))],
        compiler_params=params(32),
        cost_estimate=lasting(7),
        name="attn_in_grad",
    )(order, *d_qkvs, *flat)


def norm_one_back(das, embed, d_resid, small):
    n, length, width = d_resid.shape
    n_da = len(das)

    def kernel(small_ref, embed_ref, resid_ref, *refs):
        da_refs = refs[:n_da]
        grad, sums = refs[n_da:]
        step = pl.program_id(0)
        da = da_refs[0][0].astype(F32)
        for ref in da_refs[1:]:
            da = da + ref[0].astype(F32)
        hat, inv = norm_parts(embed_ref[0])
        grad[0] = resid_ref[0] + norm_back(da * small_ref[0:1, :], hat, inv)
        row = lambda v: jnp.sum(v, axis=0, keepdims=True)
        parts = jnp.concatenate([row(da * hat), row(da), jnp.zeros((6, width), F32)])

        @pl.when(step == 0)
        def _():
            sums[...] = parts

        @pl.when(step > 0)
        def _():
            sums[...] += parts

    clip = pl.BlockSpec((1, length, width), lambda i: (i, 0, 0))
    return pl.pallas_call(
        kernel,
        grid=(n,),
        in_specs=[whole((16, width)), clip, clip] + [clip] * n_da,
        out_specs=[clip, whole((8, width))],
        out_shape=[
            jax.ShapeDtypeStruct(d_resid.shape, F32),
            jax.ShapeDtypeStruct((8, width), F32),
        ],
        compiler_params=params(24),
        cost_estimate=lasting(4),
        name="norm_one_back",
    )(small, embed, d_resid, *das)


def update_group(weight, grad, moment, average, grad_norm, weight_norm):
    effective = grad + WEIGHT_DECAY * weight
    moment_new = MOMENTUM_DECAY * moment + effective
    rate = TRUST_RATE * weight_norm / (grad_norm + WEIGHT_DECAY * weight_norm)
    weight_new = weight - rate * (effective + MOMENTUM_DECAY * moment_new)
    average_new = AVERAGE_DECAY * average + (1.0 - AVERAGE_DECAY) * weight_new
    return (weight_new, moment_new, average_new)


def update_all(state, sums, place, halves_q, halves_r, g_up, g_down, cuts):
    rows, width = state[1].shape
    part = width // 2
    pairs = part // 128
    n_sq = 9

    def kernel(place_ref, sums_ref, q_own, q_other, r_own, r_other, up_ref, down_ref, *refs):
        ins, outs = refs[:15], refs[15:30]
        norms_ref = refs[30]
        core, chip = place_ref[0], place_ref[1]
        small_rows = sums_ref[0:12, :]
        squares = [sums_ref[12:13, k : k + 1] for k in range(n_sq)]
        squares = squares[:4] + [jnp.sum(small_rows * small_rows).reshape(1, 1)] + squares[4:]
        norms = [jnp.sqrt(s) for s in squares]

        def write(group, weight_cols, grad):
            at = (slice(None), weight_cols)
            values = update_group(
                ins[group][at], grad, ins[5 + group][at], ins[10 + group][at],
                norms[group], norms[5 + group],
            )
            for k in range(3):
                outs[5 * k + group][at] = values[k]

        first = core == 0
        for c in range(2):
            pick = lambda own, other: jnp.where(first if c == 0 else ~first, own, other)
            for pair in range(pairs):
                for t in range(3):
                    if pair < 2:
                        cut = slice(384 * pair + 128 * t, 384 * pair + 128 * t + 128)
                        grad = pick(q_own[:, cut], q_other[:, cut])
                    else:
                        cut = slice(128 * t, 128 * t + 128)
                        grad = pick(r_own[:, cut], r_other[:, cut])
                    at = t * width + c * part + 128 * pair
                    write(0, slice(at, at + 128), grad)
            cut = slice(768, 768 + part)
            write(1, slice(c * part, c * part + part), pick(q_own[:, cut], q_other[:, cut]))
        write(2, slice(None), up_ref[...])
        write(3, slice(None), down_ref[...])

        @pl.when(pl.program_id(0) == 0)
        def _():
            lane = lax.broadcasted_iota(jnp.int32, (1, 128), 1)
            row = jnp.zeros((1, 128), F32)
            for k in range(10):
                row = jnp.where(lane == k, norms[k], row)
            norms_ref[...] = row
            shift = lax.rem(width - chip * rows, width)
            mine = pltpu.roll(sums_ref[...], shift, 1)[:, :128]
            grad = mine.T[:rows]
            at = lax.broadcasted_iota(jnp.int32, (rows, 1), 0)
            column = lax.broadcasted_iota(jnp.int32, (1, 16), 1)
            share = rows // 4
            for col in range(4):
                total = jnp.zeros((rows, 128), F32)
                for quarter in range(4):
                    source = (at - share * quarter) * 4 + col
                    inside = (at >= share * quarter) & (at < share * quarter + share)
                    here = inside & (lane == source)
                    total = jnp.where(here, mine[8 + quarter : 9 + quarter, :], total)
                value = jnp.sum(total, axis=1, keepdims=True)
                grad = jnp.where(column == 8 + col, value, grad)
            write(4, slice(None), grad.T[:12])

    tall = lambda x: pl.BlockSpec((x.shape[0] // cuts, x.shape[1]), lambda i: (i, 0))
    state_specs = [whole(x.shape) if k % 5 == 4 else tall(x) for k, x in enumerate(state)]
    return pl.pallas_call(
        kernel,
        grid=(cuts,),
        in_specs=[SMEM, whole(sums.shape)]
        + [tall(x) for x in (*halves_q, *halves_r, g_up, g_down)]
        + state_specs,
        out_specs=state_specs + [whole((1, 128))],
        out_shape=[jax.ShapeDtypeStruct(x.shape, F32) for x in state]
        + [jax.ShapeDtypeStruct((1, 128), F32)],
        compiler_params=params(48),
        cost_estimate=lasting(6),
        name="update_all",
    )(place, sums, *halves_q, *halves_r, g_up, g_down, *state)


def weight_squares(state):
    def kernel(*refs):
        lane = lax.broadcasted_iota(jnp.int32, (1, 128), 1)
        row = jnp.zeros((1, 128), F32)
        for k, ref in enumerate(refs[:-1]):
            row = jnp.where(lane == k, 0.5 * jnp.sum(ref[...] * ref[...]), row)
        refs[-1][...] = row

    return pl.pallas_call(
        kernel,
        grid=(1,),
        in_specs=[whole(x.shape) for x in state],
        out_specs=whole((1, 128)),
        out_shape=jax.ShapeDtypeStruct((1, 128), F32),
        compiler_params=params(24),
        cost_estimate=lasting(2),
        name="weight_squares",
    )(*state)


def interleave(own, other, place):
    rows, double = own[0].shape
    width = double // 2
    run = rows

    def kernel(place_ref, *refs):
        own_refs, other_refs = refs[:2], refs[2:4]
        up, down, squares = refs[4:]
        first = place_ref[0] == 0
        lane = lax.broadcasted_iota(jnp.int32, (1, 128), 1)
        total_up = sum(jnp.sum(r[:, :width] * r[:, :width]) for r in own_refs)
        total_down = sum(jnp.sum(r[:, width:] * r[:, width:]) for r in own_refs)
        squares[...] = jnp.where(lane == 0, total_up, jnp.where(lane == 1, total_down, 0.0))
        cells = []
        for c in range(2):
            for h in range(2):
                ahead = first if c == 0 else ~first
                cell = jnp.where(ahead, own_refs[h][...], other_refs[h][...])
                cells.append(cell[:, :width])
                at = (2 * c + h) * rows
                down[at : at + rows, :] = cell[:, width:]
        for tile in range(4 * width // 128):
            value = None
            low = 128 * tile
            for k in range(low // run, (low + 127) // run + 1):
                f, ch = k // 4, k % 4
                begin, place_at = f * run, k * run - low
                start = min(begin // 128 * 128, width - 256)
                window = cells[ch][:, start : start + 256]
                moved = pltpu.roll(window, (place_at - (begin - start)) % 256, 1)[:, :128]
                if value is None:
                    value = moved
                else:
                    value = jnp.where(lane >= place_at, moved, value)
            up[:, low : low + 128] = value

    return pl.pallas_call(
        kernel,
        grid=(1,),
        in_specs=[SMEM] + [whole(own[0].shape)] * 4,
        out_specs=[whole((rows, 4 * width)), whole((4 * rows, width)), whole((1, 128))],
        out_shape=[
            jax.ShapeDtypeStruct((rows, 4 * width), F32),
            jax.ShapeDtypeStruct((4 * rows, width), F32),
            jax.ShapeDtypeStruct((1, 128), F32),
        ],
        compiler_params=params(32),
        cost_estimate=lasting(3),
        name="interleave",
    )(place, *own, *other)


def gather_sums(place, sums_one, sums_two, bias_grads, bias_ups, squares_mlp, squares_w):
    width = sums_one.shape[1]
    part = width // 2

    def kernel(place_ref, one, two, *refs):
        grads, ups = refs[: len(bias_grads)], refs[len(bias_grads) : len(bias_grads) + 2]
        sq_mlp, sq_w, out = refs[-3:]
        core = place_ref[0]
        out[...] = jnp.zeros_like(out)
        out[0:2, :] = one[0:2, :]
        out[2:4, :] = two[0:2, :]
        out[6:8, :] = two[2:4, :]
        for c in range(2):

            @pl.when(core == c)
            def _():
                for pair, ref in enumerate(grads):
                    at = c * part + 128 * pair
                    out[4:5, at : at + 128] = ref[:, 0:128]
                    out[5:6, at : at + 128] = ref[:, 256:384]
                for h in range(2):
                    out[8 + 2 * c + h : 9 + 2 * c + h, :] = ups[h][...]

        lane = lax.broadcasted_iota(jnp.int32, (1, 128), 1)
        row = jnp.where((lane == 2) | (lane == 3), pltpu.roll(sq_mlp[...], 2, 1), 0.0)
        moved = pltpu.roll(sq_w[...], 4, 1)
        out[12:13, :128] = jnp.where((lane >= 4) & (lane < 9), moved, row)

    ins = [sums_one, sums_two, *bias_grads, *bias_ups, squares_mlp, squares_w]
    return pl.pallas_call(
        kernel,
        grid=(1,),
        in_specs=[SMEM] + [whole(x.shape) for x in ins],
        out_specs=whole((16, width)),
        out_shape=jax.ShapeDtypeStruct((16, width), F32),
        compiler_params=params(16),
        cost_estimate=lasting(1),
        name="gather_sums",
    )(place, *ins)


def last_shards(sums, keep_r, recv_r, shard_q):
    _, rows, columns = keep_r.shape
    wide = shard_q.shape[1]

    def kernel(sums_ref, keep, *refs):
        recvs, q, shard, out = refs[:-3], refs[-3], refs[-2], refs[-1]
        total = keep[0]
        for ref in recvs:
            total = total + ref[0].astype(F32)
        shard[...] = total
        out[...] = sums_ref[...]
        inner, outer = q[:, :768], q[:, 768:]
        square = jnp.sum(total * total) + jnp.sum(inner * inner)
        lane = lax.broadcasted_iota(jnp.int32, (1, 128), 1)
        old = sums_ref[12:13, :128]
        new = jnp.where(lane == 0, square, jnp.where(lane == 1, jnp.sum(outer * outer), old))
        out[12:13, :128] = new

    block = pl.BlockSpec((1, rows, columns), lambda i: (0, 0, 0))
    return pl.pallas_call(
        kernel,
        grid=(1,),
        in_specs=[whole(sums.shape), block] + [block] * len(recv_r) + [whole((rows, wide))],
        out_specs=[whole((rows, columns)), whole(sums.shape)],
        out_shape=[
            jax.ShapeDtypeStruct((rows, columns), F32),
            jax.ShapeDtypeStruct(sums.shape, F32),
        ],
        compiler_params=params(16),
        cost_estimate=lasting(2),
        name="last_shards",
    )(sums, keep_r, *recv_r, shard_q)


def finish(masters, moments, averages, grads, totals):
    norms = jnp.sqrt(totals)
    results = [
        update_group(masters[i], grads[i], moments[i], averages[i], norms[i], norms[5 + i])
        for i in range(5)
    ]
    return (
        tuple(r[0] for r in results)
        + tuple(r[1] for r in results)
        + tuple(r[2] for r in results)
        + (norms,)
    )


def square_sum(x):
    return jnp.sum(x * x)


def tie(*arrays):
    return lax.optimization_barrier(arrays)


def paired_device(links, tokens, positions, counts, cotangent, *state):
    state = [x.T if k % 5 == 4 else x for k, x in enumerate(state)]
    w_qkv, w_out, w_up, w_down, w_small = state[:5]
    each, length, width = tokens.shape
    rows = w_qkv.shape[0]
    core = lax.axis_index("dp")
    chip = lax.axis_index("fsdp")
    table = jnp.asarray(links.masks())
    mine = lax.dynamic_index_in_dim(table, core, 0, False) ^ chip
    partner = lax.dynamic_index_in_dim(table, 1 - core, 0, False) ^ chip
    core_id = core[None].astype(jnp.int32)
    meta = jnp.concatenate([core_id, mine, partner])
    place = jnp.concatenate([core_id, chip[None].astype(jnp.int32)])
    part = width // 2
    pairs = part // 128
    cross, flip, along_z = links.cross, links.flip, links.along_z
    half_core = lambda x, axis: lax.dynamic_index_in_dim(x, core, axis, False)
    join = lambda *blocks: jnp.concatenate(blocks, axis=0)

    def onward(first, last, keep, *recvs):
        total = keep[first:last]
        for recv in recvs:
            total = total + recv[first:last].astype(F32)
        return total

    cut = half_core(w_qkv.reshape(rows, 3, 2, pairs, 128), 2).astype(BF)
    cut = jnp.swapaxes(cut, 1, 2).reshape(rows, pairs * 384)
    small_cut = jnp.concatenate([w_small[:8], w_small[8:].T.reshape(4, rows)], axis=0)
    small_cut = jnp.pad(small_cut.astype(BF).T, ((0, 0), (0, 116)))
    pack_one = jnp.concatenate([cut[:, :768], small_cut], axis=1)[None]
    pack_one, cut, positions, counts, tokens, w_out, w_up, w_down = tie(
        pack_one, cut, positions, counts, tokens, w_out, w_up, w_down
    )
    one_z = along_z([pack_one] * 3)
    token_other = cross(tokens)
    place_other = cross(jnp.concatenate([positions, counts[:, None]], axis=1))
    out_cut = half_core(w_out.reshape(rows, 2, part), 1).astype(BF)
    pack_two = jnp.concatenate([cut[:, 768:], out_cut], axis=1)[None]
    up_cut = half_core(w_up.reshape(rows, 16, 2, 2, rows), 2).astype(BF)
    down_cut = half_core(w_down.reshape(2, 2, rows, width), 0).astype(BF)
    pack_a, pack_b = [
        jnp.concatenate([up_cut[:, :, h].reshape(rows, 16 * rows), down_cut[h]], axis=1)[None]
        for h in range(2)
    ]
    *one_z, pack_two, pack_a, pack_b = tie(*one_z, pack_two, pack_a, pack_b)
    one_4 = join(pack_one, *one_z)

    column = lambda x: x.astype(F32)[..., None]
    one_4, pack_two, tokens = tie(one_4, pack_two, tokens)
    one_b = flip(one_4, 4)
    two_z = along_z([pack_two] * 3)
    embed = embed_rows([tokens], [column(positions)])
    one_b, *two_z, embed = tie(one_b, *two_z, embed)
    one_8, two_4 = join(one_4, one_b), join(pack_two, *two_z)

    one_8, two_4, pack_a, token_other, cotangent = tie(
        one_8, two_4, pack_a, token_other, cotangent
    )
    one_c = flip(one_8, 8)
    two_b = flip(two_4, 4)
    a_z = along_z([pack_a] * 3)
    cot_other = cross(cotangent)
    embed_other = embed_rows([token_other], [column(place_other[:, :length])])
    squares_w = weight_squares(state[:5])
    one_c, two_b, embed_other, squares_w = tie(one_c, two_b, embed_other, squares_w)
    counts_all = jnp.concatenate([counts, place_other[:, length]])
    two_8 = join(two_4, two_b)

    embed_other, two_8, pack_b = tie(embed_other, two_8, pack_b)
    qkv_one, embeds = [one_8, one_c], [embed, embed_other]
    two_c = flip(two_8, 8)
    b_z = along_z([pack_b] * 3)
    forward = lambda source, small, pieces, pair, at: attend_forward(
        source, small, mine, core_id, counts_all, pieces, rows, each, 2 * pair, 2, 6, at
    )
    small, attn_in, qkv_0, logs_0, mix_own_0, mix_send_0 = forward(embeds, None, qkv_one, 0, 0)
    two_c, mix_send_0, *a_z, attn_in = tie(two_c, mix_send_0, *a_z, attn_in)
    a_4 = join(pack_a, *a_z)
    qkv_two = [two_8, two_c]
    two_8o, two_co = two_8[:, :, part:], two_c[:, :, part:]

    a_4, attn_in_1, mix_send_0, two_8o, two_co = tie(a_4, attn_in, mix_send_0, two_8o, two_co)
    a_b = flip(a_4, 4)
    mix_recv_0 = cross(mix_send_0)
    out_c, out_d = cross(two_8o), cross(two_co)
    qkv_1, logs_1, mix_own_1, mix_send_1 = forward([attn_in_1], small, qkv_one, 1, 1)
    a_b, mix_send_1, *b_z = tie(a_b, mix_send_1, *b_z)
    a_8, b_4 = join(a_4, a_b), join(pack_b, *b_z)

    a_8, b_4, mix_send_1, attn_in_2 = tie(a_8, b_4, mix_send_1, attn_in)
    a_c = flip(a_8, 8)
    mix_recv_1 = cross(mix_send_1)
    qkv_2, logs_2, mix_own_2, mix_send_2 = forward([attn_in_2], small, qkv_two, 2, 0)
    mix_send_2, mix_recv_0, mix_recv_1, b_4 = tie(mix_send_2, mix_recv_0, mix_recv_1, b_4)

    mix_recv_2 = cross(mix_send_2)
    b_b = flip(b_4, 4)
    mixes = [mix_own_0, mix_own_1, mix_own_2, mix_recv_0, mix_recv_1, mix_recv_2]
    places = [(0, 0), (0, 128), (0, 256), (1, 0), (1, 128), (1, 256)]
    out_pieces = ([two_8, two_c], [out_c, out_d])
    resid, mlp_own = project_norm(mixes, places, embed, small, meta, *out_pieces, rows)
    mlp_own, a_c, b_b = tie(mlp_own, a_c, b_b)
    mlp_other = cross(mlp_own)
    b_8 = join(b_4, b_b)

    mlp_own, mlp_other, b_8 = tie(mlp_own, mlp_other, b_8)
    b_c = flip(b_8, 8)
    biases = [lax.dynamic_slice(small, (8 + 2 * core + h, 0), (1, width)) for h in range(2)]
    groups, cots = [mlp_own, mlp_other], [cotangent, cot_other]
    own_out_a, own_dm_a, sent_out_a, sent_dm_a, bias_up_a, keep_a, send_a = mlp_both(
        groups, cots, mine, counts_all, biases[0], [a_8, a_c], rows, True
    )
    mlp_own, mlp_other, send_a, b_c, sent_dm_a, sent_out_a = tie(
        mlp_own, mlp_other, send_a, b_c, sent_dm_a, sent_out_a
    )
    groups = [mlp_own, mlp_other]
    a_r3 = flip(send_a, 8)
    recv_dm_a, recv_out_a = cross(sent_dm_a), cross(sent_out_a)
    own_out_b, own_dm_b, sent_out_b, sent_dm_b, bias_up_b, keep_b, send_b = mlp_both(
        groups, cots, mine, counts_all, biases[1], [b_8, b_c], rows, True
    )
    sent_dm_b, sent_out_b, send_b, a_r3, recv_dm_a, recv_out_a = tie(
        sent_dm_b, sent_out_b, send_b, a_r3, recv_dm_a, recv_out_a
    )
    b_r3 = flip(send_b, 8)
    recv_dm_b = cross(sent_dm_b)
    send_a = onward(4, 8, keep_a, a_r3).astype(BF)
    recv_dm_b, send_a = tie(recv_dm_b, send_a)

    a_r2 = flip(send_a, 4)
    dms = [own_dm_a, own_dm_b, recv_dm_a, recv_dm_b]
    d_mix_own, d_mix_send, proj, d_resid, sums_two = norm_two_back(
        dms, resid, cotangent, small, meta, counts, *out_pieces, rows, part
    )
    d_mix_send, proj, sent_out_b = tie(d_mix_send, proj, sent_out_b)
    d_mix_recv = cross(d_mix_send)
    keep_o, send_o = out_weight_grad(mixes, places, proj, meta, rows)
    d_mix_recv, send_o, b_r3, a_r2 = tie(d_mix_recv, send_o, b_r3, a_r2)
    send_b = onward(4, 8, keep_b, b_r3).astype(BF)
    sends_a = [onward(k, k + 1, keep_a, a_r3, a_r2).astype(BF) for k in (1, 2, 3)]

    d_mix_recv, send_b, send_o, sent_out_b, *sends_a = tie(
        d_mix_recv, send_b, send_o, sent_out_b, *sends_a
    )
    b_r2 = flip(send_b, 4)
    a_rz = along_z(sends_a)
    recv_o = cross(send_o)
    recv_out_b = cross(sent_out_b)
    d_mixes = [d_mix_own, d_mix_recv]
    back = lambda qkv, logs, pair, ins: attend_back(
        [ins], qkv, logs, d_mixes, mine, counts_all, rows, True, 0, pair, 1
    )
    d_qkv_0, bias_grad_0, keep_0, send_0 = back(qkv_0, logs_0, 0, attn_in)
    send_0, b_r2, *a_rz, recv_o, recv_out_b = tie(send_0, b_r2, *a_rz, recv_o, recv_out_b)
    sends_b = [onward(k, k + 1, keep_b, b_r3, b_r2).astype(BF) for k in (1, 2, 3)]
    shard_a = onward(0, 1, keep_a, a_r3, a_r2, *a_rz)[0]

    send_0, shard_a, attn_in_1, *sends_b = tie(send_0, shard_a, attn_in, *sends_b)
    b_rz = along_z(sends_b)
    other_a = cross(shard_a)
    d_qkv_1, bias_grad_1, keep_1, send_1 = back(qkv_1, logs_1, 1, attn_in_1)
    send_1, *b_rz, other_a = tie(send_1, *b_rz, other_a)
    keep_q = jnp.concatenate([keep_0, keep_1, keep_o[:8] + recv_o[:8].astype(F32)], axis=2)
    send_o = keep_o[8:] + recv_o[8:].astype(F32)
    send_q = jnp.concatenate([send_0, send_1, send_o.astype(BF)], axis=2)
    shard_b = onward(0, 1, keep_b, b_r3, b_r2, *b_rz)[0]

    send_q, shard_b, attn_in_2 = tie(send_q, shard_b, attn_in)
    q_r3 = flip(send_q, 8)
    other_b = cross(shard_b)
    d_qkv_2, bias_grad_2, keep_r, send_r = back(qkv_2, logs_2, 2, attn_in_2)
    d_qkv_2, send_r, q_r3, other_b = tie(d_qkv_2, send_r, q_r3, other_b)
    send_q = onward(4, 8, keep_q, q_r3).astype(BF)

    d_qkv_2, send_r, send_q = tie(d_qkv_2, send_r, send_q)
    r_r3 = flip(send_r, 8)
    q_r2 = flip(send_q, 4)
    da_own, da_send = attn_in_grad(
        [d_qkv_0, d_qkv_1, d_qkv_2], mine, [(qkv_one, 768), (qkv_two, 384)], rows, each, width
    )
    da_send, r_r3, q_r2 = tie(da_send, r_r3, q_r2)
    send_r = onward(4, 8, keep_r, r_r3).astype(BF)
    sends_q = [onward(k, k + 1, keep_q, q_r3, q_r2).astype(BF) for k in (1, 2, 3)]

    da_send, send_r, *sends_q = tie(da_send, send_r, *sends_q)
    da_recv = cross(da_send)
    r_r2 = flip(send_r, 4)
    q_rz = along_z(sends_q)
    token_grad, sums_one = norm_one_back([da_own, da_recv], embed, d_resid, small)
    r_r2, sums_one = tie(r_r2, sums_one)
    sends_r = [onward(k, k + 1, keep_r, r_r3, r_r2).astype(BF) for k in (1, 2, 3)]

    resid, *sends_r = tie(resid, *sends_r)
    r_rz = along_z(sends_r)
    g_up, g_down, squares_mlp = interleave((shard_a, shard_b), (other_a, other_b), place)
    bias_grads = [bias_grad_0, bias_grad_1, bias_grad_2]
    sums = gather_sums(
        place, sums_one, sums_two, bias_grads, (bias_up_a, bias_up_b), squares_mlp, squares_w
    )
    block_rows = resid + small[7]
    for value in (own_out_a, own_out_b, recv_out_a, recv_out_b):
        block_rows = block_rows + value.astype(F32)
    block_out = block_rows.astype(BF)
    *q_rz, block_out, sums = tie(*q_rz, block_out, sums)
    shard_q = onward(0, 1, keep_q, q_r3, q_r2, *q_rz)[0]
    *r_rz, shard_q = tie(*r_rz, shard_q)
    other_q = cross(shard_q)
    shard_r, sums = last_shards(sums, keep_r, [r_r3, r_r2, *r_rz], shard_q)
    other_r = cross(shard_r)
    sums = links.sum_all(sums)
    results = update_all(
        state, sums, place, (shard_q, other_q), (shard_r, other_r), g_up, g_down, 3
    )
    outs = [x.T if k % 5 == 4 else x for k, x in enumerate(results[:15])]
    return (block_out, token_grad) + tuple(outs) + (results[15][0, :10],)


def plain_device(tokens, positions, counts, cotangent, *state):
    masters, moments, averages = state[:5], state[5:10], state[10:]
    each, length, width = tokens.shape
    heads = width // HEAD_DIM
    pairs = heads // 2
    full = [
        lax.all_gather(w.astype(BF), "fsdp", axis=0, tiled=True) for w in masters
    ]
    wq, wo, up, down, table = full
    wq = jnp.swapaxes(wq.reshape(width, 3, pairs, 128), 1, 2).reshape(1, width, 3 * width)
    table = table.astype(F32)
    vectors = jnp.concatenate([table[:, :8].T, jnp.zeros((8, width), F32)], axis=0)
    bias_up = table[:, 8:].reshape(1, -1)
    hidden = bias_up.shape[1]
    order = jnp.zeros((33,), jnp.int32)
    embed = embed_rows([tokens], [positions.astype(F32)[..., None]])
    attn_in, qkv, logs, mixed = attend_forward(
        [embed], vectors, order, order, counts, [wq], width, each, 0, heads, 0, 0
    )
    places = [(0, 0)]
    resid, mlp_in = project_norm([mixed], places, embed, vectors, order, [wo[None]], [], width)
    outs, dms, bias_ups, ups, downs = [], [], [], [], []
    parts = 4
    size = hidden // parts
    for h in range(parts):
        cols = slice(h * size, (h + 1) * size)
        out, dm, bias, g_up, g_down = mlp_both(
            [mlp_in],
            [cotangent],
            order,
            counts,
            bias_up[:, cols],
            [up[:, cols][None], down[cols][None]],
            width,
            False,
        )
        outs.append(out)
        dms.append(dm)
        bias_ups.append(bias)
        ups.append(g_up[0])
        downs.append(g_down[0])
    d_mix, proj, d_resid, sums_two = norm_two_back(
        dms, resid, cotangent, vectors, order, counts, [wo[None]], [], width, width
    )
    g_out = out_weight_grad([mixed], places, proj, order, width)[0][0]
    d_qkv, bias_grad, g_qkv = attend_back(
        [attn_in], qkv, logs, [d_mix], order, counts, width, False, 0, 0, pairs
    )
    natural = lambda g: jnp.swapaxes(g.reshape(-1, pairs, 3, 128), 1, 2).reshape(-1, 3 * width)
    g_qkv, bias_grad = natural(g_qkv), natural(bias_grad)
    da = attn_in_grad([d_qkv], order, [([wq], 3 * width)], width, each, width)[0]
    token_grad, sums_one = norm_one_back([da], embed, d_resid, vectors)
    block_rows = resid + vectors[7]
    for value in outs:
        block_rows = block_rows + value
    block_out = block_rows.astype(BF)
    columns = jnp.stack(
        [
            sums_one[0],
            sums_one[1],
            sums_two[0],
            sums_two[1],
            bias_grad[0, :width],
            bias_grad[0, 2 * width :],
            sums_two[2],
            sums_two[3],
        ],
        axis=1,
    )
    small = jnp.concatenate(
        [columns, jnp.concatenate(bias_ups, axis=1).reshape(width, -1)], axis=1
    )
    partial = (
        g_qkv,
        g_out,
        jnp.concatenate(ups, axis=1),
        jnp.concatenate(downs, axis=0),
        small,
    )
    grads = []
    for grad in partial:
        shard = lax.psum_scatter(grad, "fsdp", scatter_dimension=0, tiled=True)
        grads.append(lax.psum(shard, "dp"))
    squares = jnp.stack([square_sum(g) for g in grads] + [square_sum(w) for w in masters])
    totals = lax.psum(squares, "fsdp")
    return (block_out, token_grad) + finish(masters, moments, averages, tuple(grads), totals)


def solution(mesh):
    clips = P(("dp", "fsdp"), None, None)
    in_specs = (clips, P(("dp", "fsdp"), None), P(("dp", "fsdp")), clips) + (P("fsdp", None),) * 15
    out_specs = (clips, clips) + (P("fsdp", None),) * 15 + (P(),)
    links = Links(mesh.shape["dp"], mesh.shape["fsdp"])

    def on_device(*args):
        if links.paired:
            return paired_device(links, *args)
        return plain_device(*args)

    return jax.shard_map(
        on_device, mesh=mesh, in_specs=in_specs, out_specs=out_specs, check_vma=False
    )
```

```python
import math

import jax
import jax.numpy as jnp
import numpy as np
from jax import lax
from jax.experimental import pallas as pl
from jax.experimental.pallas import tpu as pltpu
from jax.sharding import PartitionSpec as P

HEAD_DIM = 64
EPS_NORM = 1e-06
MOMENTUM_DECAY = 0.9
WEIGHT_DECAY = 0.0001
TRUST_RATE = 0.2
AVERAGE_DECAY = 0.8
NEG = -1000000000.0
LEAST = 0

BF = jnp.bfloat16
F32 = jnp.float32
AXES = ("dp", "fsdp")
SHORT = pl.CostEstimate(flops=1, bytes_accessed=1, transcendentals=0)
def lasting(us):
    return pl.CostEstimate(flops=us * 10**9, bytes_accessed=us * 3 * 10**6, transcendentals=0)


ANY = pl.BlockSpec(memory_space=pl.ANY)
SMEM = pl.BlockSpec(memory_space=pltpu.SMEM)


def params(mib):
    return pltpu.CompilerParams(
        vmem_limit_bytes=max(mib, LEAST) * 1024 * 1024, dimension_semantics=("arbitrary",)
    )


def call(kernel, token, in_specs, out_specs, out_shape, **rest):
    many = isinstance(out_shape, (list, tuple))
    shapes = list(out_shape) if many else [out_shape]
    specs = list(out_specs) if many else [out_specs]
    n_in = len(in_specs)

    def body(token_ref, *refs):
        kernel(*refs[:n_in], *refs[n_in + 1 :])

    run = pl.pallas_call(
        body,
        in_specs=[ANY] + list(in_specs),
        out_specs=[ANY] + specs,
        out_shape=[jax.ShapeDtypeStruct(token.shape, token.dtype)] + shapes,
        input_output_aliases={0: 0},
        **rest,
    )

    def apply(*args):
        token_out, *outs = run(token, *args)
        return (token_out, *outs)

    return apply


def dot(a, b):
    return lax.dot_general(a, b, (((1,), (0,)), ((), ())), preferred_element_type=F32)


def dot_nt(a, b):
    return lax.dot_general(a, b, (((1,), (1,)), ((), ())), preferred_element_type=F32)


def dot_tn(a, b):
    return lax.dot_general(a, b, (((0,), (0,)), ((), ())), preferred_element_type=F32)


def whole(shape):
    zeros = (0,) * len(shape)
    return pl.BlockSpec(shape, lambda *i: zeros)


class Links:
    def __init__(self, dp, fsdp):
        self.paired = dp == 2 and fsdp == 16
        self.bits = ((4, 4), (8, 8), (1, 2), (2, 1))

    def masks(self):
        table = np.zeros((2, 16), np.int32)
        for core in range(2):
            for p in range(16):
                for bit in range(4):
                    if p >> bit & 1:
                        table[core, p] ^= self.bits[bit][core]
        return table

    def flip(self, x, p):
        table = self.masks()
        pairs = [(c * 16 + f, c * 16 + (f ^ int(table[c, p]))) for c in range(2) for f in range(16)]
        return lax.ppermute(x, AXES, pairs)

    def cross(self, x):
        pairs = [(c * 16 + f, (1 - c) * 16 + f) for c in range(2) for f in range(16)]
        return lax.ppermute(x, AXES, pairs)

    def along_z(self, blocks):
        return [self.flip(block, p) for p, block in zip((1, 2, 3), blocks)]

    def sum_all(self, x):
        x = x + self.cross(x)
        for step in (1, 4):
            one, two, three = [self.flip(x, step * p) for p in (1, 2, 3)]
            x = (x + one) + (two + three)
        return x


def assemble(pieces, order, rows, target, sems, at=0, columns=None):
    copies = []
    n = 0
    for piece in pieces:
        for j in range(piece.shape[0]):
            source = piece.at[j] if columns is None else piece.at[j, :, columns]
            start = pl.multiple_of(order(n) * rows, 16)
            copies.append(
                pltpu.make_async_copy(source, target.at[pl.ds(start, rows)], sems.at[at + n])
            )
            n += 1
    return copies


def deliver(source, order, rows, first, targets, sems, at=0, columns=None):
    copies = []
    n = first
    for target in targets:
        for j in range(target.shape[0]):
            start = pl.multiple_of(order(n) * rows, 16)
            place = target.at[j] if columns is None else target.at[j, :, columns]
            copies.append(
                pltpu.make_async_copy(source.at[pl.ds(start, rows)], place, sems.at[at + n - first])
            )
            n += 1
    return copies


def run_all(copies):
    for copy in copies:
        copy.start()
    for copy in copies:
        copy.wait()


def norm_parts(values):
    center = values - jnp.mean(values, axis=-1, keepdims=True)
    inv = lax.rsqrt(jnp.mean(center * center, axis=-1, keepdims=True) + EPS_NORM)
    return center * inv, inv


def norm_back(u, hat, inv):
    first = jnp.mean(u, axis=-1, keepdims=True)
    second = jnp.mean(u * hat, axis=-1, keepdims=True)
    return inv * (u - first - hat * second)


def sine_terms(count):
    x = 0.25 * np.cos(np.pi * (np.arange(400) + 0.5) / 800)
    powers = x[:, None] ** (2 * np.arange(count)[None, :] + 1)
    scale = powers.max(axis=0)
    found = np.linalg.lstsq(powers / scale, np.sin(2 * np.pi * x), rcond=None)[0]
    return [float(c) for c in found / scale]


SINE = sine_terms(6)
TO_WHOLE = 1.5 * 2.0**23


def embed_kernel(each, n_groups):
    def kernel(table, *refs):
        toks, poss = refs[:n_groups], refs[n_groups : 2 * n_groups]
        embed = refs[-1]
        step = pl.program_id(0)
        p = choose(poss, step, each)
        turns = p * table[0:1, :] + table[2:3, :]
        turns = turns - ((turns + TO_WHOLE) - TO_WHOLE) + p * table[1:2, :]
        x = 0.25 - jnp.abs(turns)
        x2 = x * x
        poly = SINE[-1]
        for coef in SINE[-2::-1]:
            poly = poly * x2 + coef
        embed[0] = choose(toks, step, each).astype(F32) + x * poly

    return kernel


def embed_rows(token, tokens, positions):
    each, length, width = tokens[0].shape
    exact = 10000.0 ** (-2.0 * (np.arange(width) // 2) / width) / (2.0 * math.pi)
    scale = 2.0 ** (11 - np.floor(np.log2(exact)))
    high = np.round(exact * scale) / scale
    table = np.zeros((8, width), np.float32)
    table[0], table[1], table[2] = high, exact - high, -0.25 * (np.arange(width) % 2 == 0)
    specs, clips = pair_specs(tokens, (length, width))
    pos_specs, _ = pair_specs(positions, (length, 1))
    size = clips * length * width
    return call(
        embed_kernel(each, len(tokens)),
        token,
        grid=(clips,),
        in_specs=[whole((8, width))] + specs + pos_specs,
        out_specs=pl.BlockSpec((1, length, width), lambda i: (i, 0, 0)),
        out_shape=jax.ShapeDtypeStruct((clips, length, width), F32),
        compiler_params=params(24),
        cost_estimate=lasting(4),
        name="embed_rows",
    )(jnp.asarray(table), *tokens, *positions)


def pair_specs(groups, block, column=0):
    specs, first = [], 0
    for array in groups:
        n = array.shape[0]

        def index(*at, first=first, n=n):
            return (jnp.clip(at[-1] - first, 0, n - 1), 0, column)

        specs.append(pl.BlockSpec((1,) + block, index))
        first += n
    return specs, first


def choose(refs, step, each):
    value = refs[0][0]
    for k in range(1, len(refs)):
        value = jnp.where(step >= k * each, refs[k][0], value)
    return value


def attend_forward(
    token, sources, small, order, core, counts, pieces, rows, each, first, heads, apart, block
):
    length, width = sources[0].shape[1:]
    source_each, n_sources = sources[0].shape[0], len(sources)
    source_specs, clips = pair_specs(sources, (length, width))
    part = heads * HEAD_DIM
    columns = 3 * part
    fresh = sources[0].dtype == F32
    gathered = small is None
    total_columns = columns + (128 if gathered else 0)
    split = clips > each
    n_pieces = len(pieces)
    blocks = sum(piece.shape[0] for piece in pieces)
    smalls = [] if gathered else [small]

    def kernel(order_ref, core_ref, count_ref, *refs):
        source_refs = refs[:n_sources]
        refs = list(refs[n_sources:])
        small_in = None if gathered else refs.pop(0)
        piece_refs = refs[:n_pieces]
        refs = refs[n_pieces:]
        vectors = refs.pop(0) if gathered else small_in
        normed = refs.pop(0) if fresh else None
        qkv, logs, mixes = refs[0], refs[1], refs[2 : 4 if split else 3]
        weight, bias, sems = refs[-3:]
        step = pl.program_id(0)

        @pl.when(step == 0)
        def _():
            cut = slice(columns * block, columns * block + columns)
            target = weight.at[:, :columns]
            copies = assemble(piece_refs, lambda n: order_ref[n], rows, target, sems, 0, cut)
            if gathered:
                last = piece_refs[0].shape[2]
                target = weight.at[:, columns:]
                cut = slice(last - 128, last)
                copies += assemble(
                    piece_refs, lambda n: order_ref[n], rows, target, sems, blocks, cut
                )
            run_all(copies)
            if gathered:
                vectors[...] = weight[:, columns:].astype(F32).T[:16]
            bias[...] = jnp.zeros_like(bias)
            for pair in range(heads // 2):
                head = first + core_ref[0] * apart + 2 * pair
                at = pl.ds(pl.multiple_of(head * HEAD_DIM, 128), 128)
                bias[0:1, 384 * pair : 384 * pair + 128] = vectors[4:5, at]
                bias[0:1, 384 * pair + 256 : 384 * pair + 384] = vectors[5:6, at]

        if fresh:
            hat, _ = norm_parts(choose(source_refs, step, source_each))
            x = (hat * vectors[0:1, :] + vectors[1:2, :]).astype(BF)
            normed[0] = x
        else:
            x = choose(source_refs, step, source_each)
        low = (dot(x, weight[:, :columns]) + bias[0:1, :]).astype(BF)
        qkv[0] = low
        valid = lax.broadcasted_iota(jnp.int32, (length, 1), 0) < count_ref[step]
        lane = lax.broadcasted_iota(jnp.int32, (1, 2 * HEAD_DIM), 1)
        outs, log_rows = [], []
        for pair in range(heads // 2):
            at = 384 * pair
            q = low[:, at : at + 128] * jnp.asarray(HEAD_DIM**-0.5, BF)
            k = low[:, at + 128 : at + 256]
            v = low[:, at + 256 : at + 384]
            mixed_heads = []
            for half in range(2):
                mine = (lane >= HEAD_DIM) if half else (lane < HEAD_DIM)
                s = dot_nt(jnp.where(mine, k, jnp.zeros_like(k)), q)
                s = jnp.where(valid, s, NEG)
                top = jnp.max(s, axis=0, keepdims=True)
                e = jnp.exp(s - top)
                total = jnp.sum(e, axis=0, keepdims=True)
                p = (e * (1.0 / total)).astype(BF)
                mixed_heads.append(dot_tn(p, v))
                log_rows.append(top + jnp.log(total))
            outs.append(jnp.where(lane < HEAD_DIM, mixed_heads[0], mixed_heads[1]))
        mixed = jnp.concatenate(outs, axis=1).astype(BF)
        logs[0] = jnp.concatenate(log_rows, axis=0)
        if split:

            @pl.when(step < each)
            def _():
                mixes[0][0] = mixed

            @pl.when(step >= each)
            def _():
                mixes[1][0] = mixed

        else:
            mixes[0][0] = mixed

    clip = lambda c: pl.BlockSpec((1, length, c), lambda i: (i, 0, 0))
    own = pl.BlockSpec((1, length, part), lambda i: (jnp.minimum(i, each - 1), 0, 0))
    other = pl.BlockSpec((1, length, part), lambda i: (jnp.clip(i - each, 0, each - 1), 0, 0))
    out_specs, out_shapes = [], []
    if gathered:
        out_specs.append(whole((16, width)))
        out_shapes.append(jax.ShapeDtypeStruct((16, width), F32))
    if fresh:
        out_specs.append(clip(width))
        out_shapes.append(jax.ShapeDtypeStruct((clips, length, width), BF))
    out_specs += [clip(columns), pl.BlockSpec((1, heads, length), lambda i: (i, 0, 0)), own]
    out_shapes += [
        jax.ShapeDtypeStruct((clips, length, columns), BF),
        jax.ShapeDtypeStruct((clips, heads, length), F32),
        jax.ShapeDtypeStruct((each, length, part), BF),
    ]
    if split:
        out_specs.append(other)
        out_shapes.append(jax.ShapeDtypeStruct((clips - each, length, part), BF))
    n_rows = clips * length
    return call(
        kernel,
        token,
        grid=(clips,),
        in_specs=[SMEM, SMEM, SMEM]
        + source_specs
        + [whole((16, width))] * len(smalls)
        + [ANY] * n_pieces,
        out_specs=out_specs,
        out_shape=out_shapes,
        scratch_shapes=[
            pltpu.VMEM((width, total_columns), BF),
            pltpu.VMEM((8, columns), F32),
            pltpu.SemaphoreType.DMA((2 * blocks,)),
        ],
        compiler_params=params(48),
        cost_estimate=lasting(8),
        name="attend_forward",
    )(order, core, counts, *sources, *smalls, *pieces)


def out_weight_copies(own, other, meta, rows, weight, sems):
    cut = slice(own[0].shape[2] - weight.shape[2], None)
    if other is None:
        return assemble(own, lambda n: meta[1 + n], rows, weight.at[0], sems, 0, cut)
    core = meta[0]
    copies = assemble(own, lambda n: meta[1 + n], rows, weight.at[core], sems, 0, cut)
    far = weight.at[1 - core]
    return copies + assemble(other, lambda n: meta[17 + n], rows, far, sems, 16, cut)


def project_norm(token, mixes, places, embed, small, meta, pieces, others, rows):
    n, length, width = mixes[0].shape[0], embed.shape[1], embed.shape[2]
    parts = [mix.shape[2] for mix in mixes]
    n_mix, n_p, n_o = len(mixes), len(pieces), len(others)
    halves = 2 if others else 1
    half_width = width // halves

    def kernel(meta_ref, small_ref, embed_ref, *refs):
        mix_refs = refs[:n_mix]
        own_refs = refs[n_mix : n_mix + n_p]
        other_refs = refs[n_mix + n_p : n_mix + n_p + n_o] or None
        resid, mlp_in, weight, sems = refs[n_mix + n_p + n_o :]

        @pl.when(pl.program_id(0) == 0)
        def _():
            run_all(out_weight_copies(own_refs, other_refs, meta_ref, rows, weight, sems))

        outs = []
        for half in range(halves):
            total = 0.0
            for k, mix in enumerate(mix_refs):
                flip, first = places[k]
                at = first
                if halves > 1:
                    at = pl.multiple_of((meta_ref[0] ^ flip) * half_width + first, 128)
                total = total + dot(mix[0], weight[half, pl.ds(at, parts[k]), :])
            outs.append(total)
        total = jnp.concatenate(outs, axis=1) if halves > 1 else outs[0]
        values = embed_ref[0] + total + small_ref[6:7, :]
        resid[0] = values
        hat, _ = norm_parts(values)
        mlp_in[0] = (hat * small_ref[2:3, :] + small_ref[3:4, :]).astype(BF)

    clip = pl.BlockSpec((1, length, width), lambda i: (i, 0, 0))
    mix_specs = [pl.BlockSpec((1, length, c), lambda i: (i, 0, 0)) for c in parts]
    size = n * length * width
    return call(
        kernel,
        token,
        grid=(n,),
        in_specs=[SMEM, whole((16, width)), clip] + mix_specs + [ANY] * (n_p + n_o),
        out_specs=[clip, clip],
        out_shape=[
            jax.ShapeDtypeStruct((n, length, width), F32),
            jax.ShapeDtypeStruct((n, length, width), BF),
        ],
        scratch_shapes=[
            pltpu.VMEM((halves, width, half_width), BF),
            pltpu.SemaphoreType.DMA((32,)),
        ],
        compiler_params=params(24),
        cost_estimate=lasting(6),
        name="project_norm",
    )(meta, small, embed, *mixes, *pieces, *others)


def mlp_both(
    token, groups, cots, order, counts, bias, bias_row, pieces, rows, relative
):
    each, length, width = groups[0].shape
    hidden = bias.shape[1]
    n_groups, n_pieces = len(groups), len(pieces)
    n_blocks = sum(piece.shape[0] for piece in pieces)
    hidden_rows = hidden // n_blocks
    specs, clips = pair_specs(groups, (length, width))
    n_places = width // rows
    half = n_places // 2
    if relative:
        grad_shapes = [jax.ShapeDtypeStruct((half, rows, 2 * width), BF)]
        grad_shapes += [jax.ShapeDtypeStruct((half // 2, rows, 2 * width), BF)] * 2
    else:
        grad_shapes = [
            jax.ShapeDtypeStruct((1, width, hidden), F32),
            jax.ShapeDtypeStruct((1, hidden, width), F32),
        ]
    own_shape = (each, length, width)
    own_type = BF if n_groups > 1 else F32
    out_shapes = [jax.ShapeDtypeStruct(own_shape, own_type)] * 2
    if n_groups > 1:
        out_shapes += [jax.ShapeDtypeStruct(own_shape, BF)] * 2
    out_shapes += [jax.ShapeDtypeStruct((1, hidden), F32)]

    def kernel(order_ref, count_ref, bias_ref, *refs):
        ins = refs[:n_groups]
        cot_refs = refs[n_groups : 2 * n_groups]
        piece_refs = refs[2 * n_groups : 2 * n_groups + n_pieces]
        outs = refs[2 * n_groups + n_pieces :]
        own_out, own_dm = outs[0], outs[1]
        sent = outs[2:4] if n_groups > 1 else None
        n_out = 4 if n_groups > 1 else 2
        bias_grad = outs[n_out]
        grads = outs[n_out + 1 : -7]
        (up, down, g_up, g_down, low_up, low_down, sems) = outs[-7:]
        i = pl.program_id(0)
        place = lambda n: order_ref[n]

        def weights_in():
            if not relative:
                return [
                    [pltpu.make_async_copy(piece_refs[0].at[0], up, sems.at[0])],
                    [pltpu.make_async_copy(piece_refs[1].at[0], down, sems.at[1])],
                ]
            cut = slice(hidden, None)
            return [
                assemble(piece_refs, place, rows, up, sems, 0, slice(0, hidden)),
                assemble(piece_refs, place, hidden_rows, down, sems, n_blocks, cut),
            ]

        @pl.when(i == 0)
        def _():
            first, second = weights_in()
            run_all(first + second)

        x = choose(ins, i, each)
        valid = lax.broadcasted_iota(jnp.int32, (length, 1), 0) < count_ref[i]
        cot = choose(cot_refs, i, each)
        dd = jnp.where(valid, cot, jnp.zeros_like(cot))
        at_row = bias_row + 2 * order_ref[16] if relative else bias_row
        pre = dot(x, up[...]) + bias_ref[pl.ds(at_row, 1), :]
        cdf = 0.5 + 0.5 * lax.erf(pre * 0.7071067811865476)
        pdf = jnp.exp(pre * pre * -0.5) * 0.3989422804014327
        act = (pre * cdf).astype(BF)
        d_pre = (dot_nt(dd, down[...]) * (cdf + pre * pdf)).astype(BF)
        out = dot(act, down[...])
        dm = dot_nt(d_pre, up[...])
        up_part = dot(x.T, d_pre)
        down_part = dot(act.T, dd)
        bias_part = jnp.sum(d_pre.astype(F32), axis=0, keepdims=True)

        @pl.when(i < each)
        def _():
            own_out[0] = out.astype(own_type)
            own_dm[0] = dm.astype(own_type)

        if sent is not None:

            @pl.when(i >= each)
            def _():
                sent[0][0] = out.astype(BF)
                sent[1][0] = dm.astype(BF)

        @pl.when(i == 0)
        def _():
            g_up[...] = up_part
            g_down[...] = down_part
            bias_grad[...] = bias_part

        @pl.when((i > 0) & (i < clips - 1))
        def _():
            g_up[...] += up_part
            g_down[...] += down_part
            bias_grad[...] += bias_part

        @pl.when(i == clips - 1)
        def _():
            bias_grad[...] += bias_part
            one, two = slice(0, width), slice(width, 2 * width)
            if relative:
                low_up[...] = (g_up[...] + up_part).astype(BF)
                copies = deliver(low_up, place, rows, 0, grads, sems, 0, one)
                for copy in copies:
                    copy.start()
                low_down[...] = (g_down[...] + down_part).astype(BF)
                more = deliver(low_down, place, rows, 0, grads, sems, 2 * half, two)
                for copy in more:
                    copy.start()
                for copy in copies + more:
                    copy.wait()
            else:
                g_up[...] += up_part
                g_down[...] += down_part
                copies = [
                    pltpu.make_async_copy(g_up, grads[0].at[0], sems.at[0]),
                    pltpu.make_async_copy(g_down, grads[1].at[0], sems.at[1]),
                ]
                run_all(copies)

    own_index = lambda i: (jnp.minimum(i, each - 1), 0, 0)
    sent_index = lambda i: (jnp.clip(i - each, 0, each - 1), 0, 0)
    out_specs = [pl.BlockSpec((1, length, width), own_index)] * 2
    if n_groups > 1:
        out_specs += [pl.BlockSpec((1, length, width), sent_index)] * 2
    out_specs += [whole((1, hidden))] + [ANY] * len(grad_shapes)
    low_shape = (width, hidden) if relative else (16, 128)
    low_shape_down = (hidden, width) if relative else (16, 128)
    n_rows = clips * length
    return call(
        kernel,
        token,
        grid=(clips,),
        in_specs=[SMEM, SMEM, whole(bias.shape)] + specs + specs + [ANY] * n_pieces,
        out_specs=out_specs,
        out_shape=out_shapes + grad_shapes,
        scratch_shapes=[
            pltpu.VMEM((width, hidden), BF),
            pltpu.VMEM((hidden, width), BF),
            pltpu.VMEM((width, hidden), F32),
            pltpu.VMEM((hidden, width), F32),
            pltpu.VMEM(low_shape, BF),
            pltpu.VMEM(low_shape_down, BF),
            pltpu.SemaphoreType.DMA((max(2 * n_blocks, 2 * n_places, 2),)),
        ],
        compiler_params=params(56),
        cost_estimate=lasting(23),
        name="mlp_both",
    )(order, counts, bias, *groups, *cots, *pieces)


def norm_two_back(token, dms, resid, cot, small, meta, counts, pieces, others, rows, part):
    n, length, width = resid.shape
    n_dm, n_p, n_o = len(dms), len(pieces), len(others)
    halves = 2 if others else 1
    half_width = width // halves

    def kernel(meta_ref, count_ref, small_ref, resid_ref, cot_ref, *refs):
        dm_refs = refs[:n_dm]
        own_refs = refs[n_dm : n_dm + n_p]
        other_refs = refs[n_dm + n_p : n_dm + n_p + n_o] or None
        outs = refs[n_dm + n_p + n_o :]
        mixes = outs[: halves]
        proj, d_resid, sums, weight, sems = outs[halves:]
        step = pl.program_id(0)

        @pl.when(step == 0)
        def _():
            run_all(out_weight_copies(own_refs, other_refs, meta_ref, rows, weight, sems))

        valid = lax.broadcasted_iota(jnp.int32, (length, 1), 0) < count_ref[step]
        dy = jnp.where(valid, cot_ref[0].astype(F32), 0.0)
        dm = dm_refs[0][0].astype(F32)
        for ref in dm_refs[1:]:
            dm = dm + ref[0].astype(F32)
        hat, inv = norm_parts(resid_ref[0])
        total = dy + norm_back(dm * small_ref[2:3, :], hat, inv)
        d_resid[0] = total
        low = total.astype(BF)
        proj[0] = low
        row = lambda v: jnp.sum(v, axis=0, keepdims=True)
        parts = jnp.concatenate(
            [row(dm * hat), row(dm), row(low.astype(F32)), row(dy), jnp.zeros((4, width), F32)]
        )
        for k in range(halves):
            at = pl.multiple_of((meta_ref[0] ^ k) * part, 128) if halves > 1 else 0
            value = 0.0
            for half in range(halves):
                cut = low[:, half * half_width : (half + 1) * half_width]
                value = value + dot_nt(cut, weight[half, pl.ds(at, part), :])
            mixes[k][0] = value.astype(BF)

        @pl.when(step == 0)
        def _():
            sums[...] = parts

        @pl.when(step > 0)
        def _():
            sums[...] += parts

    clip = pl.BlockSpec((1, length, width), lambda i: (i, 0, 0))
    mix_spec = pl.BlockSpec((1, length, part), lambda i: (i, 0, 0))
    shape = resid.shape
    mix_shape = jax.ShapeDtypeStruct((n, length, part), BF)
    return call(
        kernel,
        token,
        grid=(n,),
        in_specs=[SMEM, SMEM, whole((16, width)), clip, clip]
        + [clip] * n_dm
        + [ANY] * (n_p + n_o),
        out_specs=[mix_spec] * halves + [clip, clip, whole((8, width))],
        out_shape=[mix_shape] * halves
        + [
            jax.ShapeDtypeStruct(shape, BF),
            jax.ShapeDtypeStruct(shape, F32),
            jax.ShapeDtypeStruct((8, width), F32),
        ],
        scratch_shapes=[
            pltpu.VMEM((halves, width, half_width), BF),
            pltpu.SemaphoreType.DMA((32,)),
        ],
        compiler_params=params(32),
        cost_estimate=lasting(7),
        name="norm_two_back",
    )(meta, counts, small, resid, cot, *dms, *pieces, *others)


def out_weight_grad(token, mixes, places, proj, meta, rows):
    n, length, width = proj.shape
    parts = [mix.shape[2] for mix in mixes]
    n_mix = len(mixes)
    halves = 2 if any(flip for flip, _ in places) else 1
    half_width = width // halves
    blocks = width // rows

    def kernel(meta_ref, proj_ref, *refs):
        mix_refs = refs[:n_mix]
        if halves > 1:
            keep, send, total, low, sems = refs[n_mix:]
        else:
            keep, total, sems = refs[n_mix:]
        step = pl.program_id(0)

        @pl.when(step == 0)
        def _():
            total[...] = jnp.zeros_like(total)

        for k in range(n_mix):
            turned = mix_refs[k][0].T
            flip, at = places[k]
            if halves > 1:
                at = pl.multiple_of((meta_ref[0] ^ flip) * half_width + at, 128)
            for half in range(halves):
                cut = proj_ref[0, :, half * half_width : (half + 1) * half_width]
                total[half, pl.ds(at, parts[k]), :] += dot(turned, cut)

        @pl.when(step == n - 1)
        def _():
            if halves > 1:
                core = meta_ref[0]
                low[...] = total[...].astype(BF)
                here, there = low.at[core], low.at[1 - core]
                copies = deliver(here, lambda n: meta_ref[1 + n], rows, 0, [keep], sems, 0)
                copies += deliver(there, lambda n: meta_ref[17 + n], rows, 0, [send], sems, blocks)
                run_all(copies)
            else:
                run_all([pltpu.make_async_copy(total, keep, sems.at[0])])

    clip = lambda c: pl.BlockSpec((1, length, c), lambda i: (i, 0, 0))
    if halves > 1:
        shapes = [
            jax.ShapeDtypeStruct((blocks, rows, half_width), BF),
            jax.ShapeDtypeStruct((blocks, rows, half_width), BF),
        ]
        scratch = [
            pltpu.VMEM((halves, width, half_width), F32),
            pltpu.VMEM((halves, width, half_width), BF),
            pltpu.SemaphoreType.DMA((2 * blocks,)),
        ]
    else:
        shapes = [jax.ShapeDtypeStruct((1, width, width), F32)]
        scratch = [pltpu.VMEM((1, width, width), F32), pltpu.SemaphoreType.DMA((1,))]
    return call(
        kernel,
        token,
        grid=(n,),
        in_specs=[SMEM, clip(width)] + [clip(c) for c in parts],
        out_specs=[ANY] * len(shapes),
        out_shape=shapes,
        scratch_shapes=scratch,
        compiler_params=params(24),
        cost_estimate=lasting(5),
        name="out_weight_grad",
    )(meta, proj, *mixes)


def attend_back(token, groups, qkv, logs, d_mixes, order, counts, rows, relative, first, at_pair, pairs):
    each, length, width = groups[0].shape
    clips = qkv.shape[0]
    columns, part = 384 * pairs, 128 * pairs
    all_heads = logs.shape[1]
    n_groups = len(groups)
    n_mix = len(d_mixes)
    specs, _ = pair_specs(groups, (length, width))
    mix_each = d_mixes[0].shape[0]
    mix_specs, _ = pair_specs(d_mixes, (length, part), at_pair // pairs)
    blocks = width // rows
    half_blocks = blocks // 2

    def kernel(order_ref, count_ref, qkv_ref, log_ref, *refs):
        ins = refs[:n_groups]
        mix_refs = refs[n_groups : n_groups + n_mix]
        refs = refs[n_groups + n_mix :]
        d_qkv, bias_grad = refs[:2]
        if relative:
            keep, send, total, low, sems = refs[2:]
        else:
            keep, total, sems = refs[2:]
        step = pl.program_id(0)
        valid = lax.broadcasted_iota(jnp.int32, (length, 1), 0) < count_ref[step]
        lane = lax.broadcasted_iota(jnp.int32, (1, 2 * HEAD_DIM), 1)
        d_mix = choose(mix_refs, step, mix_each)
        pieces = []
        scale = HEAD_DIM**-0.5
        for pair in range(pairs):
            at = 384 * pair
            q = qkv_ref[0, :, at : at + 128] * jnp.asarray(scale, BF)
            k = qkv_ref[0, :, at + 128 : at + 256]
            v = qkv_ref[0, :, at + 256 : at + 384]
            do = d_mix[:, 128 * pair : 128 * pair + 128]
            k_t = k.T
            dk = dv = None
            turned_q = []
            for half in range(2):
                mine = (lane >= HEAD_DIM) if half else (lane < HEAD_DIM)
                only = lambda x: jnp.where(mine, x, jnp.zeros_like(x))
                s = dot_nt(only(k), q)
                h = 2 * (first + pair) + half
                p = jnp.exp(jnp.where(valid, s, NEG) - log_ref[0, h : h + 1, :])
                dp = dot_nt(only(v), do)
                inner = jnp.sum(dp * p, axis=0, keepdims=True)
                ds = (p * (dp - inner)).astype(BF)
                dv_half = dot(p.astype(BF), only(do))
                dk_half = dot(ds, only(q))
                dv = dv_half if dv is None else dv + dv_half
                dk = dk_half if dk is None else dk + dk_half
                turned_q.append(dot(k_t[HEAD_DIM * half : HEAD_DIM * half + HEAD_DIM], ds))
            pieces += [(jnp.concatenate(turned_q, axis=0) * scale).T, dk, dv]
        low_rows = jnp.concatenate(pieces, axis=1).astype(BF)
        d_qkv[0] = low_rows
        bias_part = jnp.sum(low_rows.astype(F32), axis=0, keepdims=True)
        weight_part = dot(choose(ins, step, each).T, low_rows)

        @pl.when(step == 0)
        def _():
            total[...] = weight_part
            bias_grad[...] = bias_part

        @pl.when(step > 0)
        def _():
            total[...] += weight_part
            bias_grad[...] += bias_part

        @pl.when(step == clips - 1)
        def _():
            place = lambda n: order_ref[n]
            if relative:
                low[...] = total[...].astype(BF)
                run_all(deliver(low, place, rows, 0, [keep, send], sems))
            else:
                run_all([pltpu.make_async_copy(total, keep.at[0], sems.at[0])])

    clip = lambda c: pl.BlockSpec((1, length, c), lambda i: (i, 0, 0))
    block_at = first // pairs
    qkv_spec = pl.BlockSpec((1, length, columns), lambda i: (i, 0, block_at))
    if relative:
        shapes = [
            jax.ShapeDtypeStruct((half_blocks, rows, columns), BF),
            jax.ShapeDtypeStruct((half_blocks, rows, columns), BF),
        ]
        scratch = [pltpu.VMEM((width, columns), F32), pltpu.VMEM((width, columns), BF)]
    else:
        shapes = [jax.ShapeDtypeStruct((1, width, columns), F32)]
        scratch = [pltpu.VMEM((width, columns), F32)]
    n_rows = clips * length
    return call(
        kernel,
        token,
        grid=(clips,),
        in_specs=[
            SMEM,
            SMEM,
            qkv_spec,
            pl.BlockSpec((1, all_heads, length), lambda i: (i, 0, 0)),
        ]
        + specs
        + mix_specs,
        out_specs=[clip(columns), whole((1, columns))] + [ANY] * len(shapes),
        out_shape=[
            jax.ShapeDtypeStruct((clips, length, columns), BF),
            jax.ShapeDtypeStruct((1, columns), F32),
        ]
        + shapes,
        scratch_shapes=scratch + [pltpu.SemaphoreType.DMA((blocks,))],
        compiler_params=params(48),
        cost_estimate=lasting(12),
        name="attend_back",
    )(order, counts, qkv, logs, *groups, *d_mixes)


def attn_in_grad(token, d_qkvs, order, pieces, rows, each, width):
    clips, length, _ = d_qkvs[0].shape
    sizes = [d.shape[2] for d in d_qkvs]
    total = sum(sizes)
    n_d = len(d_qkvs)
    flat = [array for arrays, _ in pieces for array in arrays]
    blocks = sum(array.shape[0] for array in flat)
    split = clips > each

    def kernel(order_ref, *refs):
        row_refs = refs[:n_d]
        piece_refs = refs[n_d : n_d + len(flat)]
        outs = refs[n_d + len(flat) :]
        weight, sems = outs[-2:]
        step = pl.program_id(0)

        @pl.when(step == 0)
        def _():
            copies, used, column = [], 0, 0
            for arrays, size in pieces:
                refs_here = piece_refs[used : used + len(arrays)]
                target = weight.at[:, column : column + size]
                copies += assemble(
                    refs_here, lambda n: order_ref[n], rows, target, sems, len(copies), slice(0, size)
                )
                used += len(arrays)
                column += size
            run_all(copies)

        low = jnp.concatenate([ref[0] for ref in row_refs], axis=1) if n_d > 1 else row_refs[0][0]
        value = dot_nt(low, weight[...])
        if split:

            @pl.when(step < each)
            def _():
                outs[0][0] = value

            @pl.when(step >= each)
            def _():
                outs[1][0] = value.astype(BF)
        else:
            outs[0][0] = value

    own = pl.BlockSpec((1, length, width), lambda i: (jnp.minimum(i, each - 1), 0, 0))
    other = pl.BlockSpec((1, length, width), lambda i: (jnp.clip(i - each, 0, each - 1), 0, 0))
    shapes = [jax.ShapeDtypeStruct((each, length, width), F32)]
    if split:
        shapes.append(jax.ShapeDtypeStruct((each, length, width), BF))
    return call(
        kernel,
        token,
        grid=(clips,),
        in_specs=[SMEM]
        + [pl.BlockSpec((1, length, c), lambda i: (i, 0, 0)) for c in sizes]
        + [ANY] * len(flat),
        out_specs=[own, other][: len(shapes)],
        out_shape=shapes,
        scratch_shapes=[pltpu.VMEM((width, total), BF), pltpu.SemaphoreType.DMA((blocks,))],
        compiler_params=params(32),
        cost_estimate=lasting(7),
        name="attn_in_grad",
    )(order, *d_qkvs, *flat)


def norm_one_back(token, das, embed, d_resid, small):
    n, length, width = d_resid.shape
    n_da = len(das)

    def kernel(small_ref, embed_ref, resid_ref, *refs):
        da_refs = refs[:n_da]
        grad, sums = refs[n_da:]
        step = pl.program_id(0)
        da = da_refs[0][0].astype(F32)
        for ref in da_refs[1:]:
            da = da + ref[0].astype(F32)
        hat, inv = norm_parts(embed_ref[0])
        grad[0] = resid_ref[0] + norm_back(da * small_ref[0:1, :], hat, inv)
        row = lambda v: jnp.sum(v, axis=0, keepdims=True)
        parts = jnp.concatenate([row(da * hat), row(da), jnp.zeros((6, width), F32)])

        @pl.when(step == 0)
        def _():
            sums[...] = parts

        @pl.when(step > 0)
        def _():
            sums[...] += parts

    clip = pl.BlockSpec((1, length, width), lambda i: (i, 0, 0))
    return call(
        kernel,
        token,
        grid=(n,),
        in_specs=[whole((16, width)), clip, clip] + [clip] * n_da,
        out_specs=[clip, whole((8, width))],
        out_shape=[
            jax.ShapeDtypeStruct(d_resid.shape, F32),
            jax.ShapeDtypeStruct((8, width), F32),
        ],
        compiler_params=params(24),
        cost_estimate=lasting(4),
        name="norm_one_back",
    )(small, embed, d_resid, *das)


def update_group(weight, grad, moment, average, grad_norm, weight_norm):
    effective = grad + WEIGHT_DECAY * weight
    moment_new = MOMENTUM_DECAY * moment + effective
    rate = TRUST_RATE * weight_norm / (grad_norm + WEIGHT_DECAY * weight_norm)
    weight_new = weight - rate * (effective + MOMENTUM_DECAY * moment_new)
    average_new = AVERAGE_DECAY * average + (1.0 - AVERAGE_DECAY) * weight_new
    return (weight_new, moment_new, average_new)


def update_all(token, state, sums, place, halves, g_up, g_down, cuts):
    rows, width = state[1].shape
    part = width // 2
    pairs = part // 128
    n_sq = 9

    def kernel(place_ref, sums_ref, own_ref, other_ref, up_ref, down_ref, *refs):
        ins, outs = refs[:15], refs[15:30]
        norms_ref = refs[30]
        core, chip = place_ref[0], place_ref[1]
        small_rows = sums_ref[0:12, :]
        squares = [sums_ref[12:13, k : k + 1] for k in range(n_sq)]
        squares = squares[:4] + [jnp.sum(small_rows * small_rows).reshape(1, 1)] + squares[4:]
        norms = [jnp.sqrt(s) for s in squares]

        def write(group, weight_cols, grad):
            at = (slice(None), weight_cols)
            values = update_group(
                ins[group][at], grad, ins[5 + group][at], ins[10 + group][at],
                norms[group], norms[5 + group],
            )
            for k in range(3):
                outs[5 * k + group][at] = values[k]

        first = core == 0
        for c in range(2):
            pick = lambda own, other: jnp.where(first if c == 0 else ~first, own, other)
            for pair in range(pairs):
                for t in range(3):
                    cut = slice(384 * pair + 128 * t, 384 * pair + 128 * t + 128)
                    at = t * width + c * part + 128 * pair
                    write(0, slice(at, at + 128), pick(own_ref[:, cut], other_ref[:, cut]))
            cut = slice(384 * pairs, 384 * pairs + part)
            write(1, slice(c * part, c * part + part), pick(own_ref[:, cut], other_ref[:, cut]))
        write(2, slice(None), up_ref[...])
        write(3, slice(None), down_ref[...])

        @pl.when(pl.program_id(0) == 0)
        def _():
            lane = lax.broadcasted_iota(jnp.int32, (1, 128), 1)
            row = jnp.zeros((1, 128), F32)
            for k in range(10):
                row = jnp.where(lane == k, norms[k], row)
            norms_ref[...] = row
            shift = lax.rem(width - chip * rows, width)
            mine = pltpu.roll(sums_ref[...], shift, 1)[:, :128]
            grad = mine.T[:rows]
            at = lax.broadcasted_iota(jnp.int32, (rows, 1), 0)
            column = lax.broadcasted_iota(jnp.int32, (1, 16), 1)
            share = rows // 4
            for col in range(4):
                total = jnp.zeros((rows, 128), F32)
                for quarter in range(4):
                    source = (at - share * quarter) * 4 + col
                    inside = (at >= share * quarter) & (at < share * quarter + share)
                    here = inside & (lane == source)
                    total = jnp.where(here, mine[8 + quarter : 9 + quarter, :], total)
                value = jnp.sum(total, axis=1, keepdims=True)
                grad = jnp.where(column == 8 + col, value, grad)
            write(4, slice(None), grad.T[:12])

    tall = lambda x: pl.BlockSpec((x.shape[0] // cuts, x.shape[1]), lambda i: (i, 0))
    state_specs = [whole(x.shape) if k % 5 == 4 else tall(x) for k, x in enumerate(state)]
    return call(
        kernel,
        token,
        grid=(cuts,),
        in_specs=[SMEM, whole(sums.shape)]
        + [tall(x) for x in (*halves, g_up, g_down)]
        + state_specs,
        out_specs=state_specs + [whole((1, 128))],
        out_shape=[jax.ShapeDtypeStruct(x.shape, F32) for x in state]
        + [jax.ShapeDtypeStruct((1, 128), F32)],
        compiler_params=params(48),
        cost_estimate=lasting(6),
        name="update_all",
    )(place, sums, *halves, g_up, g_down, *state)


def weight_squares(token, state):
    def kernel(*refs):
        lane = lax.broadcasted_iota(jnp.int32, (1, 128), 1)
        row = jnp.zeros((1, 128), F32)
        for k, ref in enumerate(refs[:-1]):
            row = jnp.where(lane == k, 0.5 * jnp.sum(ref[...] * ref[...]), row)
        refs[-1][...] = row

    return call(
        kernel,
        token,
        grid=(1,),
        in_specs=[whole(x.shape) for x in state],
        out_specs=whole((1, 128)),
        out_shape=jax.ShapeDtypeStruct((1, 128), F32),
        compiler_params=params(24),
        cost_estimate=lasting(2),
        name="weight_squares",
    )(*state)


def interleave(token, own, other, place):
    rows, total = own.shape
    width = total // 4
    run = rows

    def kernel(place_ref, own_ref, other_ref, up, down, squares):
        both = [slice(2 * width * h, 2 * width * (h + 1)) for h in range(2)]
        own_refs = [own_ref[:, cut] for cut in both]
        other_refs = [other_ref[:, cut] for cut in both]
        first = place_ref[0] == 0
        lane = lax.broadcasted_iota(jnp.int32, (1, 128), 1)
        total_up = sum(jnp.sum(r[:, :width] * r[:, :width]) for r in own_refs)
        total_down = sum(jnp.sum(r[:, width:] * r[:, width:]) for r in own_refs)
        squares[...] = jnp.where(lane == 0, total_up, jnp.where(lane == 1, total_down, 0.0))
        cells = []
        for c in range(2):
            for h in range(2):
                ahead = first if c == 0 else ~first
                cell = jnp.where(ahead, own_refs[h], other_refs[h])
                cells.append(cell[:, :width])
                at = (2 * c + h) * rows
                down[at : at + rows, :] = cell[:, width:]
        for tile in range(4 * width // 128):
            value = None
            low = 128 * tile
            for k in range(low // run, (low + 127) // run + 1):
                f, ch = k // 4, k % 4
                begin, place_at = f * run, k * run - low
                start = min(begin // 128 * 128, width - 256)
                window = cells[ch][:, start : start + 256]
                moved = pltpu.roll(window, (place_at - (begin - start)) % 256, 1)[:, :128]
                if value is None:
                    value = moved
                else:
                    value = jnp.where(lane >= place_at, moved, value)
            up[:, low : low + 128] = value

    return call(
        kernel,
        token,
        grid=(1,),
        in_specs=[SMEM] + [whole(own.shape)] * 2,
        out_specs=[whole((rows, 4 * width)), whole((4 * rows, width)), whole((1, 128))],
        out_shape=[
            jax.ShapeDtypeStruct((rows, 4 * width), F32),
            jax.ShapeDtypeStruct((4 * rows, width), F32),
            jax.ShapeDtypeStruct((1, 128), F32),
        ],
        compiler_params=params(32),
        cost_estimate=lasting(3),
        name="interleave",
    )(place, own, other)


def gather_sums(token, place, sums_one, sums_two, bias_grads, bias_ups, squares_mlp, squares_w):
    width = sums_one.shape[1]
    part = width // 2

    def kernel(place_ref, one, two, *refs):
        grads, ups = refs[: len(bias_grads)], refs[len(bias_grads) : len(bias_grads) + 2]
        sq_mlp, sq_w, out = refs[-3:]
        core = place_ref[0]
        out[...] = jnp.zeros_like(out)
        out[0:2, :] = one[0:2, :]
        out[2:4, :] = two[0:2, :]
        out[6:8, :] = two[2:4, :]
        for c in range(2):

            @pl.when(core == c)
            def _():
                at = c * part
                for ref in grads:
                    for cut in range(0, ref.shape[1], 384):
                        out[4:5, at : at + 128] = ref[:, cut : cut + 128]
                        out[5:6, at : at + 128] = ref[:, cut + 256 : cut + 384]
                        at += 128
                for h in range(2):
                    out[8 + 2 * c + h : 9 + 2 * c + h, :] = ups[h][...]

        lane = lax.broadcasted_iota(jnp.int32, (1, 128), 1)
        row = jnp.where((lane == 2) | (lane == 3), pltpu.roll(sq_mlp[...], 2, 1), 0.0)
        moved = pltpu.roll(sq_w[...], 4, 1)
        out[12:13, :128] = jnp.where((lane >= 4) & (lane < 9), moved, row)

    ins = [sums_one, sums_two, *bias_grads, *bias_ups, squares_mlp, squares_w]
    return call(
        kernel,
        token,
        grid=(1,),
        in_specs=[SMEM] + [whole(x.shape) for x in ins],
        out_specs=whole((16, width)),
        out_shape=jax.ShapeDtypeStruct((16, width), F32),
        compiler_params=params(16),
        cost_estimate=lasting(1),
        name="gather_sums",
    )(place, *ins)


def last_shards(token, sums, wide, narrow, recv_z):
    rows, columns = wide[0].shape[1:]
    more = narrow[0].shape[2]
    inner = 2 * more

    def kernel(sums_ref, *refs):
        wides, narrows, last = refs[:3], refs[3:6], refs[6:9]
        shard, out = refs[9:]
        total = sum(ref[0].astype(F32) for ref in wides)
        extra = sum(ref[0].astype(F32) for ref in narrows)
        for ref in last:
            came = ref[0].astype(F32)
            total = total + came[:, :columns]
            extra = extra + came[:, columns:]
        heads, outer = total[:, :inner], total[:, inner:]
        shard[:, :inner] = heads
        shard[:, inner : inner + more] = extra
        shard[:, inner + more :] = outer
        out[...] = sums_ref[...]
        square = jnp.sum(heads * heads) + jnp.sum(extra * extra)
        lane = lax.broadcasted_iota(jnp.int32, (1, 128), 1)
        old = sums_ref[12:13, :128]
        new = jnp.where(lane == 0, square, jnp.where(lane == 1, jnp.sum(outer * outer), old))
        out[12:13, :128] = new

    block = lambda c: pl.BlockSpec((1, rows, c), lambda i: (0, 0, 0))
    return call(
        kernel,
        token,
        grid=(1,),
        in_specs=[whole(sums.shape)]
        + [block(columns)] * 3
        + [block(more)] * 3
        + [block(columns + more)] * 3,
        out_specs=[whole((rows, columns + more)), whole(sums.shape)],
        out_shape=[
            jax.ShapeDtypeStruct((rows, columns + more), F32),
            jax.ShapeDtypeStruct(sums.shape, F32),
        ],
        compiler_params=params(16),
        cost_estimate=lasting(2),
        name="last_shards",
    )(sums, *wide, *narrow, *recv_z)


def finish(masters, moments, averages, grads, totals):
    norms = jnp.sqrt(totals)
    results = [
        update_group(masters[i], grads[i], moments[i], averages[i], norms[i], norms[5 + i])
        for i in range(5)
    ]
    return (
        tuple(r[0] for r in results)
        + tuple(r[1] for r in results)
        + tuple(r[2] for r in results)
        + (norms,)
    )


def square_sum(x):
    return jnp.sum(x * x)


def tie(*arrays):
    return lax.optimization_barrier(arrays)


def paired_device(links, tokens, positions, counts, cotangent, *state):
    state = [x.T if k % 5 == 4 else x for k, x in enumerate(state)]
    w_qkv, w_out, w_up, w_down, w_small = state[:5]
    each, length, width = tokens.shape
    rows = w_qkv.shape[0]
    core = lax.axis_index("dp")
    chip = lax.axis_index("fsdp")
    table = jnp.asarray(links.masks())
    core_id = core[None].astype(jnp.int32)
    mine = lax.dynamic_index_in_dim(table, core, 0, False) ^ chip
    partner = lax.dynamic_index_in_dim(table, 1 - core, 0, False) ^ chip
    meta = jnp.concatenate([core_id, mine, partner])
    mine = jnp.concatenate([mine, core_id])
    place = jnp.concatenate([core_id, chip[None].astype(jnp.int32)])
    part = width // 2
    pairs = part // 128
    cross, flip, along_z = links.cross, links.flip, links.along_z
    half_core = lambda x, axis: lax.dynamic_index_in_dim(x, core, axis, False)
    join = lambda *blocks: jnp.concatenate(blocks, axis=0)
    beside = lambda *blocks: jnp.concatenate(blocks, axis=2)

    def onward(first, last, keep, *recvs):
        total = keep[first:last].astype(F32)
        for recv in recvs:
            total = total + recv[first:last].astype(F32)
        return total

    cut = half_core(w_qkv.reshape(rows, 3, 2, pairs, 128), 2).astype(BF)
    cut = jnp.swapaxes(cut, 1, 2).reshape(rows, pairs * 384)
    out_cut = half_core(w_out.reshape(rows, 2, part), 1).astype(BF)
    small_cut = jnp.concatenate([w_small[:8], w_small[8:].T.reshape(4, rows)], axis=0)
    small_cut = jnp.pad(small_cut.astype(BF).T, ((0, 0), (0, 116)))
    pack_q = jnp.concatenate([cut[:, :768], small_cut, cut[:, 768:], out_cut], axis=1)[None]
    token = jnp.zeros((8, 128), F32)
    token, pack_q, w_up, w_down, tokens, positions, counts = tie(
        token, pack_q, w_up, w_down, tokens, positions, counts
    )
    q_z = along_z([pack_q] * 3)
    token_other = cross(tokens)
    place_other = cross(jnp.concatenate([positions, counts[:, None]], axis=1))
    column = lambda x: x.astype(F32)[..., None]
    token, embed = embed_rows(token, [tokens], [column(positions)])
    up_cut = half_core(w_up.reshape(rows, 16, 2, 2, rows), 2).astype(BF)
    down_cut = half_core(w_down.reshape(2, 2, rows, width), 0).astype(BF)
    ups = [up_cut[:, :, h].reshape(1, rows, 16 * rows) for h in range(2)]
    downs = [down_cut[h][None] for h in range(2)]
    pack_b = beside(ups[1], downs[1])
    token, ups[0], downs[0], pack_b, token_other, place_other, *q_z = tie(
        token, ups[0], downs[0], pack_b, token_other, place_other, *q_z
    )
    q_4 = join(pack_q, *q_z)

    token, q_4, up_a, token_other, place_other = tie(
        token, q_4, ups[0], token_other, place_other
    )
    q_b = flip(q_4, 4)
    a_zu = along_z([up_a] * 3)
    token, embed_other = embed_rows(
        token, [token_other], [column(place_other[:, :length])]
    )
    counts_all = jnp.concatenate([counts, place_other[:, length]])
    token, q_b, cotangent, *a_zu = tie(token, q_b, cotangent, *a_zu)
    one_8 = join(q_4[:, :, :896], q_b[:, :, :896])
    two_8 = join(q_4[:, :, 896:], q_b[:, :, 896:])

    token, one_8, two_8, down_a, cotangent = tie(token, one_8, two_8, downs[0], cotangent)
    one_c = flip(one_8, 8)
    a_zd = along_z([down_a] * 3)
    cot_other = cross(cotangent)
    token, squares_w = weight_squares(token, state[:5])
    token, one_c, cot_other, squares_w, *a_zd = tie(token, one_c, cot_other, squares_w, *a_zd)
    a_4 = beside(join(up_a, *a_zu), join(down_a, *a_zd))

    embeds = [embed, embed_other]
    token, a_4, two_8, pack_b = tie(token, a_4, two_8, pack_b)
    two_c = flip(two_8, 8)
    a_b = flip(a_4, 4)
    b_z = along_z([pack_b] * 3)
    token, small, attn_in, qkv_1, logs_1, mix_own_1, mix_send_1 = attend_forward(
        token, embeds, None, mine, core_id, counts_all, [one_8, one_c], rows, each, 0, 4, 6, 0
    )
    token, a_4, a_b, two_c, small, attn_in, qkv_1, logs_1, mix_own_1, mix_send_1, *b_z = tie(
        token, a_4, a_b, two_c, small, attn_in, qkv_1, logs_1, mix_own_1, mix_send_1, *b_z
    )
    a_c1 = flip(a_4, 8)
    mix_recv_1 = cross(mix_send_1)
    out_c, out_d = cross(two_8), cross(two_c)
    b_4 = join(pack_b, *b_z)
    token, qkv_2, logs_2, mix_own_2, mix_send_2 = attend_forward(
        token, [attn_in], small, mine, core_id, counts_all, [two_8, two_c], rows, each, 4, 2, 6, 0
    )
    token, a_b, a_c1, b_4, mix_recv_1, out_c, out_d, qkv_2, logs_2, mix_own_2, mix_send_2 = tie(
        token, a_b, a_c1, b_4, mix_recv_1, out_c, out_d, qkv_2, logs_2, mix_own_2, mix_send_2
    )
    a_c2 = flip(a_b, 8)
    mix_recv_2 = cross(mix_send_2)
    mixes = [mix_own_1, mix_own_2, mix_recv_1, mix_recv_2]
    places = [(0, 0), (0, 256), (1, 0), (1, 256)]
    out_pieces = ([two_8, two_c], [out_c, out_d])
    token, resid, mlp_own = project_norm(
        token, mixes, places, embed, small, meta, *out_pieces, rows
    )
    token, a_c2, resid, mlp_own = tie(token, a_c2, resid, mlp_own)
    mlp_other = cross(mlp_own)

    token, mlp_own, mlp_other, b_4, resid = tie(token, mlp_own, mlp_other, b_4, resid)
    b_rest = [flip(b_4, p) for p in (4, 8, 12)]
    groups, cots = [mlp_own, mlp_other], [cotangent, cot_other]
    token, *made_a = mlp_both(
        token, groups, cots, mine, counts_all, small, 8, [a_4, a_b, a_c1, a_c2], rows, True
    )
    token, *both = tie(token, *b_rest, *made_a)
    b_rest, made_a = both[:3], both[3:]
    own_out_a, own_dm_a, sent_out_a, sent_dm_a, bias_up_a, keep_a, *sends = made_a

    a_r3 = [flip(send, 8) for send in sends]
    recv_dm_a, recv_out_a = cross(sent_dm_a), cross(sent_out_a)
    token, *made_b = mlp_both(
        token, groups, cots, mine, counts_all, small, 9, [b_4, *b_rest], rows, True
    )
    token, *both = tie(token, *a_r3, recv_dm_a, recv_out_a, *made_b)
    a_r3, (recv_dm_a, recv_out_a), made_b = both[:2], both[2:4], both[4:]
    own_out_b, own_dm_b, sent_out_b, sent_dm_b, bias_up_b, keep_b, *sends = made_b

    recv_dm_b = cross(sent_dm_b)
    send_a = (keep_a[4:].astype(F32) + a_r3[1].astype(F32)).astype(BF)
    token, recv_dm_b, send_a = tie(token, recv_dm_b, send_a)
    a_r2 = flip(send_a, 4)
    dms = [own_dm_a, own_dm_b, recv_dm_a, recv_dm_b]
    token, d_mix_own, d_mix_send, proj, d_resid, sums_two = norm_two_back(
        token, dms, resid, cotangent, small, meta, counts, *out_pieces, rows, part
    )
    token, a_r2, d_mix_own, d_mix_send, proj, d_resid, sums_two, sent_out_b = tie(
        token, a_r2, d_mix_own, d_mix_send, proj, d_resid, sums_two, sent_out_b
    )

    d_mix_recv = cross(d_mix_send)
    recv_out_b = cross(sent_out_b)
    sends_a = [onward(k, k + 1, keep_a, a_r3[0], a_r2).astype(BF) for k in (1, 2, 3)]
    token, keep_o, send_o = out_weight_grad(token, mixes, places, proj, meta, rows)
    token, d_mix_recv, keep_o, send_o, recv_out_b, *both = tie(
        token, d_mix_recv, keep_o, send_o, recv_out_b, *sends, *sends_a
    )
    sends, sends_a = both[:2], both[2:]

    b_r3 = [flip(send, 8) for send in sends]
    a_rz = along_z(sends_a)
    recv_o = cross(send_o)
    d_mixes = [d_mix_own, d_mix_recv]
    back = lambda token, qkv, logs, first, pair: attend_back(
        token, [attn_in], qkv, logs, d_mixes, mine, counts_all, rows, True, first, pair, 1
    )
    token, *made_0 = back(token, qkv_1, logs_1, 0, 0)
    token, *both = tie(token, *b_r3, *a_rz, recv_o, *made_0)
    b_r3, a_rz, (recv_o, d_qkv_0, bias_grad_0, keep_0, send_0) = both[:2], both[2:5], both[5:]
    send_b = (keep_b[4:].astype(F32) + b_r3[1].astype(F32)).astype(BF)
    total_o = (keep_o.astype(F32) + recv_o.astype(F32)).astype(BF)

    token, total_o, send_b = tie(token, total_o, send_b)
    b_r2 = flip(send_b, 4)
    token, *made_1 = back(token, qkv_1, logs_1, 1, 1)
    token, b_r2, d_qkv_1, bias_grad_1, keep_1, send_1 = tie(token, b_r2, *made_1)
    sends_b = [onward(k, k + 1, keep_b, b_r3[0], b_r2).astype(BF) for k in (1, 2, 3)]
    send_q = beside(send_0, send_1, total_o[8:])

    token, send_q, *sends_b = tie(token, send_q, *sends_b)
    q_r3 = flip(send_q, 8)
    b_rz = along_z(sends_b)
    token, *made_2 = back(token, qkv_2, logs_2, 0, 2)
    token, q_r3, *both = tie(token, q_r3, *b_rz, *made_2)
    b_rz, (d_qkv_2, bias_grad_2, keep_r, send_r) = both[:3], both[3:]
    keep_q = beside(keep_0, keep_1, total_o[:8])
    send_q = onward(4, 8, keep_q, q_r3).astype(BF)

    token, send_q, send_r = tie(token, send_q, send_r)
    r_r3 = flip(send_r, 8)
    q_r2 = flip(send_q, 4)
    token, da_own, da_send = attn_in_grad(
        token, [d_qkv_0, d_qkv_1, d_qkv_2], mine, [([one_8, one_c], 768), ([two_8, two_c], 384)], rows, each, width
    )
    token, r_r3, q_r2, da_own, da_send = tie(token, r_r3, q_r2, da_own, da_send)

    send_r = onward(4, 8, keep_r, r_r3).astype(BF)
    token, send_r = tie(token, send_r)
    r_r2 = flip(send_r, 4)
    da_recv = cross(da_send)
    token, token_grad, sums_one = norm_one_back(
        token, [da_own, da_recv], embed, d_resid, small
    )
    token, r_r2, token_grad, sums_one = tie(token, r_r2, token_grad, sums_one)

    sends_z = [
        beside(
            onward(k, k + 1, keep_q, q_r3, q_r2).astype(BF),
            onward(k, k + 1, keep_r, r_r3, r_r2).astype(BF),
        )
        for k in (1, 2, 3)
    ]
    token, resid, keep_a, keep_b, *sends_z = tie(token, resid, keep_a, keep_b, *sends_z)
    recv_z = along_z(sends_z)
    shard_m = jnp.concatenate(
        [
            onward(0, 1, keep_a, a_r3[0], a_r2, *a_rz)[0],
            onward(0, 1, keep_b, b_r3[0], b_r2, *b_rz)[0],
        ],
        axis=1,
    )
    other_m = cross(shard_m)
    block_rows = resid + small[7]
    for value in (own_out_a, own_out_b, recv_out_a, recv_out_b):
        block_rows = block_rows + value.astype(F32)
    block_out = block_rows.astype(BF)
    token, g_up, g_down, squares_mlp = interleave(token, shard_m, other_m, place)
    bias_grads = [bias_grad_0, bias_grad_1, bias_grad_2]
    token, sums = gather_sums(
        token, place, sums_one, sums_two, bias_grads, (bias_up_a, bias_up_b), squares_mlp, squares_w
    )
    token, block_out, *both = tie(token, block_out, g_up, g_down, sums, *recv_z)
    g_up, g_down, sums, *recv_z = both
    token, shard_q, sums = last_shards(
        token, sums, (keep_q, q_r3, q_r2), (keep_r, r_r3, r_r2), recv_z
    )
    other_q = cross(shard_q)
    sums = links.sum_all(sums)
    results = update_all(token, state, sums, place, (shard_q, other_q), g_up, g_down, 3)[1:]
    outs = [x.T if k % 5 == 4 else x for k, x in enumerate(results[:15])]
    return (block_out, token_grad) + tuple(outs) + (results[15][0, :10],)


def plain_device(tokens, positions, counts, cotangent, *state):
    masters, moments, averages = state[:5], state[5:10], state[10:]
    each, length, width = tokens.shape
    heads = width // HEAD_DIM
    pairs = heads // 2
    full = [
        lax.all_gather(w.astype(BF), "fsdp", axis=0, tiled=True) for w in masters
    ]
    wq, wo, up, down, table = full
    wq = jnp.swapaxes(wq.reshape(width, 3, pairs, 128), 1, 2).reshape(1, width, 3 * width)
    table = table.astype(F32)
    vectors = jnp.concatenate([table[:, :8].T, jnp.zeros((8, width), F32)], axis=0)
    bias_up = table[:, 8:].reshape(1, -1)
    hidden = bias_up.shape[1]
    order = jnp.zeros((33,), jnp.int32)
    token = jnp.zeros((8, 128), F32)
    token, embed = embed_rows(token, [tokens], [positions.astype(F32)[..., None]])
    token, attn_in, qkv, logs, mixed = attend_forward(
        token, [embed], vectors, order, order, counts, [wq], width, each, 0, heads, 0, 0
    )
    places = [(0, 0)]
    token, resid, mlp_in = project_norm(
        token, [mixed], places, embed, vectors, order, [wo[None]], [], width
    )
    outs, dms, bias_ups, ups, downs = [], [], [], [], []
    parts = 4
    size = hidden // parts
    for h in range(parts):
        cols = slice(h * size, (h + 1) * size)
        token, out, dm, bias, g_up, g_down = mlp_both(
            token,
            [mlp_in],
            [cotangent],
            order,
            counts,
            bias_up[:, cols],
            0,
            [up[:, cols][None], down[cols][None]],
            width,
            False,
        )
        outs.append(out)
        dms.append(dm)
        bias_ups.append(bias)
        ups.append(g_up[0])
        downs.append(g_down[0])
    token, d_mix, proj, d_resid, sums_two = norm_two_back(
        token, dms, resid, cotangent, vectors, order, counts, [wo[None]], [], width, width
    )
    token, g_out = out_weight_grad(token, [mixed], places, proj, order, width)
    g_out = g_out[0]
    token, d_qkv, bias_grad, g_qkv = attend_back(
        token, [attn_in], qkv, logs, [d_mix], order, counts, width, False, 0, 0, pairs
    )
    natural = lambda g: jnp.swapaxes(g.reshape(-1, pairs, 3, 128), 1, 2).reshape(-1, 3 * width)
    g_qkv, bias_grad = natural(g_qkv), natural(bias_grad)
    token, da = attn_in_grad(token, [d_qkv], order, [([wq], 3 * width)], width, each, width)
    token, token_grad, sums_one = norm_one_back(token, [da], embed, d_resid, vectors)
    block_rows = resid + vectors[7]
    for value in outs:
        block_rows = block_rows + value
    block_out = block_rows.astype(BF)
    columns = jnp.stack(
        [
            sums_one[0],
            sums_one[1],
            sums_two[0],
            sums_two[1],
            bias_grad[0, :width],
            bias_grad[0, 2 * width :],
            sums_two[2],
            sums_two[3],
        ],
        axis=1,
    )
    small = jnp.concatenate(
        [columns, jnp.concatenate(bias_ups, axis=1).reshape(width, -1)], axis=1
    )
    partial = (
        g_qkv,
        g_out,
        jnp.concatenate(ups, axis=1),
        jnp.concatenate(downs, axis=0),
        small,
    )
    grads = []
    for grad in partial:
        shard = lax.psum_scatter(grad, "fsdp", scatter_dimension=0, tiled=True)
        grads.append(lax.psum(shard, "dp"))
    squares = jnp.stack([square_sum(g) for g in grads] + [square_sum(w) for w in masters])
    totals = lax.psum(squares, "fsdp")
    return (block_out, token_grad) + finish(masters, moments, averages, tuple(grads), totals)


def solution(mesh):
    clips = P(("dp", "fsdp"), None, None)
    in_specs = (clips, P(("dp", "fsdp"), None), P(("dp", "fsdp")), clips) + (P("fsdp", None),) * 15
    out_specs = (clips, clips) + (P("fsdp", None),) * 15 + (P(),)
    links = Links(mesh.shape["dp"], mesh.shape["fsdp"])

    def on_device(*args):
        if links.paired:
            return paired_device(links, *args)
        return plain_device(*args)

    return jax.shard_map(
        on_device, mesh=mesh, in_specs=in_specs, out_specs=out_specs, check_vma=False
    )
```

```python
import math

import jax
import jax.numpy as jnp
import numpy as np
from jax import lax
from jax.experimental import pallas as pl
from jax.experimental.pallas import tpu as pltpu
from jax.sharding import PartitionSpec as P

HEAD_DIM = 64
EPS_NORM = 1e-06
MOMENTUM_DECAY = 0.9
WEIGHT_DECAY = 0.0001
TRUST_RATE = 0.2
AVERAGE_DECAY = 0.8
NEG = -1000000000.0
LEAST = 0

BF = jnp.bfloat16
F32 = jnp.float32
AXES = ("dp", "fsdp")
SHORT = pl.CostEstimate(flops=1, bytes_accessed=1, transcendentals=0)
def lasting(us):
    return pl.CostEstimate(flops=us * 10**9, bytes_accessed=us * 3 * 10**6, transcendentals=0)


ANY = pl.BlockSpec(memory_space=pl.ANY)
SMEM = pl.BlockSpec(memory_space=pltpu.SMEM)


def params(mib):
    return pltpu.CompilerParams(
        vmem_limit_bytes=max(mib, LEAST) * 1024 * 1024, dimension_semantics=("arbitrary",)
    )


def call(kernel, token, in_specs, out_specs, out_shape, **rest):
    many = isinstance(out_shape, (list, tuple))
    shapes = list(out_shape) if many else [out_shape]
    specs = list(out_specs) if many else [out_specs]
    n_in = len(in_specs)

    def body(token_ref, *refs):
        kernel(*refs[:n_in], *refs[n_in + 1 :])

    run = pl.pallas_call(
        body,
        in_specs=[ANY] + list(in_specs),
        out_specs=[ANY] + specs,
        out_shape=[jax.ShapeDtypeStruct(token.shape, token.dtype)] + shapes,
        input_output_aliases={0: 0},
        **rest,
    )

    def apply(*args):
        token_out, *outs = run(token, *args)
        return (token_out, *outs)

    return apply


def dot(a, b):
    return lax.dot_general(a, b, (((1,), (0,)), ((), ())), preferred_element_type=F32)


def dot_nt(a, b):
    return lax.dot_general(a, b, (((1,), (1,)), ((), ())), preferred_element_type=F32)


def dot_tn(a, b):
    return lax.dot_general(a, b, (((0,), (0,)), ((), ())), preferred_element_type=F32)


def whole(shape):
    zeros = (0,) * len(shape)
    return pl.BlockSpec(shape, lambda *i: zeros)


class Links:
    def __init__(self, dp, fsdp):
        self.paired = dp == 2 and fsdp == 16
        self.bits = ((4, 4), (8, 8), (1, 2), (2, 1))

    def masks(self):
        table = np.zeros((2, 16), np.int32)
        for core in range(2):
            for p in range(16):
                for bit in range(4):
                    if p >> bit & 1:
                        table[core, p] ^= self.bits[bit][core]
        return table

    def flip(self, x, p):
        table = self.masks()
        pairs = [(c * 16 + f, c * 16 + (f ^ int(table[c, p]))) for c in range(2) for f in range(16)]
        return lax.ppermute(x, AXES, pairs)

    def cross(self, x):
        pairs = [(c * 16 + f, (1 - c) * 16 + f) for c in range(2) for f in range(16)]
        return lax.ppermute(x, AXES, pairs)

    def along_z(self, blocks):
        return [self.flip(block, p) for p, block in zip((1, 2, 3), blocks)]

    def sum_all(self, x):
        x = x + self.cross(x)
        for step in (4, 1):
            one, two, three = [self.flip(x, step * p) for p in (1, 2, 3)]
            x = (x + one) + (two + three)
        return x


def assemble(pieces, order, rows, target, sems, at=0, columns=None):
    copies = []
    n = 0
    for piece in pieces:
        for j in range(piece.shape[0]):
            source = piece.at[j] if columns is None else piece.at[j, :, columns]
            start = pl.multiple_of(order(n) * rows, 16)
            copies.append(
                pltpu.make_async_copy(source, target.at[pl.ds(start, rows)], sems.at[at + n])
            )
            n += 1
    return copies


def deliver(source, order, rows, first, targets, sems, at=0, columns=None):
    copies = []
    n = first
    for target in targets:
        for j in range(target.shape[0]):
            start = pl.multiple_of(order(n) * rows, 16)
            place = target.at[j] if columns is None else target.at[j, :, columns]
            copies.append(
                pltpu.make_async_copy(source.at[pl.ds(start, rows)], place, sems.at[at + n - first])
            )
            n += 1
    return copies


def run_all(copies):
    for copy in copies:
        copy.start()
    for copy in copies:
        copy.wait()


def norm_parts(values):
    center = values - jnp.mean(values, axis=-1, keepdims=True)
    inv = lax.rsqrt(jnp.mean(center * center, axis=-1, keepdims=True) + EPS_NORM)
    return center * inv, inv


def norm_back(u, hat, inv):
    first = jnp.mean(u, axis=-1, keepdims=True)
    second = jnp.mean(u * hat, axis=-1, keepdims=True)
    return inv * (u - first - hat * second)


def sine_terms(count):
    x = 0.25 * np.cos(np.pi * (np.arange(400) + 0.5) / 800)
    powers = x[:, None] ** (2 * np.arange(count)[None, :] + 1)
    scale = powers.max(axis=0)
    found = np.linalg.lstsq(powers / scale, np.sin(2 * np.pi * x), rcond=None)[0]
    return [float(c) for c in found / scale]


SINE = sine_terms(6)
TO_WHOLE = 1.5 * 2.0**23


def embed_kernel(each, n_groups):
    def kernel(table, *refs):
        toks, poss = refs[:n_groups], refs[n_groups : 2 * n_groups]
        embed = refs[-1]
        step = pl.program_id(0)
        p = choose(poss, step, each)
        turns = p * table[0:1, :] + table[2:3, :]
        turns = turns - ((turns + TO_WHOLE) - TO_WHOLE) + p * table[1:2, :]
        x = 0.25 - jnp.abs(turns)
        x2 = x * x
        poly = SINE[-1]
        for coef in SINE[-2::-1]:
            poly = poly * x2 + coef
        embed[0] = choose(toks, step, each).astype(F32) + x * poly

    return kernel


def embed_rows(token, tokens, positions):
    each, length, width = tokens[0].shape
    exact = 10000.0 ** (-2.0 * (np.arange(width) // 2) / width) / (2.0 * math.pi)
    scale = 2.0 ** (11 - np.floor(np.log2(exact)))
    high = np.round(exact * scale) / scale
    table = np.zeros((8, width), np.float32)
    table[0], table[1], table[2] = high, exact - high, -0.25 * (np.arange(width) % 2 == 0)
    specs, clips = pair_specs(tokens, (length, width))
    pos_specs, _ = pair_specs(positions, (length, 1))
    size = clips * length * width
    return call(
        embed_kernel(each, len(tokens)),
        token,
        grid=(clips,),
        in_specs=[whole((8, width))] + specs + pos_specs,
        out_specs=pl.BlockSpec((1, length, width), lambda i: (i, 0, 0)),
        out_shape=jax.ShapeDtypeStruct((clips, length, width), F32),
        compiler_params=params(24),
        cost_estimate=lasting(4),
        name="embed_rows",
    )(jnp.asarray(table), *tokens, *positions)


def pair_specs(groups, block, column=0):
    specs, first = [], 0
    for array in groups:
        n = array.shape[0]

        def index(*at, first=first, n=n):
            return (jnp.clip(at[-1] - first, 0, n - 1), 0, column)

        specs.append(pl.BlockSpec((1,) + block, index))
        first += n
    return specs, first


def choose(refs, step, each):
    value = refs[0][0]
    for k in range(1, len(refs)):
        value = jnp.where(step >= k * each, refs[k][0], value)
    return value


def attend_forward(
    token, sources, small, order, core, counts, pieces, rows, each, first, heads, apart, block
):
    length, width = sources[0].shape[1:]
    source_each, n_sources = sources[0].shape[0], len(sources)
    source_specs, clips = pair_specs(sources, (length, width))
    part = heads * HEAD_DIM
    columns = 3 * part
    fresh = sources[0].dtype == F32
    gathered = small is None
    total_columns = columns + (128 if gathered else 0)
    split = clips > each
    n_pieces = len(pieces)
    blocks = sum(piece.shape[0] for piece in pieces)
    smalls = [] if gathered else [small]

    def kernel(order_ref, core_ref, count_ref, *refs):
        source_refs = refs[:n_sources]
        refs = list(refs[n_sources:])
        small_in = None if gathered else refs.pop(0)
        piece_refs = refs[:n_pieces]
        refs = refs[n_pieces:]
        vectors = refs.pop(0) if gathered else small_in
        normed = refs.pop(0) if fresh else None
        qkv, logs, mixes = refs[0], refs[1], refs[2 : 4 if split else 3]
        weight, bias, sems = refs[-3:]
        step = pl.program_id(0)

        @pl.when(step == 0)
        def _():
            cut = slice(columns * block, columns * block + columns)
            target = weight.at[:, :columns]
            copies = assemble(piece_refs, lambda n: order_ref[n], rows, target, sems, 0, cut)
            if gathered:
                last = piece_refs[0].shape[2]
                target = weight.at[:, columns:]
                cut = slice(last - 128, last)
                copies += assemble(
                    piece_refs, lambda n: order_ref[n], rows, target, sems, blocks, cut
                )
            run_all(copies)
            if gathered:
                vectors[...] = weight[:, columns:].astype(F32).T[:16]
            bias[...] = jnp.zeros_like(bias)
            for pair in range(heads // 2):
                head = first + core_ref[0] * apart + 2 * pair
                at = pl.ds(pl.multiple_of(head * HEAD_DIM, 128), 128)
                bias[0:1, 384 * pair : 384 * pair + 128] = vectors[4:5, at]
                bias[0:1, 384 * pair + 256 : 384 * pair + 384] = vectors[5:6, at]

        if fresh:
            hat, _ = norm_parts(choose(source_refs, step, source_each))
            x = (hat * vectors[0:1, :] + vectors[1:2, :]).astype(BF)
            normed[0] = x
        else:
            x = choose(source_refs, step, source_each)
        low = (dot(x, weight[:, :columns]) + bias[0:1, :]).astype(BF)
        qkv[0] = low
        valid = lax.broadcasted_iota(jnp.int32, (length, 1), 0) < count_ref[step]
        lane = lax.broadcasted_iota(jnp.int32, (1, 2 * HEAD_DIM), 1)
        outs, log_rows = [], []
        for pair in range(heads // 2):
            at = 384 * pair
            q = low[:, at : at + 128] * jnp.asarray(HEAD_DIM**-0.5, BF)
            k = low[:, at + 128 : at + 256]
            v = low[:, at + 256 : at + 384]
            mixed_heads = []
            for half in range(2):
                mine = (lane >= HEAD_DIM) if half else (lane < HEAD_DIM)
                s = dot_nt(jnp.where(mine, k, jnp.zeros_like(k)), q)
                s = jnp.where(valid, s, NEG)
                top = jnp.max(s, axis=0, keepdims=True)
                e = jnp.exp(s - top)
                total = jnp.sum(e, axis=0, keepdims=True)
                p = (e * (1.0 / total)).astype(BF)
                mixed_heads.append(dot_tn(p, v))
                log_rows.append(top + jnp.log(total))
            outs.append(jnp.where(lane < HEAD_DIM, mixed_heads[0], mixed_heads[1]))
        mixed = jnp.concatenate(outs, axis=1).astype(BF)
        logs[0] = jnp.concatenate(log_rows, axis=0)
        if split:

            @pl.when(step < each)
            def _():
                mixes[0][0] = mixed

            @pl.when(step >= each)
            def _():
                mixes[1][0] = mixed

        else:
            mixes[0][0] = mixed

    clip = lambda c: pl.BlockSpec((1, length, c), lambda i: (i, 0, 0))
    own = pl.BlockSpec((1, length, part), lambda i: (jnp.minimum(i, each - 1), 0, 0))
    other = pl.BlockSpec((1, length, part), lambda i: (jnp.clip(i - each, 0, each - 1), 0, 0))
    out_specs, out_shapes = [], []
    if gathered:
        out_specs.append(whole((16, width)))
        out_shapes.append(jax.ShapeDtypeStruct((16, width), F32))
    if fresh:
        out_specs.append(clip(width))
        out_shapes.append(jax.ShapeDtypeStruct((clips, length, width), BF))
    out_specs += [clip(columns), pl.BlockSpec((1, heads, length), lambda i: (i, 0, 0)), own]
    out_shapes += [
        jax.ShapeDtypeStruct((clips, length, columns), BF),
        jax.ShapeDtypeStruct((clips, heads, length), F32),
        jax.ShapeDtypeStruct((each, length, part), BF),
    ]
    if split:
        out_specs.append(other)
        out_shapes.append(jax.ShapeDtypeStruct((clips - each, length, part), BF))
    n_rows = clips * length
    return call(
        kernel,
        token,
        grid=(clips,),
        in_specs=[SMEM, SMEM, SMEM]
        + source_specs
        + [whole((16, width))] * len(smalls)
        + [ANY] * n_pieces,
        out_specs=out_specs,
        out_shape=out_shapes,
        scratch_shapes=[
            pltpu.VMEM((width, total_columns), BF),
            pltpu.VMEM((8, columns), F32),
            pltpu.SemaphoreType.DMA((2 * blocks,)),
        ],
        compiler_params=params(48),
        cost_estimate=lasting(8),
        name="attend_forward",
    )(order, core, counts, *sources, *smalls, *pieces)


def out_weight_copies(own, other, meta, rows, weight, sems):
    cut = slice(own[0].shape[2] - weight.shape[2], None)
    if other is None:
        return assemble(own, lambda n: meta[1 + n], rows, weight.at[0], sems, 0, cut)
    core = meta[0]
    copies = assemble(own, lambda n: meta[1 + n], rows, weight.at[core], sems, 0, cut)
    far = weight.at[1 - core]
    return copies + assemble(other, lambda n: meta[17 + n], rows, far, sems, 16, cut)


def project_norm(token, mixes, places, embed, small, meta, pieces, others, rows):
    n, length, width = mixes[0].shape[0], embed.shape[1], embed.shape[2]
    parts = [mix.shape[2] for mix in mixes]
    n_mix, n_p, n_o = len(mixes), len(pieces), len(others)
    halves = 2 if others else 1
    half_width = width // halves

    def kernel(meta_ref, small_ref, embed_ref, *refs):
        mix_refs = refs[:n_mix]
        own_refs = refs[n_mix : n_mix + n_p]
        other_refs = refs[n_mix + n_p : n_mix + n_p + n_o] or None
        resid, mlp_in, weight, sems = refs[n_mix + n_p + n_o :]

        @pl.when(pl.program_id(0) == 0)
        def _():
            run_all(out_weight_copies(own_refs, other_refs, meta_ref, rows, weight, sems))

        outs = []
        for half in range(halves):
            total = 0.0
            for k, mix in enumerate(mix_refs):
                flip, first = places[k]
                at = first
                if halves > 1:
                    at = pl.multiple_of((meta_ref[0] ^ flip) * half_width + first, 128)
                total = total + dot(mix[0], weight[half, pl.ds(at, parts[k]), :])
            outs.append(total)
        total = jnp.concatenate(outs, axis=1) if halves > 1 else outs[0]
        values = embed_ref[0] + total + small_ref[6:7, :]
        resid[0] = values
        hat, _ = norm_parts(values)
        mlp_in[0] = (hat * small_ref[2:3, :] + small_ref[3:4, :]).astype(BF)

    clip = pl.BlockSpec((1, length, width), lambda i: (i, 0, 0))
    mix_specs = [pl.BlockSpec((1, length, c), lambda i: (i, 0, 0)) for c in parts]
    size = n * length * width
    return call(
        kernel,
        token,
        grid=(n,),
        in_specs=[SMEM, whole((16, width)), clip] + mix_specs + [ANY] * (n_p + n_o),
        out_specs=[clip, clip],
        out_shape=[
            jax.ShapeDtypeStruct((n, length, width), F32),
            jax.ShapeDtypeStruct((n, length, width), BF),
        ],
        scratch_shapes=[
            pltpu.VMEM((halves, width, half_width), BF),
            pltpu.SemaphoreType.DMA((32,)),
        ],
        compiler_params=params(24),
        cost_estimate=lasting(6),
        name="project_norm",
    )(meta, small, embed, *mixes, *pieces, *others)


def mlp_both(
    token, groups, cots, order, counts, bias, bias_row, pieces, rows, relative
):
    each, length, width = groups[0].shape
    hidden = bias.shape[1]
    n_groups, n_pieces = len(groups), len(pieces)
    n_blocks = sum(piece.shape[0] for piece in pieces)
    hidden_rows = hidden // n_blocks
    specs, clips = pair_specs(groups, (length, width))
    n_places = width // rows
    half = n_places // 2
    if relative:
        grad_shapes = [jax.ShapeDtypeStruct((half, rows, 2 * width), BF)]
        grad_shapes += [jax.ShapeDtypeStruct((half // 2, rows, 2 * width), BF)] * 2
    else:
        grad_shapes = [
            jax.ShapeDtypeStruct((1, width, hidden), F32),
            jax.ShapeDtypeStruct((1, hidden, width), F32),
        ]
    own_shape = (each, length, width)
    own_type = BF if n_groups > 1 else F32
    out_shapes = [jax.ShapeDtypeStruct(own_shape, own_type)] * 2
    if n_groups > 1:
        out_shapes += [jax.ShapeDtypeStruct(own_shape, BF)] * 2
    out_shapes += [jax.ShapeDtypeStruct((1, hidden), F32)]

    def kernel(order_ref, count_ref, bias_ref, *refs):
        ins = refs[:n_groups]
        cot_refs = refs[n_groups : 2 * n_groups]
        piece_refs = refs[2 * n_groups : 2 * n_groups + n_pieces]
        outs = refs[2 * n_groups + n_pieces :]
        own_out, own_dm = outs[0], outs[1]
        sent = outs[2:4] if n_groups > 1 else None
        n_out = 4 if n_groups > 1 else 2
        bias_grad = outs[n_out]
        grads = outs[n_out + 1 : -7]
        (up, down, g_up, g_down, low_up, low_down, sems) = outs[-7:]
        i = pl.program_id(0)
        place = lambda n: order_ref[n]

        def weights_in():
            if not relative:
                return [
                    [pltpu.make_async_copy(piece_refs[0].at[0], up, sems.at[0])],
                    [pltpu.make_async_copy(piece_refs[1].at[0], down, sems.at[1])],
                ]
            cut = slice(hidden, None)
            return [
                assemble(piece_refs, place, rows, up, sems, 0, slice(0, hidden)),
                assemble(piece_refs, place, hidden_rows, down, sems, n_blocks, cut),
            ]

        @pl.when(i == 0)
        def _():
            first, second = weights_in()
            run_all(first + second)

        x = choose(ins, i, each)
        valid = lax.broadcasted_iota(jnp.int32, (length, 1), 0) < count_ref[i]
        cot = choose(cot_refs, i, each)
        dd = jnp.where(valid, cot, jnp.zeros_like(cot))
        at_row = bias_row + 2 * order_ref[16] if relative else bias_row
        pre = dot(x, up[...]) + bias_ref[pl.ds(at_row, 1), :]
        cdf = 0.5 + 0.5 * lax.erf(pre * 0.7071067811865476)
        pdf = jnp.exp(pre * pre * -0.5) * 0.3989422804014327
        act = (pre * cdf).astype(BF)
        d_pre = (dot_nt(dd, down[...]) * (cdf + pre * pdf)).astype(BF)
        out = dot(act, down[...])
        dm = dot_nt(d_pre, up[...])
        up_part = dot(x.T, d_pre)
        down_part = dot(act.T, dd)
        bias_part = jnp.sum(d_pre.astype(F32), axis=0, keepdims=True)

        @pl.when(i < each)
        def _():
            own_out[0] = out.astype(own_type)
            own_dm[0] = dm.astype(own_type)

        if sent is not None:

            @pl.when(i >= each)
            def _():
                sent[0][0] = out.astype(BF)
                sent[1][0] = dm.astype(BF)

        @pl.when(i == 0)
        def _():
            g_up[...] = up_part
            g_down[...] = down_part
            bias_grad[...] = bias_part

        @pl.when((i > 0) & (i < clips - 1))
        def _():
            g_up[...] += up_part
            g_down[...] += down_part
            bias_grad[...] += bias_part

        @pl.when(i == clips - 1)
        def _():
            bias_grad[...] += bias_part
            one, two = slice(0, width), slice(width, 2 * width)
            if relative:
                low_up[...] = (g_up[...] + up_part).astype(BF)
                copies = deliver(low_up, place, rows, 0, grads, sems, 0, one)
                for copy in copies:
                    copy.start()
                low_down[...] = (g_down[...] + down_part).astype(BF)
                more = deliver(low_down, place, rows, 0, grads, sems, 2 * half, two)
                for copy in more:
                    copy.start()
                for copy in copies + more:
                    copy.wait()
            else:
                g_up[...] += up_part
                g_down[...] += down_part
                copies = [
                    pltpu.make_async_copy(g_up, grads[0].at[0], sems.at[0]),
                    pltpu.make_async_copy(g_down, grads[1].at[0], sems.at[1]),
                ]
                run_all(copies)

    own_index = lambda i: (jnp.minimum(i, each - 1), 0, 0)
    sent_index = lambda i: (jnp.clip(i - each, 0, each - 1), 0, 0)
    out_specs = [pl.BlockSpec((1, length, width), own_index)] * 2
    if n_groups > 1:
        out_specs += [pl.BlockSpec((1, length, width), sent_index)] * 2
    out_specs += [whole((1, hidden))] + [ANY] * len(grad_shapes)
    low_shape = (width, hidden) if relative else (16, 128)
    low_shape_down = (hidden, width) if relative else (16, 128)
    n_rows = clips * length
    return call(
        kernel,
        token,
        grid=(clips,),
        in_specs=[SMEM, SMEM, whole(bias.shape)] + specs + specs + [ANY] * n_pieces,
        out_specs=out_specs,
        out_shape=out_shapes + grad_shapes,
        scratch_shapes=[
            pltpu.VMEM((width, hidden), BF),
            pltpu.VMEM((hidden, width), BF),
            pltpu.VMEM((width, hidden), F32),
            pltpu.VMEM((hidden, width), F32),
            pltpu.VMEM(low_shape, BF),
            pltpu.VMEM(low_shape_down, BF),
            pltpu.SemaphoreType.DMA((max(2 * n_blocks, 2 * n_places, 2),)),
        ],
        compiler_params=params(56),
        cost_estimate=lasting(23),
        name="mlp_both",
    )(order, counts, bias, *groups, *cots, *pieces)


def norm_two_back(token, dms, resid, cot, small, meta, counts, pieces, others, rows, part):
    n, length, width = resid.shape
    n_dm, n_p, n_o = len(dms), len(pieces), len(others)
    halves = 2 if others else 1
    half_width = width // halves

    def kernel(meta_ref, count_ref, small_ref, resid_ref, cot_ref, *refs):
        dm_refs = refs[:n_dm]
        own_refs = refs[n_dm : n_dm + n_p]
        other_refs = refs[n_dm + n_p : n_dm + n_p + n_o] or None
        outs = refs[n_dm + n_p + n_o :]
        mixes = outs[: halves]
        proj, d_resid, sums, weight, sems = outs[halves:]
        step = pl.program_id(0)

        @pl.when(step == 0)
        def _():
            run_all(out_weight_copies(own_refs, other_refs, meta_ref, rows, weight, sems))

        valid = lax.broadcasted_iota(jnp.int32, (length, 1), 0) < count_ref[step]
        dy = jnp.where(valid, cot_ref[0].astype(F32), 0.0)
        dm = dm_refs[0][0].astype(F32)
        for ref in dm_refs[1:]:
            dm = dm + ref[0].astype(F32)
        hat, inv = norm_parts(resid_ref[0])
        total = dy + norm_back(dm * small_ref[2:3, :], hat, inv)
        d_resid[0] = total
        low = total.astype(BF)
        proj[0] = low
        row = lambda v: jnp.sum(v, axis=0, keepdims=True)
        parts = jnp.concatenate(
            [row(dm * hat), row(dm), row(low.astype(F32)), row(dy), jnp.zeros((4, width), F32)]
        )
        for k in range(halves):
            at = pl.multiple_of((meta_ref[0] ^ k) * part, 128) if halves > 1 else 0
            value = 0.0
            for half in range(halves):
                cut = low[:, half * half_width : (half + 1) * half_width]
                value = value + dot_nt(cut, weight[half, pl.ds(at, part), :])
            mixes[k][0] = value.astype(BF)

        @pl.when(step == 0)
        def _():
            sums[...] = parts

        @pl.when(step > 0)
        def _():
            sums[...] += parts

    clip = pl.BlockSpec((1, length, width), lambda i: (i, 0, 0))
    mix_spec = pl.BlockSpec((1, length, part), lambda i: (i, 0, 0))
    shape = resid.shape
    mix_shape = jax.ShapeDtypeStruct((n, length, part), BF)
    return call(
        kernel,
        token,
        grid=(n,),
        in_specs=[SMEM, SMEM, whole((16, width)), clip, clip]
        + [clip] * n_dm
        + [ANY] * (n_p + n_o),
        out_specs=[mix_spec] * halves + [clip, clip, whole((8, width))],
        out_shape=[mix_shape] * halves
        + [
            jax.ShapeDtypeStruct(shape, BF),
            jax.ShapeDtypeStruct(shape, F32),
            jax.ShapeDtypeStruct((8, width), F32),
        ],
        scratch_shapes=[
            pltpu.VMEM((halves, width, half_width), BF),
            pltpu.SemaphoreType.DMA((32,)),
        ],
        compiler_params=params(32),
        cost_estimate=lasting(7),
        name="norm_two_back",
    )(meta, counts, small, resid, cot, *dms, *pieces, *others)


def out_weight_grad(token, mixes, places, proj, meta, rows):
    n, length, width = proj.shape
    parts = [mix.shape[2] for mix in mixes]
    n_mix = len(mixes)
    halves = 2 if any(flip for flip, _ in places) else 1
    half_width = width // halves
    blocks = width // rows

    def kernel(meta_ref, proj_ref, *refs):
        mix_refs = refs[:n_mix]
        if halves > 1:
            keep, send, total, low, sems = refs[n_mix:]
        else:
            keep, total, sems = refs[n_mix:]
        step = pl.program_id(0)

        @pl.when(step == 0)
        def _():
            total[...] = jnp.zeros_like(total)

        for k in range(n_mix):
            turned = mix_refs[k][0].T
            flip, at = places[k]
            if halves > 1:
                at = pl.multiple_of((meta_ref[0] ^ flip) * half_width + at, 128)
            for half in range(halves):
                cut = proj_ref[0, :, half * half_width : (half + 1) * half_width]
                total[half, pl.ds(at, parts[k]), :] += dot(turned, cut)

        @pl.when(step == n - 1)
        def _():
            if halves > 1:
                core = meta_ref[0]
                low[...] = total[...].astype(BF)
                here, there = low.at[core], low.at[1 - core]
                copies = deliver(here, lambda n: meta_ref[1 + n], rows, 0, [keep], sems, 0)
                copies += deliver(there, lambda n: meta_ref[17 + n], rows, 0, [send], sems, blocks)
                run_all(copies)
            else:
                run_all([pltpu.make_async_copy(total, keep, sems.at[0])])

    clip = lambda c: pl.BlockSpec((1, length, c), lambda i: (i, 0, 0))
    if halves > 1:
        shapes = [
            jax.ShapeDtypeStruct((blocks, rows, half_width), BF),
            jax.ShapeDtypeStruct((blocks, rows, half_width), BF),
        ]
        scratch = [
            pltpu.VMEM((halves, width, half_width), F32),
            pltpu.VMEM((halves, width, half_width), BF),
            pltpu.SemaphoreType.DMA((2 * blocks,)),
        ]
    else:
        shapes = [jax.ShapeDtypeStruct((1, width, width), F32)]
        scratch = [pltpu.VMEM((1, width, width), F32), pltpu.SemaphoreType.DMA((1,))]
    return call(
        kernel,
        token,
        grid=(n,),
        in_specs=[SMEM, clip(width)] + [clip(c) for c in parts],
        out_specs=[ANY] * len(shapes),
        out_shape=shapes,
        scratch_shapes=scratch,
        compiler_params=params(24),
        cost_estimate=lasting(5),
        name="out_weight_grad",
    )(meta, proj, *mixes)


def attend_back(token, groups, qkv, logs, d_mixes, order, counts, rows, relative, first, at_pair, pairs):
    each, length, width = groups[0].shape
    clips = qkv.shape[0]
    columns, part = 384 * pairs, 128 * pairs
    all_heads = logs.shape[1]
    n_groups = len(groups)
    n_mix = len(d_mixes)
    specs, _ = pair_specs(groups, (length, width))
    mix_each = d_mixes[0].shape[0]
    mix_specs, _ = pair_specs(d_mixes, (length, part), at_pair // pairs)
    blocks = width // rows
    half_blocks = blocks // 2

    def kernel(order_ref, count_ref, qkv_ref, log_ref, *refs):
        ins = refs[:n_groups]
        mix_refs = refs[n_groups : n_groups + n_mix]
        refs = refs[n_groups + n_mix :]
        d_qkv, bias_grad = refs[:2]
        if relative:
            keep, send, total, low, sems = refs[2:]
        else:
            keep, total, sems = refs[2:]
        step = pl.program_id(0)
        valid = lax.broadcasted_iota(jnp.int32, (length, 1), 0) < count_ref[step]
        lane = lax.broadcasted_iota(jnp.int32, (1, 2 * HEAD_DIM), 1)
        d_mix = choose(mix_refs, step, mix_each)
        pieces = []
        scale = HEAD_DIM**-0.5
        for pair in range(pairs):
            at = 384 * pair
            q = qkv_ref[0, :, at : at + 128] * jnp.asarray(scale, BF)
            k = qkv_ref[0, :, at + 128 : at + 256]
            v = qkv_ref[0, :, at + 256 : at + 384]
            do = d_mix[:, 128 * pair : 128 * pair + 128]
            k_t = k.T
            dk = dv = None
            turned_q = []
            for half in range(2):
                mine = (lane >= HEAD_DIM) if half else (lane < HEAD_DIM)
                only = lambda x: jnp.where(mine, x, jnp.zeros_like(x))
                s = dot_nt(only(k), q)
                h = 2 * (first + pair) + half
                p = jnp.exp(jnp.where(valid, s, NEG) - log_ref[0, h : h + 1, :])
                dp = dot_nt(only(v), do)
                inner = jnp.sum(dp * p, axis=0, keepdims=True)
                ds = (p * (dp - inner)).astype(BF)
                dv_half = dot(p.astype(BF), only(do))
                dk_half = dot(ds, only(q))
                dv = dv_half if dv is None else dv + dv_half
                dk = dk_half if dk is None else dk + dk_half
                turned_q.append(dot(k_t[HEAD_DIM * half : HEAD_DIM * half + HEAD_DIM], ds))
            pieces += [(jnp.concatenate(turned_q, axis=0) * scale).T, dk, dv]
        low_rows = jnp.concatenate(pieces, axis=1).astype(BF)
        d_qkv[0] = low_rows
        bias_part = jnp.sum(low_rows.astype(F32), axis=0, keepdims=True)
        weight_part = dot(choose(ins, step, each).T, low_rows)

        @pl.when(step == 0)
        def _():
            total[...] = weight_part
            bias_grad[...] = bias_part

        @pl.when(step > 0)
        def _():
            total[...] += weight_part
            bias_grad[...] += bias_part

        @pl.when(step == clips - 1)
        def _():
            place = lambda n: order_ref[n]
            if relative:
                low[...] = total[...].astype(BF)
                run_all(deliver(low, place, rows, 0, [keep, send], sems))
            else:
                run_all([pltpu.make_async_copy(total, keep.at[0], sems.at[0])])

    clip = lambda c: pl.BlockSpec((1, length, c), lambda i: (i, 0, 0))
    block_at = first // pairs
    qkv_spec = pl.BlockSpec((1, length, columns), lambda i: (i, 0, block_at))
    if relative:
        shapes = [
            jax.ShapeDtypeStruct((half_blocks, rows, columns), BF),
            jax.ShapeDtypeStruct((half_blocks, rows, columns), BF),
        ]
        scratch = [pltpu.VMEM((width, columns), F32), pltpu.VMEM((width, columns), BF)]
    else:
        shapes = [jax.ShapeDtypeStruct((1, width, columns), F32)]
        scratch = [pltpu.VMEM((width, columns), F32)]
    n_rows = clips * length
    return call(
        kernel,
        token,
        grid=(clips,),
        in_specs=[
            SMEM,
            SMEM,
            qkv_spec,
            pl.BlockSpec((1, all_heads, length), lambda i: (i, 0, 0)),
        ]
        + specs
        + mix_specs,
        out_specs=[clip(columns), whole((1, columns))] + [ANY] * len(shapes),
        out_shape=[
            jax.ShapeDtypeStruct((clips, length, columns), BF),
            jax.ShapeDtypeStruct((1, columns), F32),
        ]
        + shapes,
        scratch_shapes=scratch + [pltpu.SemaphoreType.DMA((blocks,))],
        compiler_params=params(48),
        cost_estimate=lasting(12),
        name="attend_back",
    )(order, counts, qkv, logs, *groups, *d_mixes)


def attn_in_grad(token, d_qkvs, order, pieces, rows, each, width):
    clips, length, _ = d_qkvs[0].shape
    sizes = [d.shape[2] for d in d_qkvs]
    total = sum(sizes)
    n_d = len(d_qkvs)
    flat = [array for arrays, _ in pieces for array in arrays]
    blocks = sum(array.shape[0] for array in flat)
    split = clips > each

    def kernel(order_ref, *refs):
        row_refs = refs[:n_d]
        piece_refs = refs[n_d : n_d + len(flat)]
        outs = refs[n_d + len(flat) :]
        weight, sems = outs[-2:]
        step = pl.program_id(0)

        @pl.when(step == 0)
        def _():
            copies, used, column = [], 0, 0
            for arrays, size in pieces:
                refs_here = piece_refs[used : used + len(arrays)]
                target = weight.at[:, column : column + size]
                copies += assemble(
                    refs_here, lambda n: order_ref[n], rows, target, sems, len(copies), slice(0, size)
                )
                used += len(arrays)
                column += size
            run_all(copies)

        low = jnp.concatenate([ref[0] for ref in row_refs], axis=1) if n_d > 1 else row_refs[0][0]
        value = dot_nt(low, weight[...])
        if split:

            @pl.when(step < each)
            def _():
                outs[0][0] = value

            @pl.when(step >= each)
            def _():
                outs[1][0] = value.astype(BF)
        else:
            outs[0][0] = value

    own = pl.BlockSpec((1, length, width), lambda i: (jnp.minimum(i, each - 1), 0, 0))
    other = pl.BlockSpec((1, length, width), lambda i: (jnp.clip(i - each, 0, each - 1), 0, 0))
    shapes = [jax.ShapeDtypeStruct((each, length, width), F32)]
    if split:
        shapes.append(jax.ShapeDtypeStruct((each, length, width), BF))
    return call(
        kernel,
        token,
        grid=(clips,),
        in_specs=[SMEM]
        + [pl.BlockSpec((1, length, c), lambda i: (i, 0, 0)) for c in sizes]
        + [ANY] * len(flat),
        out_specs=[own, other][: len(shapes)],
        out_shape=shapes,
        scratch_shapes=[pltpu.VMEM((width, total), BF), pltpu.SemaphoreType.DMA((blocks,))],
        compiler_params=params(32),
        cost_estimate=lasting(7),
        name="attn_in_grad",
    )(order, *d_qkvs, *flat)


def norm_one_back(token, das, embed, d_resid, small):
    n, length, width = d_resid.shape
    n_da = len(das)

    def kernel(small_ref, embed_ref, resid_ref, *refs):
        da_refs = refs[:n_da]
        grad, sums = refs[n_da:]
        step = pl.program_id(0)
        da = da_refs[0][0].astype(F32)
        for ref in da_refs[1:]:
            da = da + ref[0].astype(F32)
        hat, inv = norm_parts(embed_ref[0])
        grad[0] = resid_ref[0] + norm_back(da * small_ref[0:1, :], hat, inv)
        row = lambda v: jnp.sum(v, axis=0, keepdims=True)
        parts = jnp.concatenate([row(da * hat), row(da), jnp.zeros((6, width), F32)])

        @pl.when(step == 0)
        def _():
            sums[...] = parts

        @pl.when(step > 0)
        def _():
            sums[...] += parts

    clip = pl.BlockSpec((1, length, width), lambda i: (i, 0, 0))
    return call(
        kernel,
        token,
        grid=(n,),
        in_specs=[whole((16, width)), clip, clip] + [clip] * n_da,
        out_specs=[clip, whole((8, width))],
        out_shape=[
            jax.ShapeDtypeStruct(d_resid.shape, F32),
            jax.ShapeDtypeStruct((8, width), F32),
        ],
        compiler_params=params(24),
        cost_estimate=lasting(4),
        name="norm_one_back",
    )(small, embed, d_resid, *das)


def update_group(weight, grad, moment, average, grad_norm, weight_norm):
    effective = grad + WEIGHT_DECAY * weight
    moment_new = MOMENTUM_DECAY * moment + effective
    rate = TRUST_RATE * weight_norm / (grad_norm + WEIGHT_DECAY * weight_norm)
    weight_new = weight - rate * (effective + MOMENTUM_DECAY * moment_new)
    average_new = AVERAGE_DECAY * average + (1.0 - AVERAGE_DECAY) * weight_new
    return (weight_new, moment_new, average_new)


def update_all(token, state, sums, place, halves, g_up, g_down, cuts):
    rows, width = state[1].shape
    part = width // 2
    pairs = part // 128
    n_sq = 9

    def kernel(place_ref, sums_ref, own_ref, other_ref, up_ref, down_ref, *refs):
        ins, outs = refs[:15], refs[15:30]
        norms_ref = refs[30]
        core, chip = place_ref[0], place_ref[1]
        small_rows = sums_ref[0:12, :]
        squares = [sums_ref[12:13, k : k + 1] for k in range(n_sq)]
        squares = squares[:4] + [jnp.sum(small_rows * small_rows).reshape(1, 1)] + squares[4:]
        norms = [jnp.sqrt(s) for s in squares]

        def write(group, weight_cols, grad):
            at = (slice(None), weight_cols)
            values = update_group(
                ins[group][at], grad, ins[5 + group][at], ins[10 + group][at],
                norms[group], norms[5 + group],
            )
            for k in range(3):
                outs[5 * k + group][at] = values[k]

        first = core == 0
        for c in range(2):
            pick = lambda own, other: jnp.where(first if c == 0 else ~first, own, other)
            for pair in range(pairs):
                for t in range(3):
                    cut = slice(384 * pair + 128 * t, 384 * pair + 128 * t + 128)
                    at = t * width + c * part + 128 * pair
                    write(0, slice(at, at + 128), pick(own_ref[:, cut], other_ref[:, cut]))
            cut = slice(384 * pairs, 384 * pairs + part)
            write(1, slice(c * part, c * part + part), pick(own_ref[:, cut], other_ref[:, cut]))
        write(2, slice(None), up_ref[...])
        write(3, slice(None), down_ref[...])

        @pl.when(pl.program_id(0) == 0)
        def _():
            lane = lax.broadcasted_iota(jnp.int32, (1, 128), 1)
            row = jnp.zeros((1, 128), F32)
            for k in range(10):
                row = jnp.where(lane == k, norms[k], row)
            norms_ref[...] = row
            shift = lax.rem(width - chip * rows, width)
            mine = pltpu.roll(sums_ref[...], shift, 1)[:, :128]
            grad = mine.T[:rows]
            at = lax.broadcasted_iota(jnp.int32, (rows, 1), 0)
            column = lax.broadcasted_iota(jnp.int32, (1, 16), 1)
            share = rows // 4
            for col in range(4):
                total = jnp.zeros((rows, 128), F32)
                for quarter in range(4):
                    source = (at - share * quarter) * 4 + col
                    inside = (at >= share * quarter) & (at < share * quarter + share)
                    here = inside & (lane == source)
                    total = jnp.where(here, mine[8 + quarter : 9 + quarter, :], total)
                value = jnp.sum(total, axis=1, keepdims=True)
                grad = jnp.where(column == 8 + col, value, grad)
            write(4, slice(None), grad.T[:12])

    tall = lambda x: pl.BlockSpec((x.shape[0] // cuts, x.shape[1]), lambda i: (i, 0))
    state_specs = [whole(x.shape) if k % 5 == 4 else tall(x) for k, x in enumerate(state)]
    return call(
        kernel,
        token,
        grid=(cuts,),
        in_specs=[SMEM, whole(sums.shape)]
        + [tall(x) for x in (*halves, g_up, g_down)]
        + state_specs,
        out_specs=state_specs + [whole((1, 128))],
        out_shape=[jax.ShapeDtypeStruct(x.shape, F32) for x in state]
        + [jax.ShapeDtypeStruct((1, 128), F32)],
        compiler_params=params(48),
        cost_estimate=lasting(6),
        name="update_all",
    )(place, sums, *halves, g_up, g_down, *state)


def weight_squares(token, state):
    def kernel(*refs):
        lane = lax.broadcasted_iota(jnp.int32, (1, 128), 1)
        row = jnp.zeros((1, 128), F32)
        for k, ref in enumerate(refs[:-1]):
            row = jnp.where(lane == k, 0.5 * jnp.sum(ref[...] * ref[...]), row)
        refs[-1][...] = row

    return call(
        kernel,
        token,
        grid=(1,),
        in_specs=[whole(x.shape) for x in state],
        out_specs=whole((1, 128)),
        out_shape=jax.ShapeDtypeStruct((1, 128), F32),
        compiler_params=params(24),
        cost_estimate=lasting(2),
        name="weight_squares",
    )(*state)


def interleave(token, own, other, place):
    rows, total = own.shape
    width = total // 4
    run = rows

    def kernel(place_ref, own_ref, other_ref, up, down, squares):
        both = [slice(2 * width * h, 2 * width * (h + 1)) for h in range(2)]
        own_refs = [own_ref[:, cut] for cut in both]
        other_refs = [other_ref[:, cut] for cut in both]
        first = place_ref[0] == 0
        lane = lax.broadcasted_iota(jnp.int32, (1, 128), 1)
        total_up = sum(jnp.sum(r[:, :width] * r[:, :width]) for r in own_refs)
        total_down = sum(jnp.sum(r[:, width:] * r[:, width:]) for r in own_refs)
        squares[...] = jnp.where(lane == 0, total_up, jnp.where(lane == 1, total_down, 0.0))
        cells = []
        for c in range(2):
            for h in range(2):
                ahead = first if c == 0 else ~first
                cell = jnp.where(ahead, own_refs[h], other_refs[h])
                cells.append(cell[:, :width])
                at = (2 * c + h) * rows
                down[at : at + rows, :] = cell[:, width:]
        for tile in range(4 * width // 128):
            value = None
            low = 128 * tile
            for k in range(low // run, (low + 127) // run + 1):
                f, ch = k // 4, k % 4
                begin, place_at = f * run, k * run - low
                start = min(begin // 128 * 128, width - 256)
                window = cells[ch][:, start : start + 256]
                moved = pltpu.roll(window, (place_at - (begin - start)) % 256, 1)[:, :128]
                if value is None:
                    value = moved
                else:
                    value = jnp.where(lane >= place_at, moved, value)
            up[:, low : low + 128] = value

    return call(
        kernel,
        token,
        grid=(1,),
        in_specs=[SMEM] + [whole(own.shape)] * 2,
        out_specs=[whole((rows, 4 * width)), whole((4 * rows, width)), whole((1, 128))],
        out_shape=[
            jax.ShapeDtypeStruct((rows, 4 * width), F32),
            jax.ShapeDtypeStruct((4 * rows, width), F32),
            jax.ShapeDtypeStruct((1, 128), F32),
        ],
        compiler_params=params(32),
        cost_estimate=lasting(3),
        name="interleave",
    )(place, own, other)


def gather_sums(token, place, sums_one, sums_two, bias_grads, bias_ups, squares_mlp, squares_w):
    width = sums_one.shape[1]
    part = width // 2

    def kernel(place_ref, one, two, *refs):
        grads, ups = refs[: len(bias_grads)], refs[len(bias_grads) : len(bias_grads) + 2]
        sq_mlp, sq_w, out = refs[-3:]
        core = place_ref[0]
        out[...] = jnp.zeros_like(out)
        out[0:2, :] = one[0:2, :]
        out[2:4, :] = two[0:2, :]
        out[6:8, :] = two[2:4, :]
        for c in range(2):

            @pl.when(core == c)
            def _():
                at = c * part
                for ref in grads:
                    for cut in range(0, ref.shape[1], 384):
                        out[4:5, at : at + 128] = ref[:, cut : cut + 128]
                        out[5:6, at : at + 128] = ref[:, cut + 256 : cut + 384]
                        at += 128
                for h in range(2):
                    out[8 + 2 * c + h : 9 + 2 * c + h, :] = ups[h][...]

        lane = lax.broadcasted_iota(jnp.int32, (1, 128), 1)
        row = jnp.where((lane == 2) | (lane == 3), pltpu.roll(sq_mlp[...], 2, 1), 0.0)
        moved = pltpu.roll(sq_w[...], 4, 1)
        out[12:13, :128] = jnp.where((lane >= 4) & (lane < 9), moved, row)

    ins = [sums_one, sums_two, *bias_grads, *bias_ups, squares_mlp, squares_w]
    return call(
        kernel,
        token,
        grid=(1,),
        in_specs=[SMEM] + [whole(x.shape) for x in ins],
        out_specs=whole((16, width)),
        out_shape=jax.ShapeDtypeStruct((16, width), F32),
        compiler_params=params(16),
        cost_estimate=lasting(1),
        name="gather_sums",
    )(place, *ins)


def last_shards(token, sums, wide, narrow, recv_z):
    rows, columns = wide[0].shape[1:]
    more = narrow[0].shape[2]
    inner = 2 * more

    def kernel(sums_ref, *refs):
        wides, narrows, last = refs[:3], refs[3:6], refs[6:9]
        shard, out = refs[9:]
        total = sum(ref[0].astype(F32) for ref in wides)
        extra = sum(ref[0].astype(F32) for ref in narrows)
        for ref in last:
            came = ref[0].astype(F32)
            total = total + came[:, :columns]
            extra = extra + came[:, columns:]
        heads, outer = total[:, :inner], total[:, inner:]
        shard[:, :inner] = heads
        shard[:, inner : inner + more] = extra
        shard[:, inner + more :] = outer
        out[...] = sums_ref[...]
        square = jnp.sum(heads * heads) + jnp.sum(extra * extra)
        lane = lax.broadcasted_iota(jnp.int32, (1, 128), 1)
        old = sums_ref[12:13, :128]
        new = jnp.where(lane == 0, square, jnp.where(lane == 1, jnp.sum(outer * outer), old))
        out[12:13, :128] = new

    block = lambda c: pl.BlockSpec((1, rows, c), lambda i: (0, 0, 0))
    return call(
        kernel,
        token,
        grid=(1,),
        in_specs=[whole(sums.shape)]
        + [block(columns)] * 3
        + [block(more)] * 3
        + [block(columns + more)] * 3,
        out_specs=[whole((rows, columns + more)), whole(sums.shape)],
        out_shape=[
            jax.ShapeDtypeStruct((rows, columns + more), F32),
            jax.ShapeDtypeStruct(sums.shape, F32),
        ],
        compiler_params=params(16),
        cost_estimate=lasting(2),
        name="last_shards",
    )(sums, *wide, *narrow, *recv_z)


def finish(masters, moments, averages, grads, totals):
    norms = jnp.sqrt(totals)
    results = [
        update_group(masters[i], grads[i], moments[i], averages[i], norms[i], norms[5 + i])
        for i in range(5)
    ]
    return (
        tuple(r[0] for r in results)
        + tuple(r[1] for r in results)
        + tuple(r[2] for r in results)
        + (norms,)
    )


def square_sum(x):
    return jnp.sum(x * x)


def tie(*arrays):
    return lax.optimization_barrier(arrays)


def paired_device(links, tokens, positions, counts, cotangent, *state):
    state = [x.T if k % 5 == 4 else x for k, x in enumerate(state)]
    w_qkv, w_out, w_up, w_down, w_small = state[:5]
    each, length, width = tokens.shape
    rows = w_qkv.shape[0]
    core = lax.axis_index("dp")
    chip = lax.axis_index("fsdp")
    table = jnp.asarray(links.masks())
    core_id = core[None].astype(jnp.int32)
    mine = lax.dynamic_index_in_dim(table, core, 0, False) ^ chip
    partner = lax.dynamic_index_in_dim(table, 1 - core, 0, False) ^ chip
    meta = jnp.concatenate([core_id, mine, partner])
    mine = jnp.concatenate([mine, core_id])
    place = jnp.concatenate([core_id, chip[None].astype(jnp.int32)])
    part = width // 2
    pairs = part // 128
    cross, flip, along_z = links.cross, links.flip, links.along_z
    half_core = lambda x, axis: lax.dynamic_index_in_dim(x, core, axis, False)
    join = lambda *blocks: jnp.concatenate(blocks, axis=0)
    beside = lambda *blocks: jnp.concatenate(blocks, axis=2)

    def onward(first, last, keep, *recvs):
        total = keep[first:last].astype(F32)
        for recv in recvs:
            total = total + recv[first:last].astype(F32)
        return total

    cut = half_core(w_qkv.reshape(rows, 3, 2, pairs, 128), 2).astype(BF)
    cut = jnp.swapaxes(cut, 1, 2).reshape(rows, pairs * 384)
    out_cut = half_core(w_out.reshape(rows, 2, part), 1).astype(BF)
    small_cut = jnp.concatenate([w_small[:8], w_small[8:].T.reshape(4, rows)], axis=0)
    small_cut = jnp.pad(small_cut.astype(BF).T, ((0, 0), (0, 116)))
    pack_q = jnp.concatenate([cut[:, :768], small_cut, cut[:, 768:], out_cut], axis=1)[None]
    token = jnp.zeros((8, 128), F32)
    token, pack_q, w_up, w_down, tokens, positions, counts = tie(
        token, pack_q, w_up, w_down, tokens, positions, counts
    )
    q_z = along_z([pack_q] * 3)
    token_other = cross(tokens)
    place_other = cross(jnp.concatenate([positions, counts[:, None]], axis=1))
    column = lambda x: x.astype(F32)[..., None]
    token, embed = embed_rows(token, [tokens], [column(positions)])
    up_cut = half_core(w_up.reshape(rows, 16, 2, 2, rows), 2).astype(BF)
    down_cut = half_core(w_down.reshape(2, 2, rows, width), 0).astype(BF)
    ups = [up_cut[:, :, h].reshape(1, rows, 16 * rows) for h in range(2)]
    downs = [down_cut[h][None] for h in range(2)]
    pack_b = beside(ups[1], downs[1])
    token, ups[0], downs[0], pack_b, token_other, place_other, *q_z = tie(
        token, ups[0], downs[0], pack_b, token_other, place_other, *q_z
    )
    q_4 = join(pack_q, *q_z)

    token, q_4, up_a, token_other, place_other = tie(
        token, q_4, ups[0], token_other, place_other
    )
    q_b = flip(q_4, 4)
    a_zu = along_z([up_a] * 3)
    token, embed_other = embed_rows(
        token, [token_other], [column(place_other[:, :length])]
    )
    counts_all = jnp.concatenate([counts, place_other[:, length]])
    token, q_b, cotangent, *a_zu = tie(token, q_b, cotangent, *a_zu)
    one_8 = join(q_4[:, :, :896], q_b[:, :, :896])
    two_8 = join(q_4[:, :, 896:], q_b[:, :, 896:])

    token, one_8, two_8, down_a, cotangent = tie(token, one_8, two_8, downs[0], cotangent)
    one_c = flip(one_8, 8)
    a_zd = along_z([down_a] * 3)
    cot_other = cross(cotangent)
    token, squares_w = weight_squares(token, state[:5])
    token, one_c, cot_other, squares_w, *a_zd = tie(token, one_c, cot_other, squares_w, *a_zd)
    a_4 = beside(join(up_a, *a_zu), join(down_a, *a_zd))

    embeds = [embed, embed_other]
    token, a_4, two_8, pack_b = tie(token, a_4, two_8, pack_b)
    two_c = flip(two_8, 8)
    a_b = flip(a_4, 4)
    b_z = along_z([pack_b] * 3)
    token, small, attn_in, qkv_1, logs_1, mix_own_1, mix_send_1 = attend_forward(
        token, embeds, None, mine, core_id, counts_all, [one_8, one_c], rows, each, 0, 4, 6, 0
    )
    token, a_4, a_b, two_c, small, attn_in, qkv_1, logs_1, mix_own_1, mix_send_1, *b_z = tie(
        token, a_4, a_b, two_c, small, attn_in, qkv_1, logs_1, mix_own_1, mix_send_1, *b_z
    )
    a_c1 = flip(a_4, 8)
    mix_recv_1 = cross(mix_send_1)
    out_c, out_d = cross(two_8), cross(two_c)
    b_4 = join(pack_b, *b_z)
    token, qkv_2, logs_2, mix_own_2, mix_send_2 = attend_forward(
        token, [attn_in], small, mine, core_id, counts_all, [two_8, two_c], rows, each, 4, 2, 6, 0
    )
    token, a_b, a_c1, b_4, mix_recv_1, out_c, out_d, qkv_2, logs_2, mix_own_2, mix_send_2 = tie(
        token, a_b, a_c1, b_4, mix_recv_1, out_c, out_d, qkv_2, logs_2, mix_own_2, mix_send_2
    )
    a_c2 = flip(a_b, 8)
    mix_recv_2 = cross(mix_send_2)
    mixes = [mix_own_1, mix_own_2, mix_recv_1, mix_recv_2]
    places = [(0, 0), (0, 256), (1, 0), (1, 256)]
    out_pieces = ([two_8, two_c], [out_c, out_d])
    token, resid, mlp_own = project_norm(
        token, mixes, places, embed, small, meta, *out_pieces, rows
    )
    token, a_c2, resid, mlp_own = tie(token, a_c2, resid, mlp_own)
    mlp_other = cross(mlp_own)

    token, mlp_own, mlp_other, b_4, resid = tie(token, mlp_own, mlp_other, b_4, resid)
    b_rest = [flip(b_4, p) for p in (4, 8, 12)]
    groups, cots = [mlp_own, mlp_other], [cotangent, cot_other]
    token, *made_a = mlp_both(
        token, groups, cots, mine, counts_all, small, 8, [a_4, a_b, a_c1, a_c2], rows, True
    )
    token, *both = tie(token, *b_rest, *made_a)
    b_rest, made_a = both[:3], both[3:]
    own_out_a, own_dm_a, sent_out_a, sent_dm_a, bias_up_a, keep_a, *sends = made_a

    a_r3 = [flip(send, 8) for send in sends]
    recv_dm_a, recv_out_a = cross(sent_dm_a), cross(sent_out_a)
    token, *made_b = mlp_both(
        token, groups, cots, mine, counts_all, small, 9, [b_4, *b_rest], rows, True
    )
    token, *both = tie(token, *a_r3, recv_dm_a, recv_out_a, *made_b)
    a_r3, (recv_dm_a, recv_out_a), made_b = both[:2], both[2:4], both[4:]
    own_out_b, own_dm_b, sent_out_b, sent_dm_b, bias_up_b, keep_b, *sends = made_b

    recv_dm_b = cross(sent_dm_b)
    send_a = (keep_a[4:].astype(F32) + a_r3[1].astype(F32)).astype(BF)
    token, recv_dm_b, send_a = tie(token, recv_dm_b, send_a)
    a_r2 = flip(send_a, 4)
    dms = [own_dm_a, own_dm_b, recv_dm_a, recv_dm_b]
    token, d_mix_own, d_mix_send, proj, d_resid, sums_two = norm_two_back(
        token, dms, resid, cotangent, small, meta, counts, *out_pieces, rows, part
    )
    token, a_r2, d_mix_own, d_mix_send, proj, d_resid, sums_two, sent_out_b = tie(
        token, a_r2, d_mix_own, d_mix_send, proj, d_resid, sums_two, sent_out_b
    )

    d_mix_recv = cross(d_mix_send)
    recv_out_b = cross(sent_out_b)
    sends_a = [onward(k, k + 1, keep_a, a_r3[0], a_r2).astype(BF) for k in (1, 2, 3)]
    token, keep_o, send_o = out_weight_grad(token, mixes, places, proj, meta, rows)
    token, d_mix_recv, keep_o, send_o, recv_out_b, *both = tie(
        token, d_mix_recv, keep_o, send_o, recv_out_b, *sends, *sends_a
    )
    sends, sends_a = both[:2], both[2:]

    b_r3 = [flip(send, 8) for send in sends]
    a_rz = along_z(sends_a)
    recv_o = cross(send_o)
    d_mixes = [d_mix_own, d_mix_recv]
    back = lambda token, qkv, logs, first, pair: attend_back(
        token, [attn_in], qkv, logs, d_mixes, mine, counts_all, rows, True, first, pair, 1
    )
    token, *made_0 = back(token, qkv_1, logs_1, 0, 0)
    token, *both = tie(token, *b_r3, *a_rz, recv_o, *made_0)
    b_r3, a_rz, (recv_o, d_qkv_0, bias_grad_0, keep_0, send_0) = both[:2], both[2:5], both[5:]
    send_b = (keep_b[4:].astype(F32) + b_r3[1].astype(F32)).astype(BF)
    total_o = (keep_o.astype(F32) + recv_o.astype(F32)).astype(BF)

    token, total_o, send_b = tie(token, total_o, send_b)
    b_r2 = flip(send_b, 4)
    token, *made_1 = back(token, qkv_1, logs_1, 1, 1)
    token, b_r2, d_qkv_1, bias_grad_1, keep_1, send_1 = tie(token, b_r2, *made_1)
    sends_b = [onward(k, k + 1, keep_b, b_r3[0], b_r2).astype(BF) for k in (1, 2, 3)]
    send_q = beside(send_0, send_1, total_o[8:])

    token, send_q, *sends_b = tie(token, send_q, *sends_b)
    q_r3 = flip(send_q, 8)
    b_rz = along_z(sends_b)
    token, *made_2 = back(token, qkv_2, logs_2, 0, 2)
    token, q_r3, *both = tie(token, q_r3, *b_rz, *made_2)
    b_rz, (d_qkv_2, bias_grad_2, keep_r, send_r) = both[:3], both[3:]
    keep_q = beside(keep_0, keep_1, total_o[:8])
    send_q = onward(4, 8, keep_q, q_r3).astype(BF)

    token, send_q, send_r = tie(token, send_q, send_r)
    r_r3 = flip(send_r, 8)
    q_r2 = flip(send_q, 4)
    token, da_own, da_send = attn_in_grad(
        token, [d_qkv_0, d_qkv_1, d_qkv_2], mine, [([one_8, one_c], 768), ([two_8, two_c], 384)], rows, each, width
    )
    token, r_r3, q_r2, da_own, da_send = tie(token, r_r3, q_r2, da_own, da_send)

    send_r = onward(4, 8, keep_r, r_r3).astype(BF)
    token, send_r = tie(token, send_r)
    r_r2 = flip(send_r, 4)
    da_recv = cross(da_send)
    token, token_grad, sums_one = norm_one_back(
        token, [da_own, da_recv], embed, d_resid, small
    )
    token, r_r2, token_grad, sums_one = tie(token, r_r2, token_grad, sums_one)

    sends_z = [
        beside(
            onward(k, k + 1, keep_q, q_r3, q_r2).astype(BF),
            onward(k, k + 1, keep_r, r_r3, r_r2).astype(BF),
        )
        for k in (1, 2, 3)
    ]
    token, resid, keep_a, keep_b, *sends_z = tie(token, resid, keep_a, keep_b, *sends_z)
    recv_z = along_z(sends_z)
    shard_m = jnp.concatenate(
        [
            onward(0, 1, keep_a, a_r3[0], a_r2, *a_rz)[0],
            onward(0, 1, keep_b, b_r3[0], b_r2, *b_rz)[0],
        ],
        axis=1,
    )
    other_m = cross(shard_m)
    block_rows = resid + small[7]
    for value in (own_out_a, own_out_b, recv_out_a, recv_out_b):
        block_rows = block_rows + value.astype(F32)
    block_out = block_rows.astype(BF)
    token, g_up, g_down, squares_mlp = interleave(token, shard_m, other_m, place)
    bias_grads = [bias_grad_0, bias_grad_1, bias_grad_2]
    token, sums = gather_sums(
        token, place, sums_one, sums_two, bias_grads, (bias_up_a, bias_up_b), squares_mlp, squares_w
    )
    token, block_out, *both = tie(token, block_out, g_up, g_down, sums, *recv_z)
    g_up, g_down, sums, *recv_z = both
    token, shard_q, sums = last_shards(
        token, sums, (keep_q, q_r3, q_r2), (keep_r, r_r3, r_r2), recv_z
    )
    other_q = cross(shard_q)
    sums = links.sum_all(sums)
    results = update_all(token, state, sums, place, (shard_q, other_q), g_up, g_down, 3)[1:]
    outs = [x.T if k % 5 == 4 else x for k, x in enumerate(results[:15])]
    return (block_out, token_grad) + tuple(outs) + (results[15][0, :10],)


def plain_device(tokens, positions, counts, cotangent, *state):
    masters, moments, averages = state[:5], state[5:10], state[10:]
    each, length, width = tokens.shape
    heads = width // HEAD_DIM
    pairs = heads // 2
    full = [
        lax.all_gather(w.astype(BF), "fsdp", axis=0, tiled=True) for w in masters
    ]
    wq, wo, up, down, table = full
    wq = jnp.swapaxes(wq.reshape(width, 3, pairs, 128), 1, 2).reshape(1, width, 3 * width)
    table = table.astype(F32)
    vectors = jnp.concatenate([table[:, :8].T, jnp.zeros((8, width), F32)], axis=0)
    bias_up = table[:, 8:].reshape(1, -1)
    hidden = bias_up.shape[1]
    order = jnp.zeros((33,), jnp.int32)
    token = jnp.zeros((8, 128), F32)
    token, embed = embed_rows(token, [tokens], [positions.astype(F32)[..., None]])
    token, attn_in, qkv, logs, mixed = attend_forward(
        token, [embed], vectors, order, order, counts, [wq], width, each, 0, heads, 0, 0
    )
    places = [(0, 0)]
    token, resid, mlp_in = project_norm(
        token, [mixed], places, embed, vectors, order, [wo[None]], [], width
    )
    outs, dms, bias_ups, ups, downs = [], [], [], [], []
    parts = 4
    size = hidden // parts
    for h in range(parts):
        cols = slice(h * size, (h + 1) * size)
        token, out, dm, bias, g_up, g_down = mlp_both(
            token,
            [mlp_in],
            [cotangent],
            order,
            counts,
            bias_up[:, cols],
            0,
            [up[:, cols][None], down[cols][None]],
            width,
            False,
        )
        outs.append(out)
        dms.append(dm)
        bias_ups.append(bias)
        ups.append(g_up[0])
        downs.append(g_down[0])
    token, d_mix, proj, d_resid, sums_two = norm_two_back(
        token, dms, resid, cotangent, vectors, order, counts, [wo[None]], [], width, width
    )
    token, g_out = out_weight_grad(token, [mixed], places, proj, order, width)
    g_out = g_out[0]
    token, d_qkv, bias_grad, g_qkv = attend_back(
        token, [attn_in], qkv, logs, [d_mix], order, counts, width, False, 0, 0, pairs
    )
    natural = lambda g: jnp.swapaxes(g.reshape(-1, pairs, 3, 128), 1, 2).reshape(-1, 3 * width)
    g_qkv, bias_grad = natural(g_qkv), natural(bias_grad)
    token, da = attn_in_grad(token, [d_qkv], order, [([wq], 3 * width)], width, each, width)
    token, token_grad, sums_one = norm_one_back(token, [da], embed, d_resid, vectors)
    block_rows = resid + vectors[7]
    for value in outs:
        block_rows = block_rows + value
    block_out = block_rows.astype(BF)
    columns = jnp.stack(
        [
            sums_one[0],
            sums_one[1],
            sums_two[0],
            sums_two[1],
            bias_grad[0, :width],
            bias_grad[0, 2 * width :],
            sums_two[2],
            sums_two[3],
        ],
        axis=1,
    )
    small = jnp.concatenate(
        [columns, jnp.concatenate(bias_ups, axis=1).reshape(width, -1)], axis=1
    )
    partial = (
        g_qkv,
        g_out,
        jnp.concatenate(ups, axis=1),
        jnp.concatenate(downs, axis=0),
        small,
    )
    grads = []
    for grad in partial:
        shard = lax.psum_scatter(grad, "fsdp", scatter_dimension=0, tiled=True)
        grads.append(lax.psum(shard, "dp"))
    squares = jnp.stack([square_sum(g) for g in grads] + [square_sum(w) for w in masters])
    totals = lax.psum(squares, "fsdp")
    return (block_out, token_grad) + finish(masters, moments, averages, tuple(grads), totals)


def solution(mesh):
    clips = P(("dp", "fsdp"), None, None)
    in_specs = (clips, P(("dp", "fsdp"), None), P(("dp", "fsdp")), clips) + (P("fsdp", None),) * 15
    out_specs = (clips, clips) + (P("fsdp", None),) * 15 + (P(),)
    links = Links(mesh.shape["dp"], mesh.shape["fsdp"])

    def on_device(*args):
        if links.paired:
            return paired_device(links, *args)
        return plain_device(*args)

    return jax.shard_map(
        on_device, mesh=mesh, in_specs=in_specs, out_specs=out_specs, check_vma=False
    )
```
